128 devices in a mesh: rows: 8 (over x_hi, y), seq: 16 (over z, x_lo, core).
Axes of the slice: x: 4 (x_hi: 2, x_lo: 2; x = x_hi * 2 + x_lo), y: 4, z: 4, core: 2. Of those that a mesh axis runs over, the one named last changes fastest.
Arguments:
- hidden_in: bfloat16 [16, 1024, 1024], P('rows', 'seq'), may hold values from -6 to 6
- query_weight: bfloat16 [1024, 2048], replicated, may hold values from -0.1875 to 0.1875
- key_weight: bfloat16 [1024, 1024], replicated, may hold values from -0.1875 to 0.1875
- value_weight: bfloat16 [1024, 1024], replicated, may hold values from -0.1875 to 0.1875
- output_weight: bfloat16 [1024, 2048], replicated, may hold values from -0.5 to 0.5
- gate_weight: bfloat16 [1024, 3072], replicated, may hold values from -0.1875 to 0.1875
- up_weight: bfloat16 [1024, 3072], replicated, may hold values from -0.1875 to 0.1875
- down_weight: bfloat16 [1024, 3072], replicated, may hold values from -0.109375 to 0.109375
- query_gain: float32 [128], replicated, may hold values from 1.2 to 2.4
- key_gain: float32 [128], replicated, may hold values from 0.1 to 1.9
- attention_gain: float32 [1024], replicated, may hold values from 0.1 to 1.9
- feedforward_gain: float32 [1024], replicated, may hold values from 0.1 to 1.9
- document_ids: int32 [16, 1024], P('rows', 'seq'), may hold values from 0 to 8, as said below
- cotangent: bfloat16 [16, 1024, 1024], P('rows', 'seq'), may hold values from -6 to 6
Outputs:
- layer_output: float32 [16, 1024, 1024], P('rows', 'seq')
- input_grad: float32 [16, 1024, 1024], P('rows', 'seq')
- query_weight_grad: float32 [1024, 2048], P('seq')
- key_weight_grad: float32 [1024, 1024], P('seq')
- value_weight_grad: float32 [1024, 1024], P('seq')
- output_weight_grad: float32 [1024, 2048], P('seq')
- gate_weight_grad: float32 [1024, 3072], P('seq')
- up_weight_grad: float32 [1024, 3072], P('seq')
- down_weight_grad: float32 [1024, 3072], P('seq')
- query_gain_grad: float32 [128], replicated
- key_gain_grad: float32 [128], replicated
- attention_gain_grad: float32 [1024], replicated
- feedforward_gain_grad: float32 [1024], replicated
The draws below stay inside these ranges and needn't reach their ends.
Inputs may be any that keep to these rules, and one draw needn't show every extreme that they name: `document_ids`: along each row the ids start at 0 and never fall.
All inputs are finite; a program needn't handle non-finite values.
Results may differ from the reference program's by a relative error of at most 0.035.
Values may be sent and summed in bfloat16 or wider, within the bound.
A program may use at most 192 MiB of HBM per device.

```python
import jax
import jax.numpy as jnp
from jax import lax

D = 1024
H = 16
KVH = 8
HD = 128
FF = 3072
TOK_DEV = 64
ROWS_DEV = 2
SEQ = 1024
BATCH = 16
BOUNDS = 8


def spanning_ids(key):
    subkeys = jax.random.split(key, 4)
    begin_long = jax.random.randint(subkeys[0], (BATCH, 1), 2, TOK_DEV)
    cut_front = jax.random.randint(subkeys[1], (BATCH, 1), 1, begin_long)
    tail_length = jax.random.randint(subkeys[2], (BATCH, 1), 2, TOK_DEV)
    end_long = SEQ - tail_length
    cut_back = end_long + jax.random.randint(subkeys[3], (BATCH, 1), 1, tail_length)
    positions = jnp.arange(SEQ, dtype=jnp.int32)[None, :]
    counted = (positions >= cut_front).astype(jnp.int32) + (positions >= begin_long).astype(jnp.int32)
    counted = counted + (positions >= end_long).astype(jnp.int32) + (positions >= cut_back).astype(jnp.int32)
    return counted.astype(jnp.int32)


def scattered_ids(key):
    row_keys = jax.random.split(key, BATCH)

    def row_bounds(row_key):
        return jax.random.permutation(row_key, SEQ - 1)[:BOUNDS].astype(jnp.int32) + 1
    boundaries = jax.vmap(row_bounds)(row_keys)
    positions = jnp.arange(SEQ, dtype=jnp.int32)
    return jnp.sum((positions[None, None, :] >= boundaries[:, :, None]).astype(jnp.int32), axis=1).astype(jnp.int32)


def draw_document_ids(key, part):
    key = jax.random.fold_in(key, 11)
    subkeys = jax.random.split(key, 3)
    spanning = spanning_ids(subkeys[0])
    scattered = scattered_ids(subkeys[1])
    chosen = jax.random.randint(subkeys[2], (BATCH // ROWS_DEV, 1), 0, ROWS_DEV)
    row_place = (jnp.arange(BATCH, dtype=jnp.int32) % ROWS_DEV).reshape(BATCH // ROWS_DEV, ROWS_DEV)
    spanning_pick = (row_place == chosen).reshape(BATCH, 1)
    return jnp.where(spanning_pick, spanning, scattered).astype(jnp.int32)


def block_scale(own_key, extent, shards, smallest, largest):
    gain, own = 1.0, jax.random.fold_in(own_key, 6)
    for axis_at, parts in shards:
        heights = jnp.exp(jax.random.uniform(jax.random.fold_in(own, axis_at), (parts,), jnp.float32, smallest / len(shards), largest / len(shards)))
        gain = gain * jnp.repeat(heights, extent[axis_at] // parts).reshape([-1 if axis == axis_at else 1 for axis in range(len(extent))])
    return gain


def noise(stream_key, shape, width, most, shards=(), held_as=jnp.bfloat16):
    entries = jax.random.normal(stream_key, shape, jnp.float32) * width
    if len(shards) > 0:
        entries = block_scale(stream_key, shape, shards, -0.22, 0.18) * entries
    return jnp.clip(entries, min=-most, max=most).astype(held_as)


def setup_inputs(seed: int = 0) -> dict:
    streams_of = jax.random.split(jax.random.key(seed), 15)
    return {
        "hidden_in": noise(streams_of[0], (BATCH, SEQ, D), 1.0, 6.0, ((0, 8), (1, 16))),
        "query_weight": noise(streams_of[1], (D, H * HD), D ** -0.5, 0.1875),
        "key_weight": noise(streams_of[2], (D, KVH * HD), D ** -0.5, 0.1875),
        "value_weight": noise(streams_of[3], (D, KVH * HD), D ** -0.5, 0.1875),
        "output_weight": noise(streams_of[4], (D, H * HD), (max(1, H * HD // 16)) ** -0.5, 0.5),
        "gate_weight": noise(streams_of[5], (D, FF), D ** -0.5, 0.1875),
        "up_weight": noise(streams_of[6], (D, FF), D ** -0.5, 0.1875),
        "down_weight": noise(streams_of[7], (D, FF), FF ** -0.5, 0.109375),
        "query_gain": jnp.clip(jax.random.uniform(streams_of[8], (HD,), jnp.float32, 1.2, 2.4), 1.2, 2.4),
        "key_gain": jnp.clip(1.0 + 0.18 * jax.random.normal(streams_of[9], (HD,), jnp.float32), 0.1, 1.9),
        "attention_gain": jnp.clip(1.0 + 0.18 * jax.random.normal(streams_of[10], (D,), jnp.float32), 0.1, 1.9),
        "feedforward_gain": jnp.clip(1.0 + 0.18 * jax.random.normal(streams_of[11], (D,), jnp.float32), 0.1, 1.9),
        "document_ids": draw_document_ids(jax.random.fold_in(streams_of[14], 71), 0),
        "cotangent": noise(streams_of[13], (BATCH, SEQ, D), 1.0, 6.0, ((0, 8), (1, 16))),
    }


@jax.custom_vjp
def low(v):
    return lax.optimization_barrier(v.astype(jnp.bfloat16)).astype(jnp.float32)

@jax.custom_vjp
def low_back(v):
    return v

def low_keep(v):
    return (low(v), None)

def low_pass(kept, grad):
    return (grad,)

def back_keep(v):
    return (v, None)

def back_low(kept, grad):
    return (low(grad),)
low.defvjp(low_keep, low_pass)
low_back.defvjp(back_keep, back_low)
EPSILON = 1e-06
ROPE_BASE = 1000000.0
MASKED = -1e+30
PRECISE = lax.Precision.HIGHEST

def product(left_side, right_side):
    return jnp.dot(left_side, right_side, precision=PRECISE)

def normalize(vector, scales):
    inverse = lax.rsqrt(lax.optimization_barrier(jnp.mean(vector * vector, axis=-1, keepdims=True)) + EPSILON)
    return vector * inverse * scales

def turn_half(vector):
    half_width = vector.shape[-1] // 2
    return jnp.concatenate([-vector[..., half_width:], vector[..., :half_width]], axis=-1)

def rotary_tables(positions):
    half_width = HD // 2
    frequency = ROPE_BASE ** (-(jnp.arange(half_width, dtype=jnp.float32) * 2.0 / HD))
    angles = positions.astype(jnp.float32)[:, None] * frequency[None, :]
    angles = jnp.concatenate([angles, angles], axis=-1)
    return (jnp.cos(angles)[:, None, :], jnp.sin(angles)[:, None, :])

def rotate(vector, cosines, sines):
    return vector * cosines + turn_half(vector) * sines

def decoder_layer(tokens, query_weight, key_weight, value_weight, output_weight, gate_weight, up_weight, down_weight, query_gain, key_gain, attention_gain, feedforward_gain, documents):
    length = tokens.shape[0]
    head_count = query_weight.shape[1] // HD
    key_heads = key_weight.shape[1] // HD
    group_size = head_count // key_heads
    positions = jnp.arange(length, dtype=jnp.int32)
    cosines, sines = rotary_tables(positions)
    query_raw = low_back(product(tokens, query_weight)).reshape(length, head_count, HD)
    key_raw = low_back(product(tokens, key_weight)).reshape(length, key_heads, HD)
    values = low(low_back(product(tokens, value_weight))).reshape(length, key_heads, HD)
    query_normed = normalize(query_raw, query_gain)
    queries = low(rotate(query_normed, cosines, sines))
    key_normed = normalize(key_raw, key_gain)
    keys = low(rotate(key_normed, cosines, sines))
    keys_all = jnp.repeat(keys, group_size, axis=1)
    values_all = jnp.repeat(values, group_size, axis=1)
    block_size = min(512, length)
    score_scale = HD ** (-0.5)

    def attend(block_index):
        first_row = block_index * block_size
        block_queries = lax.dynamic_slice_in_dim(queries, first_row, block_size, 0)
        block_documents = lax.dynamic_slice_in_dim(documents, first_row, block_size, 0)
        block_positions = first_row + jnp.arange(block_size, dtype=jnp.int32)
        scores = low_back(jnp.einsum('qhd,khd->hqk', block_queries, keys_all, precision=PRECISE) * score_scale)
        visible = (block_positions[:, None] >= positions[None, :]) & (block_documents[:, None] == documents[None, :])
        running_top = lax.optimization_barrier(jnp.max(jnp.where(visible, scores, MASKED), axis=-1, keepdims=True))
        exponents = jnp.exp(jnp.where(visible, scores - running_top, MASKED))
        probs = low(exponents / lax.optimization_barrier(jnp.sum(exponents, axis=-1, keepdims=True)))
        return jnp.einsum('hqk,khd->qhd', probs, values_all, precision=PRECISE)
    mixed = lax.map(jax.checkpoint(attend), jnp.arange(length // block_size, dtype=jnp.int32))
    attended = low(low_back(mixed.reshape(length, head_count * HD)))
    branch = low_back(product(attended, output_weight.T))
    residual = tokens + normalize(branch, attention_gain)
    residual_low = low(residual)
    gate = low_back(product(residual_low, gate_weight))
    up_proj = low_back(product(residual_low, up_weight))
    activated = low(jax.nn.silu(gate) * up_proj)
    down = low_back(product(activated, down_weight.T))
    return residual + normalize(down, feedforward_gain)

def reference(hidden_in, query_weight, key_weight, value_weight, output_weight, gate_weight, up_weight, down_weight, query_gain, key_gain, attention_gain, feedforward_gain, document_ids, cotangent):
    params = tuple((weight_array.astype(jnp.float32) for weight_array in (query_weight, key_weight, value_weight, output_weight, gate_weight, up_weight, down_weight, query_gain, key_gain, attention_gain, feedforward_gain)))

    def row_step(grad_sums, row_data):
        row_hidden, row_documents, row_cotangent = row_data

        def forward(row_input, *weights_all):
            return decoder_layer(row_input, *weights_all, row_documents)
        result, pullback = jax.vjp(forward, row_hidden.astype(jnp.float32), *params)
        gradients = pullback(row_cotangent.astype(jnp.float32))
        grad_sums = tuple((running + addend for running, addend in zip(grad_sums, gradients[1:])))
        return (grad_sums, (result, gradients[0]))
    initial = tuple((jnp.zeros(weight_array.shape, jnp.float32) for weight_array in params))
    grad_sums, (outputs, input_grad) = lax.scan(row_step, initial, (hidden_in, document_ids, cotangent))
    return (outputs, input_grad, grad_sums[0], grad_sums[1], grad_sums[2], grad_sums[3], grad_sums[4], grad_sums[5], grad_sums[6], grad_sums[7], grad_sums[8], grad_sums[9], grad_sums[10])
```

```python
import functools

import jax
import jax.numpy as jnp
import numpy as np
from jax import lax
from jax.experimental import pallas as pl
from jax.experimental.pallas import tpu as pltpu
from jax.sharding import PartitionSpec as P

HD = 128
EPSILON = 1e-06
ROPE_BASE = 1000000.0
MASKED = -1e30
LOG2E = 1.4426950408889634
SCALE = HD ** (-0.5)
MESH = pl.DeviceIdType.MESH
F32 = jnp.float32
BF16 = jnp.bfloat16

YS = 4
ZS = 4
XS = 4


def place():
    rows, seq = lax.axis_index("rows"), lax.axis_index("seq")
    return (rows // YS, rows % YS, seq // 4, (seq // 2) % 2, seq % 2)


def device(xh, y, z, xl, c):
    return (xh * YS + y, z * 4 + xl * 2 + c)


def shifted(at, dx=0, dy=0, dz=0, dc=0, flip_xl=0, flip_xh=0):
    xh, y, z, xl, c = at
    if dx:
        x = (xh * 2 + xl + dx) % XS
        xh, xl = x // 2, x % 2
    if flip_xl:
        xl = 1 - xl
    if flip_xh:
        xh = 1 - xh
    if dc:
        c = 1 - c
    return (xh, (y + dy) % YS, (z + dz) % ZS, xl, c)


class Net:
    def __init__(self, send_sems, recv_sems, local_sems):
        self.send_sems, self.recv_sems, self.local_sems = send_sems, recv_sems, local_sems
        self.sent, self.kept = [], []

    def barrier(self, targets):
        barrier = pltpu.get_barrier_semaphore()
        for target in targets:
            pl.semaphore_signal(barrier, inc=1, device_id=device(*target), device_id_type=MESH)
        pl.semaphore_wait(barrier, len(targets))

    def send(self, src, dst, target):
        i = len(self.sent)
        copy = pltpu.make_async_remote_copy(
            src_ref=src,
            dst_ref=dst,
            send_sem=self.send_sems.at[i],
            recv_sem=self.recv_sems.at[i],
            device_id=device(*target),
            device_id_type=MESH,
        )
        copy.start()
        self.sent.append(copy)
        return copy

    def keep(self, src, dst):
        copy = pltpu.make_async_copy(src, dst, self.local_sems.at[len(self.kept)])
        copy.start()
        self.kept.append(copy)
        return copy


def transfer(body, name, collective_id, outs, sends, keeps):
    def call(*arrays):
        count = len(arrays)

        def kernel(*refs):
            net = Net(*refs[-3:])
            body(net, place(), refs[:count], refs[count:-3])

        return pl.pallas_call(
            kernel,
            out_shape=outs,
            in_specs=[pl.BlockSpec(memory_space=pl.ANY)] * count,
            out_specs=[pl.BlockSpec(memory_space=pl.ANY)] * len(outs),
            scratch_shapes=[
                pltpu.SemaphoreType.DMA((sends,)),
                pltpu.SemaphoreType.DMA((sends,)),
                pltpu.SemaphoreType.DMA((max(keeps, 1),)),
            ],
            compiler_params=pltpu.CompilerParams(
                collective_id=collective_id, has_side_effects=True
            ),
            name=name,
        )(*arrays)

    return call


def shape(dims, dtype=BF16):
    return jax.ShapeDtypeStruct(dims, dtype)


ZC = [(dz, dc) for dz in range(ZS) for dc in range(2) if (dz, dc) != (0, 0)]


def gather_row_body(net, at, ins, outs):
    hidden, cotangent, documents = ins
    row, upstream, row_documents = outs
    xh, y, z, xl, c = at
    others = [
        shifted(at, dz=dz, dc=dc, flip_xl=dx)
        for dz in range(ZS)
        for dx in range(2)
        for dc in range(2)
        if (dz, dx, dc) != (0, 0, 0)
    ]
    net.barrier(others)
    arrivals = []
    spread = [(dz, dx) for dz in range(ZS) for dx in range(2)]
    for dz, dx in spread:
        target = shifted(at, dz=dz, flip_xl=dx)
        source = shifted(at, dz=-dz, flip_xl=dx)
        if (dz, dx) == (0, 0):
            arrivals.append((source, None))
        else:
            arrivals.append((source, net.send(hidden.at[target[3]], row.at[z, xl, c], target)))
    mine = [net.keep(hidden.at[xl], row.at[z, xl, c])]
    partner = shifted(at, flip_xl=1)
    last = [net.send(cotangent.at[1 - xl], upstream.at[xl], partner)]
    mine.append(net.keep(cotangent.at[xl], upstream.at[xl]))
    for target in others:
        last.append(net.send(documents.at[target[3]], row_documents.at[z, xl, c], target))
    mine.append(net.keep(documents.at[xl], row_documents.at[z, xl, c]))
    mine[0].wait()
    sibling = shifted(at, dc=1)
    for source, copy in arrivals:
        if copy is not None:
            copy.wait_recv()
        block = row.at[source[2], source[3], c]
        last.append(net.send(block, block, sibling))
    for source, copy in arrivals:
        if copy is not None:
            copy.wait_send()
    for copy in mine[1:] + last:
        copy.wait()


gather_row = transfer(
    gather_row_body,
    "gather_row",
    0,
    [shape((4, 2, 2, 64, 1024)), shape((2, 64, 1024)), shape((4, 2, 2, 8, 128), jnp.int32)],
    7 + 1 + 15 + 8,
    3,
)


def to_owners_body(net, at, ins, outs):
    (heads,) = ins
    (tokens,) = outs
    xh, y, z, xl, c = at
    head = z * 2 + c
    width = heads.shape[-1]
    others = [shifted(at, dz=dz, dc=dc) for dz, dc in ZC]
    net.barrier(others)
    columns = pl.ds(pl.multiple_of(head * width, 128), width)
    copies = [net.send(heads.at[t[2], :, t[4]], tokens.at[:, :, columns], t) for t in others]
    copies.append(net.keep(heads.at[z, :, c], tokens.at[:, :, columns]))
    for copy in copies:
        copy.wait()


attended_to_owners = transfer(
    to_owners_body, "attended_to_owners", 1, [shape((2, 64, 2048))], 7, 1
)


def spread_body(net, at, ins, outs):
    attn_grad, branch, residual, gate_up, down, activated = ins
    attn_grad_row, branch_row, residual_all, gate_up_all, down_all, activated_all = outs
    xh, y, z, xl, c = at
    x = xh * 2 + xl
    zc = [shifted(at, dz=dz, dc=dc) for dz, dc in ZC]
    yc = [shifted(at, dy=dy, dc=dc) for dy, dc in ZC]
    xc = [shifted(at, dx=dx, dc=dc) for dx, dc in ZC]
    net.barrier(zc + yc[1:] + xc[1:])
    wait = []
    for t in zc:
        columns = pl.ds(pl.multiple_of((t[2] * 2 + t[4]) * 256, 128), 256)
        wait.append(net.send(attn_grad.at[:, :, columns], attn_grad_row.at[z, :, c], t))
    chains = []
    for step in range(1, 4):
        for name, src, dst in (("z", branch, branch_row), ("y", residual, residual_all), ("x", down, down_all)):
            if name == "z":
                target, source = shifted(at, dz=step), shifted(at, dz=-step)
                slot, landed = dst.at[z, :, c], dst.at[source[2], :, c]
            elif name == "y":
                target, source = shifted(at, dy=step), shifted(at, dy=-step)
                slot, landed = dst.at[y, c], dst.at[source[1], c]
            else:
                target, source = shifted(at, dx=step), shifted(at, dx=-step)
                slot, landed = dst.at[x, c], dst.at[source[0] * 2 + source[3], c]
            chains.append((net.send(src, slot, target), landed))
    for (dy, dc), t in zip(ZC, yc):
        wait.append(net.send(gate_up.at[t[1], t[4]], gate_up_all.at[y, c], t))
    for (dx, dc), t in zip(ZC, xc):
        wait.append(net.send(activated.at[t[0] * 2 + t[3], t[4]], activated_all.at[x, c], t))
    sibling = shifted(at, dc=1)
    for src, slot in (
        (branch, branch_row.at[z, :, c]),
        (residual, residual_all.at[y, c]),
        (down, down_all.at[x, c]),
    ):
        wait.append(net.send(src, slot, sibling))
        wait.append(net.keep(src, slot))
    columns = pl.ds(pl.multiple_of((z * 2 + c) * 256, 128), 256)
    wait.append(net.keep(attn_grad.at[:, :, columns], attn_grad_row.at[z, :, c]))
    wait.append(net.keep(gate_up.at[y, c], gate_up_all.at[y, c]))
    wait.append(net.keep(activated.at[x, c], activated_all.at[x, c]))
    for copy, landed in chains:
        copy.wait_recv()
        wait.append(net.send(landed, landed, sibling))
    for copy, landed in chains:
        copy.wait_send()
    for copy in wait:
        copy.wait()


spread = transfer(
    spread_body,
    "spread",
    2,
    [
        shape((4, 2, 2, 64, 256)),
        shape((4, 2, 2, 64, 1024)),
        shape((4, 2, 128, 1024)),
        shape((4, 2, 2, 128, 384)),
        shape((4, 2, 128, 1024)),
        shape((4, 2, 128, 384)),
    ],
    7 + 9 + 14 + 3 + 9,
    6,
)


def first_reduce_body(net, at, ins, outs):
    lows, own_a, own_b, own_c = ins
    tokens, all_a, all_b, all_c = outs
    xh, y, z, xl, c = at
    x = xh * 2 + xl
    zc = [shifted(at, dz=dz, dc=dc) for dz, dc in ZC]
    ys = [shifted(at, dy=step) for step in range(1, 4)]
    xs = [shifted(at, dx=step) for step in range(1, 4)]
    zs = [shifted(at, dz=step) for step in range(1, 4)]
    net.barrier(zc + ys + xs)
    wait = []
    for t in zc:
        wait.append(net.send(lows.at[t[2], :, t[4]], tokens.at[z * 2 + c], t))
    for step in range(3):
        t = ys[step]
        wait.append(net.send(own_a.at[:, :, :, t[1]], all_a.at[y], t))
        t = xs[step]
        columns = pl.ds(pl.multiple_of(t[0] * 384, 128), 384)
        wait.append(net.send(own_b.at[:, t[3], :, :, columns], all_b.at[x], t))
        t = zs[step]
        wait.append(net.send(own_c.at[t[2]], all_c.at[z], t))
    columns = pl.ds(pl.multiple_of(xh * 384, 128), 384)
    wait.append(net.keep(lows.at[z, :, c], tokens.at[z * 2 + c]))
    wait.append(net.keep(own_a.at[:, :, :, y], all_a.at[y]))
    wait.append(net.keep(own_b.at[:, xl, :, :, columns], all_b.at[x]))
    wait.append(net.keep(own_c.at[z], all_c.at[z]))
    for copy in wait:
        copy.wait()


first_reduce = transfer(
    first_reduce_body,
    "first_reduce",
    3,
    [
        shape((8, 2, 64, 512)),
        shape((4, 4, 2, 2, 16, 768)),
        shape((4, 4, 2, 64, 384)),
        shape((4, 256, 384)),
    ],
    16,
    4,
)


def second_reduce_body(net, at, ins, outs):
    own_a, own_b, own_c = ins
    all_a, all_b, all_c = outs
    xh, y, z, xl, c = at
    x = xh * 2 + xl
    ys = [shifted(at, dy=step) for step in range(1, 4)]
    xs = [shifted(at, dx=step) for step in range(1, 4)]
    zs = [shifted(at, dz=step) for step in range(1, 4)]
    net.barrier(ys + xs + zs)
    wait = []
    for step in range(3):
        t = xs[step]
        columns = pl.ds(pl.multiple_of(t[0] * 384, 128), 384)
        wait.append(net.send(own_a.at[:, t[3], :, :, columns], all_a.at[x], t))
        t = zs[step]
        wait.append(net.send(own_b.at[t[2]], all_b.at[z], t))
        t = ys[step]
        wait.append(net.send(own_c.at[:, :, t[1]], all_c.at[y], t))
    columns = pl.ds(pl.multiple_of(xh * 384, 128), 384)
    wait.append(net.keep(own_a.at[:, xl, :, :, columns], all_a.at[x]))
    wait.append(net.keep(own_b.at[z], all_b.at[z]))
    wait.append(net.keep(own_c.at[:, :, y], all_c.at[y]))
    for copy in wait:
        copy.wait()


second_reduce = transfer(
    second_reduce_body,
    "second_reduce",
    4,
    [shape((4, 4, 2, 16, 384)), shape((4, 2, 64, 384)), shape((4, 2, 2, 16, 384))],
    9,
    3,
)


def finish_body(net, at, ins, outs):
    own_a, own_b, own_c, own_out, own_grad = ins
    got_a, got_b, got_c, all_a, all_b, all_c, out, grad = outs
    xh, y, z, xl, c = at
    x = xh * 2 + xl
    head = z * 2 + c
    quarter = xl * 2 + c
    zc = [shifted(at, dz=dz, dc=dc) for dz, dc in ZC]
    pairs = [shifted(at, flip_xl=1), shifted(at, flip_xl=1, dc=1)]
    replicas = [
        shifted(at, dy=dy, flip_xh=dx) for dy in range(YS) for dx in range(2) if (dy, dx) != (0, 0)
    ]
    sibling = shifted(at, dc=1)
    net.barrier(zc + pairs + replicas)

    def columns(index):
        return pl.ds(pl.multiple_of(index * 384, 128), 384)

    first = [net.send(own_a.at[t[2], t[4]], got_a.at[:, columns(head)], t) for t in zc]
    first.append(net.keep(own_a.at[z, c], got_a.at[:, columns(head)]))
    first.append(net.send(own_b.at[1 - c], got_b.at[:, columns(c)], sibling))
    first.append(net.keep(own_b.at[c], got_b.at[:, columns(c)]))
    for t in pairs + [sibling]:
        first.append(net.send(own_c.at[t[3], t[4]], got_c.at[:, columns(quarter)], t))
    first.append(net.keep(own_c.at[xl, c], got_c.at[:, columns(quarter)]))
    partner = pairs[0]
    last = [
        net.send(own_out.at[1 - xl], out.at[xl], partner),
        net.send(own_grad.at[1 - xl], grad.at[xl], partner),
        net.keep(own_out.at[xl], out.at[xl]),
        net.keep(own_grad.at[xl], grad.at[xl]),
    ]
    for copy in first:
        copy.wait()
    places = (
        (got_a, all_a.at[xh, pl.ds(pl.multiple_of(y * 16, 16), 16)]),
        (got_b, all_b.at[xh, y]),
        (got_c, all_c.at[xh, pl.ds(pl.multiple_of(y * 16, 16), 16)]),
    )
    for src, slot in places:
        for t in replicas:
            last.append(net.send(src, slot, t))
        last.append(net.keep(src, slot))
    for copy in last:
        copy.wait()


finish = transfer(
    finish_body,
    "finish",
    5,
    [
        shape((16, 3072)),
        shape((64, 768)),
        shape((16, 1536)),
        shape((2, 64, 3072)),
        shape((2, 4, 64, 768)),
        shape((2, 64, 1536)),
        shape((2, 64, 1024), F32),
        shape((2, 64, 1024), F32),
    ],
    7 + 1 + 3 + 2 + 21,
    8,
)


BLOCK = 256


def rope_tables():
    half = HD // 2
    frequency = ROPE_BASE ** (-(np.arange(half, dtype=np.float64) * 2.0 / HD))
    angles = np.arange(1024, dtype=np.float64)[:, None] * frequency[None, :]
    cosines = np.concatenate([np.cos(angles)] * 2, axis=1)
    sines = np.concatenate([-np.sin(angles), np.sin(angles)], axis=1)
    return (cosines.astype(np.float32), sines.astype(np.float32))


def dot_nt(left, right):
    return lax.dot_general(left, right, (((1,), (1,)), ((), ())), preferred_element_type=F32)


def dot_tn(left, right):
    return lax.dot_general(left, right, (((0,), (0,)), ((), ())), preferred_element_type=F32)


def mask_of(block, document_column, document_row):
    count = (block + 1) * BLOCK
    rows = slice(block * BLOCK, count)
    same = document_column[rows, :] == document_row[:, :count]
    row_at = block * BLOCK + lax.broadcasted_iota(jnp.int32, (BLOCK, count), 0)
    column_at = lax.broadcasted_iota(jnp.int32, (BLOCK, count), 1)
    return same & (row_at >= column_at)


def forward_kernel(
    row, query_weight, key_weight, value_weight, cosines, sines, query_gain, key_gain,
    document_column, document_row,
    attn_low, attended, raw, inverses, queries, keys, values, log_total,
    weights, sems,
):
    z, c = lax.axis_index("seq") // 4, lax.axis_index("seq") % 2
    head = z * 2 + c
    copies = []
    for i, (ref, start, width) in enumerate(
        ((query_weight, 0, 256), (key_weight, 256, 128), (value_weight, 384, 128))
    ):
        columns = pl.ds(pl.multiple_of(head * width, 128), width)
        copy = pltpu.make_async_copy(ref.at[:, columns], weights.at[:, pl.ds(start, width)], sems.at[i])
        copy.start()
        copies.append(copy)
    for copy in copies:
        copy.wait()
    for block in range(4):
        rows = slice(block * BLOCK, (block + 1) * BLOCK)
        product = jnp.dot(row[rows, :], weights[...], preferred_element_type=F32)
        raw[rows, :] = product[:, :384]
        values[rows, :] = product[:, 384:].astype(BF16)
        for part in range(3):
            vector = product[:, part * HD : (part + 1) * HD]
            gain = query_gain[...] if part < 2 else key_gain[...]
            inverse = lax.rsqrt(jnp.mean(vector * vector, axis=-1, keepdims=True) + EPSILON)
            inverses[rows, part : part + 1] = inverse
            normed = vector * inverse * gain
            turned = normed * cosines[rows, :] + pltpu.roll(normed, 64, 1) * sines[rows, :]
            if part < 2:
                queries[rows, part * HD : (part + 1) * HD] = turned.astype(BF16)
            else:
                keys[rows, :] = turned.astype(BF16)
    for block in range(4):
        rows = slice(block * BLOCK, (block + 1) * BLOCK)
        count = (block + 1) * BLOCK
        visible = mask_of(block, document_column, document_row)
        for h in range(2):
            head_columns = slice(h * HD, (h + 1) * HD)
            scores = dot_nt(queries[rows, head_columns], keys[:count, :])
            scores = jnp.where(visible, scores * (SCALE * LOG2E), MASKED)
            top = jnp.max(scores, axis=-1, keepdims=True)
            soft = jnp.exp2(scores - top)
            total = jnp.sum(soft, axis=-1, keepdims=True)
            mixed = jnp.dot(soft.astype(BF16), values[:count, :], preferred_element_type=F32) / total
            attended[rows, head_columns] = mixed
            attn_low[rows, head_columns] = mixed.astype(BF16)
            log_total[rows, h : h + 1] = top + jnp.log2(total)


def vmem(count):
    return [pl.BlockSpec(memory_space=pltpu.VMEM)] * count


def attention_forward(row, weights, tables, gains, document_column, document_row):
    return pl.pallas_call(
        forward_kernel,
        out_shape=[
            shape((1024, 256)),
            shape((1024, 256), F32),
            shape((1024, 384), F32),
            shape((1024, 3), F32),
            shape((1024, 256)),
            shape((1024, 128)),
            shape((1024, 128)),
            shape((1024, 2), F32),
        ],
        in_specs=vmem(1) + [pl.BlockSpec(memory_space=pl.ANY)] * 3 + vmem(6),
        out_specs=vmem(8),
        scratch_shapes=[pltpu.VMEM((1024, 512), BF16), pltpu.SemaphoreType.DMA((3,))],
        compiler_params=pltpu.CompilerParams(vmem_limit_bytes=48 * 2**20),
        name="attention_forward",
    )(row, *weights, *tables, *gains, document_column, document_row)


def backward_kernel(
    attn_grad, attended, raw, inverses, queries, keys, values, log_total,
    cosines, sines, query_gain, key_gain, document_column, document_row,
    lows, query_gain_grad, key_gain_grad,
    key_sum, value_sum,
):
    key_sum[...] = jnp.zeros_like(key_sum)
    value_sum[...] = jnp.zeros_like(value_sum)

    def norm_back(grad, part, rows, gain):
        turned = grad * cosines[rows, :] - pltpu.roll(grad, 64, 1) * sines[rows, :]
        inverse = inverses[rows, part : part + 1]
        normed = raw[rows, part * HD : (part + 1) * HD] * inverse
        scaled = turned * gain
        result = inverse * (scaled - normed * jnp.mean(scaled * normed, axis=-1, keepdims=True))
        return (result.astype(BF16), jnp.sum(turned * normed, axis=0, keepdims=True))

    query_total = jnp.zeros((1, HD), F32)
    for block in range(4):
        rows = slice(block * BLOCK, (block + 1) * BLOCK)
        count = (block + 1) * BLOCK
        visible = mask_of(block, document_column, document_row)
        for h in range(2):
            head_columns = slice(h * HD, (h + 1) * HD)
            query = queries[rows, head_columns]
            grad = attn_grad[rows, head_columns]
            delta = jnp.sum(grad.astype(F32) * attended[rows, head_columns], axis=-1, keepdims=True)
            scores = dot_nt(query, keys[:count, :]) * (SCALE * LOG2E)
            soft = jnp.exp2(jnp.where(visible, scores - log_total[rows, h : h + 1], MASKED))
            value_sum[:count, :] += dot_tn(soft.astype(BF16), grad)
            soft_grad = dot_nt(grad, values[:count, :])
            score_low = (soft * (soft_grad - delta)).astype(BF16)
            query_grad = jnp.dot(score_low, keys[:count, :], preferred_element_type=F32) * SCALE
            key_sum[:count, :] += dot_tn(score_low, query)
            low, gain_part = norm_back(query_grad, h, rows, query_gain[...])
            lows[rows, head_columns] = low
            query_total = query_total + gain_part
    query_gain_grad[...] = query_total
    key_total = jnp.zeros((1, HD), F32)
    for block in range(4):
        rows = slice(block * BLOCK, (block + 1) * BLOCK)
        low, gain_part = norm_back(key_sum[rows, :] * SCALE, 2, rows, key_gain[...])
        lows[rows, 256:384] = low
        lows[rows, 384:] = value_sum[rows, :].astype(BF16)
        key_total = key_total + gain_part
    key_gain_grad[...] = key_total


def attention_backward(*arrays):
    return pl.pallas_call(
        backward_kernel,
        out_shape=[shape((1024, 512)), shape((1, HD), F32), shape((1, HD), F32)],
        in_specs=vmem(len(arrays)),
        out_specs=vmem(3),
        scratch_shapes=[pltpu.VMEM((1024, HD), F32), pltpu.VMEM((1024, HD), F32)],
        compiler_params=pltpu.CompilerParams(vmem_limit_bytes=48 * 2**20),
        name="attention_backward",
    )(*arrays)


def normalize(vector, scales):
    inverse = lax.rsqrt(jnp.mean(vector * vector, axis=-1, keepdims=True) + EPSILON)
    return (vector * inverse * scales, inverse)


def norm_back(gradient, vector, inverse, scales):
    normed = vector * inverse
    scales_grad = jnp.sum(gradient * normed, axis=0)
    scaled = gradient * scales
    vector_grad = inverse * (scaled - normed * jnp.mean(scaled * normed, axis=-1, keepdims=True))
    return (vector_grad, scales_grad)


def einsum(spec, left, right):
    return jnp.einsum(spec, left, right, preferred_element_type=F32)


def per_device(
    hidden_in,
    query_weight,
    key_weight,
    value_weight,
    output_weight,
    gate_weight,
    up_weight,
    down_weight,
    query_gain,
    key_gain,
    attention_gain,
    feedforward_gain,
    document_ids,
    cotangent,
):
    xh, y, z, xl, c = place()
    documents = jnp.pad(document_ids, ((0, 0), (0, 64)))
    documents = jnp.broadcast_to(documents[:, None, :], (2, 8, 128))
    row_blocks, upstream, row_documents = gather_row(hidden_in, cotangent, documents)
    row = row_blocks.reshape(1024, 1024)
    row_documents = row_documents[:, :, :, 0, :64].reshape(1024)
    document_column, document_row = row_documents[:, None], row_documents[None, :]
    tables = rope_tables()
    gains = (query_gain[None, :], key_gain[None, :])
    attn_heads, attended, raw, inverses, queries, keys, values, log_total = attention_forward(
        row, (query_weight, key_weight, value_weight), tables, gains, document_column, document_row
    )
    (attn_tokens,) = attended_to_owners(attn_heads.reshape(4, 2, 2, 64, 256))
    attn_low = attn_tokens.reshape(128, 2048)
    tokens = lax.dynamic_slice(row_blocks, (z, 0, c, 0, 0), (1, 2, 1, 64, 1024)).reshape(128, 1024)

    branch = einsum("tj,dj->td", attn_low, output_weight)
    branch_normed, branch_inverse = normalize(branch, attention_gain)
    residual = tokens.astype(F32) + branch_normed
    residual_low = residual.astype(BF16)
    gate = jnp.dot(residual_low, gate_weight, preferred_element_type=F32)
    up_proj = jnp.dot(residual_low, up_weight, preferred_element_type=F32)
    sigmoid_gate = jax.nn.sigmoid(gate)
    activated = (gate * sigmoid_gate * up_proj).astype(BF16)
    down = einsum("tf,df->td", activated, down_weight)
    down_normed, down_inverse = normalize(down, feedforward_gain)
    layer_output = residual + down_normed
    upstream = upstream.reshape(128, 1024).astype(F32)
    down_grad, feedforward_gain_grad = norm_back(upstream, down, down_inverse, feedforward_gain)
    down_low = down_grad.astype(BF16)
    act_grad = jnp.dot(down_low, down_weight, preferred_element_type=F32)
    gate_low = (act_grad * up_proj * sigmoid_gate * (1.0 + gate * (1.0 - sigmoid_gate))).astype(BF16)
    up_low = (act_grad * gate * sigmoid_gate).astype(BF16)
    residual_grad = upstream + einsum("tf,df->td", gate_low, gate_weight)
    residual_grad = residual_grad + einsum("tf,df->td", up_low, up_weight)
    branch_grad, attention_gain_grad = norm_back(residual_grad, branch, branch_inverse, attention_gain)
    branch_low = branch_grad.astype(BF16)
    attn_grad = jnp.dot(branch_low, output_weight, preferred_element_type=F32).astype(BF16)

    def by_columns(array):
        return jnp.swapaxes(array.reshape(128, 8, 384), 0, 1).reshape(4, 2, 128, 384)

    gate_up = jnp.stack([by_columns(gate_low), by_columns(up_low)], axis=2)
    attn_grad_row, branch_row, residual_all, gate_up_all, down_all, activated_all = spread(
        attn_grad.reshape(2, 64, 2048),
        branch_low.reshape(2, 64, 1024),
        residual_low,
        gate_up,
        down_low,
        by_columns(activated),
    )
    lows, query_gain_grad, key_gain_grad = attention_backward(
        attn_grad_row.reshape(1024, 256), attended, raw, inverses, queries, keys, values, log_total,
        *tables, *gains, document_column, document_row,
    )

    residual_all = residual_all.reshape(1024, 1024)
    gate_all = gate_up_all[:, :, 0].reshape(1024, 384)
    up_all = gate_up_all[:, :, 1].reshape(1024, 384)
    own_a = jnp.concatenate(
        [
            einsum("tc,tf->cf", row, lows).astype(BF16),
            einsum("tc,tf->cf", branch_row.reshape(1024, 1024), attn_heads).astype(BF16),
        ],
        axis=1,
    )
    own_b = jnp.concatenate(
        [
            einsum("tc,tf->cf", residual_all, gate_all).astype(BF16),
            einsum("tc,tf->cf", residual_all, up_all).astype(BF16),
        ],
        axis=1,
    )
    own_c = einsum(
        "tc,tf->cf", down_all.reshape(1024, 1024), activated_all.reshape(1024, 384)
    ).astype(BF16)
    low_tokens, all_a, all_b, all_c = first_reduce(
        lows.reshape(4, 2, 2, 64, 512),
        own_a.reshape(4, 2, 2, 4, 16, 768),
        own_b.reshape(4, 2, 2, 64, 768),
        own_c.reshape(4, 256, 384),
    )

    def total(array):
        return jnp.sum(array.astype(F32), axis=0).astype(BF16)

    all_a, all_b, all_c = second_reduce(
        total(all_a), total(all_b), total(all_c).reshape(2, 2, 4, 16, 384)
    )
    low_tokens = low_tokens.reshape(8, 128, 512)
    query_low = jnp.swapaxes(low_tokens[:, :, :256], 0, 1).reshape(128, 2048)
    key_low = jnp.swapaxes(low_tokens[:, :, 256:384], 0, 1).reshape(128, 1024)
    value_low = jnp.swapaxes(low_tokens[:, :, 384:], 0, 1).reshape(128, 1024)
    input_grad = residual_grad + einsum("tj,dj->td", query_low, query_weight)
    input_grad = input_grad + einsum("tj,dj->td", key_low, key_weight)
    input_grad = input_grad + einsum("tj,dj->td", value_low, value_weight)
    _, _, _, all_a, all_b, all_c, out, grad = finish(
        total(all_a),
        total(all_b),
        total(all_c),
        layer_output.reshape(2, 64, 1024),
        input_grad.reshape(2, 64, 1024),
    )
    heads_first = all_a[0].reshape(64, 8, 384)
    heads_last = all_a[1].reshape(64, 8, 384)
    hidden_units = jnp.swapaxes(all_b, 1, 2).reshape(2, 64, 3072)
    gain_totals = lax.psum(
        (query_gain_grad[0], key_gain_grad[0], attention_gain_grad, feedforward_gain_grad),
        ("rows", "seq"),
    )
    return (
        out,
        grad,
        heads_first[:, :, :256].reshape(64, 2048).astype(F32),
        heads_first[:, :, 256:].reshape(64, 1024).astype(F32),
        heads_last[:, :, :128].reshape(64, 1024).astype(F32),
        heads_last[:, :, 128:].reshape(64, 2048).astype(F32),
        hidden_units[0].astype(F32),
        hidden_units[1].astype(F32),
        jnp.swapaxes(all_c, 0, 1).reshape(64, 3072).astype(F32),
    ) + gain_totals


def solution(mesh):
    tokens = P("rows", "seq", None)
    split = P("seq", None)
    return jax.shard_map(
        per_device,
        mesh=mesh,
        in_specs=(tokens,) + (P(),) * 11 + (P("rows", "seq"), tokens),
        out_specs=(tokens, tokens) + (split,) * 7 + (P(),) * 4,
        check_vma=False,
    )
```

```python
import functools

import jax
import jax.numpy as jnp
import numpy as np
from jax import lax
from jax.experimental import pallas as pl
from jax.experimental.pallas import tpu as pltpu
from jax.sharding import PartitionSpec as P

HD = 128
EPSILON = 1e-06
ROPE_BASE = 1000000.0
MASKED = -1e30
LOG2E = 1.4426950408889634
SCALE = HD ** (-0.5)
MESH = pl.DeviceIdType.MESH
F32 = jnp.float32
BF16 = jnp.bfloat16

YS = 4
ZS = 4
XS = 4


def place():
    rows, seq = lax.axis_index("rows"), lax.axis_index("seq")
    return (rows // YS, rows % YS, seq // 4, (seq // 2) % 2, seq % 2)


def device(xh, y, z, xl, c):
    return (xh * YS + y, z * 4 + xl * 2 + c)


def shifted(at, dx=0, dy=0, dz=0, dc=0, flip_xl=0, flip_xh=0):
    xh, y, z, xl, c = at
    if dx:
        x = (xh * 2 + xl + dx) % XS
        xh, xl = x // 2, x % 2
    if flip_xl:
        xl = 1 - xl
    if flip_xh:
        xh = 1 - xh
    if dc:
        c = 1 - c
    return (xh, (y + dy) % YS, (z + dz) % ZS, xl, c)


class Landing:
    def __init__(self, copy):
        self.copy, self.here = copy, False

    def arrive(self):
        if not self.here:
            self.copy.wait_recv()
            self.here = True


class Net:
    def __init__(self, send_sems, recv_sems, local_sems):
        self.send_sems, self.recv_sems, self.local_sems = send_sems, recv_sems, local_sems
        self.sent, self.kept = [], 0

    def barrier(self, targets):
        barrier = pltpu.get_barrier_semaphore()
        for target in targets:
            pl.semaphore_signal(barrier, inc=1, device_id=device(*target), device_id_type=MESH)
        pl.semaphore_wait(barrier, len(targets))

    def send(self, src, dst, target):
        i = len(self.sent)
        copy = pltpu.make_async_remote_copy(
            src_ref=src,
            dst_ref=dst,
            send_sem=self.send_sems.at[i],
            recv_sem=self.recv_sems.at[i],
            device_id=device(*target),
            device_id_type=MESH,
        )
        copy.start()
        self.sent.append(Landing(copy))
        return self.sent[-1]

    def keep(self, src, dst):
        copy = pltpu.make_async_copy(src, dst, self.local_sems.at[self.kept])
        self.kept += 1
        copy.start()
        return copy

    def drain(self):
        for landing in self.sent:
            landing.arrive()
            landing.copy.wait_send()


def shape(dims, dtype=BF16):
    return jax.ShapeDtypeStruct(dims, dtype)


ZC = [(dz, dc) for dz in range(ZS) for dc in range(2) if (dz, dc) != (0, 0)]
ORDER = (0, 1, 3, 2)
BLOCK = 256
SENDS = 188
KEEPS = 64


def rope_tables():
    half = HD // 2
    frequency = ROPE_BASE ** (-(np.arange(half, dtype=np.float64) * 2.0 / HD))
    angles = np.arange(1024, dtype=np.float64)[:, None] * frequency[None, :]
    cosines = np.concatenate([np.cos(angles)] * 2, axis=1)
    sines = np.concatenate([-np.sin(angles), np.sin(angles)], axis=1)
    return (cosines.astype(np.float32), sines.astype(np.float32))


def dot_nn(left, right):
    return jnp.dot(left, right, preferred_element_type=F32)


def dot_nt(left, right):
    return lax.dot_general(left, right, (((1,), (1,)), ((), ())), preferred_element_type=F32)


def dot_tn(left, right):
    return lax.dot_general(left, right, (((0,), (0,)), ((), ())), preferred_element_type=F32)


def normalize(vector, scales):
    inverse = lax.rsqrt(jnp.mean(vector * vector, axis=-1, keepdims=True) + EPSILON)
    return (vector * inverse * scales, inverse)


def norm_back(gradient, vector, inverse, scales):
    normed = vector * inverse
    scales_grad = jnp.sum(gradient * normed, axis=0, keepdims=True)
    scaled = gradient * scales
    vector_grad = inverse * (scaled - normed * jnp.mean(scaled * normed, axis=-1, keepdims=True))
    return (vector_grad, scales_grad)


def aligned(index, width):
    return pl.ds(pl.multiple_of(index * width, width), width)


class Refs:
    pass


INPUTS = (
    "hidden", "cotangent", "documents",
    "query_weight", "key_weight", "value_weight", "output_weight", "gate_weight", "up_weight", "down_weight",
    "cosines", "sines", "query_gain", "key_gain", "attention_gain", "feedforward_gain",
)
IN_VMEM = ("cosines", "sines", "query_gain", "key_gain", "attention_gain", "feedforward_gain")
OUTPUTS = (
    ("out", (2, 64, 1024), F32),
    ("grad", (2, 64, 1024), F32),
    ("wide", (2, 64, 2048), BF16),
    ("narrow", (2, 64, 1024), BF16),
    ("gate_up_grad", (2, 64, 3072), BF16),
    ("down_grad", (64, 3072), BF16),
    ("gains", (24, 128), F32),
    ("residual_all", (1024, 1024), BF16),
    ("gate_up_all", (1024, 768), BF16),
    ("down_all", (1024, 1024), BF16),
    ("activated_all", (1024, 384), BF16),
)
SCRATCH = (
    ("head_weights", (1024, 512), BF16),
    ("wo", (1024, 2048), BF16),
    ("wgu", (1024, 6144), BF16),
    ("wd", (1024, 3072), BF16),
    ("row", (4, 2, 2, 64, 1024), BF16),
    ("upstream", (2, 64, 1024), BF16),
    ("row_documents", (4, 2, 2, 8, 128), F32),
    ("document_column", (1024, 128), F32),
    ("raw", (1024, 384), F32),
    ("inverses", (1024, 3), F32),
    ("queries", (1024, 256), BF16),
    ("keys", (1024, 128), BF16),
    ("values", (1024, 128), BF16),
    ("attended", (1024, 256), F32),
    ("attn_heads", (4, 2, 2, 64, 256), BF16),
    ("log_total", (1024, 2), F32),
    ("attn_tokens", (2, 64, 2048), BF16),
    ("branch", (128, 1024), F32),
    ("residual", (128, 1024), F32),
    ("residual_low", (128, 1024), BF16),
    ("gate_factor", (128, 3072), F32),
    ("up_factor", (128, 3072), F32),
    ("activated", (128, 3072), BF16),
    ("layer_output", (2, 64, 1024), F32),
    ("down_low", (128, 1024), BF16),
    ("gate_up_low", (128, 6144), BF16),
    ("residual_grad", (128, 1024), F32),
    ("branch_low", (2, 64, 1024), BF16),
    ("attn_grad", (2, 64, 2048), BF16),
    ("attn_grad_row", (4, 2, 2, 64, 256), BF16),
    ("branch_row", (4, 2, 2, 64, 1024), BF16),
    ("lows", (4, 2, 2, 64, 512), BF16),
    ("key_sum", (1024, 128), F32),
    ("value_sum", (1024, 128), F32),
    ("low_tokens", (2, 64, 4096), BF16),
    ("input_grad", (2, 64, 1024), F32),
    ("own_a", (4, 2, 2, 4, 16, 768), BF16),
    ("own_b", (4, 2, 2, 64, 768), BF16),
    ("own_c", (4, 2, 2, 4, 16, 384), BF16),
    ("all_a", (3, 4, 2, 2, 16, 768), BF16),
    ("all_b", (3, 4, 2, 64, 384), BF16),
    ("all_c", (3, 2, 2, 4, 16, 384), BF16),
    ("next_a", (4, 2, 2, 16, 768), BF16),
    ("next_b", (4, 2, 64, 384), BF16),
    ("next_c", (2, 2, 4, 16, 384), BF16),
    ("then_a", (3, 4, 2, 16, 384), BF16),
    ("then_b", (3, 2, 64, 384), BF16),
    ("then_c", (3, 2, 2, 16, 384), BF16),
    ("done_a", (4, 2, 16, 384), BF16),
    ("done_b", (2, 64, 384), BF16),
    ("done_c", (2, 2, 16, 384), BF16),
    ("got_wide", (16, 2048), BF16),
    ("got_narrow", (16, 1024), BF16),
    ("got_b", (64, 768), BF16),
    ("got_c", (16, 1536), BF16),
    ("gains_own", (24, 128), F32),
    ("gains_next", (24, 128), F32),
    ("gains_last", (24, 128), F32),
    ("gains_final", (24, 128), F32),
    ("gains_y", (3, 24, 128), F32),
    ("gains_x", (3, 24, 128), F32),
    ("gains_zc", (7, 24, 128), F32),
)


def layer_kernel(*refs):
    names = INPUTS + tuple(n for n, _, _ in OUTPUTS) + tuple(n for n, _, _ in SCRATCH)
    r = Refs()
    for name, ref in zip(names, refs):
        setattr(r, name, ref)
    net = Net(*refs[len(names) :])
    at = place()
    xh, y, z, xl, c = at
    x = xh * 2 + xl
    head = z * 2 + c
    sibling = shifted(at, dc=1)
    partner = shifted(at, flip_xl=1)
    seq_others = [
        shifted(at, dz=dz, dc=dc, flip_xl=dx)
        for dz in range(ZS)
        for dx in range(2)
        for dc in range(2)
        if (dz, dx, dc) != (0, 0, 0)
    ]
    zc = [shifted(at, dz=dz, dc=dc) for dz, dc in ZC]
    yc = [shifted(at, dy=dy, dc=dc) for dy, dc in ZC]
    xc = [shifted(at, dx=dx, dc=dc) for dx, dc in ZC]
    ys = [shifted(at, dy=step) for step in range(1, 4)]
    xs = [shifted(at, dx=step) for step in range(1, 4)]
    zs = [shifted(at, dz=step) for step in range(1, 4)]
    replicas = [
        shifted(at, dy=dy, flip_xh=dx) for dy in range(YS) for dx in range(2) if (dy, dx) != (0, 0)
    ]

    loads = [
        net.keep(ref.at[:, aligned(head, width)], r.head_weights.at[:, pl.ds(start, width)])
        for ref, start, width in (
            (r.query_weight, 0, 256),
            (r.key_weight, 256, 128),
            (r.value_weight, 384, 128),
        )
    ]
    load_wo = net.keep(r.output_weight, r.wo)
    load_wgu = [
        net.keep(r.gate_weight, r.wgu.at[:, pl.ds(0, 3072)]),
        net.keep(r.up_weight, r.wgu.at[:, pl.ds(3072, 3072)]),
    ]
    load_wd = net.keep(r.down_weight, r.wd)

    barrier_targets = list(seq_others) + yc[1:] + xc[1:] + replicas
    net.barrier(barrier_targets)
    direct = {}
    for dz in (0, 1, 3, 2):
        for dx in range(2):
            if (dz, dx) != (0, 0):
                target = shifted(at, dz=dz, flip_xl=dx)
                direct[dz, dx] = net.send(r.hidden.at[target[3]], r.row.at[z, xl, c], target)
    own_block = net.keep(r.hidden.at[xl], r.row.at[z, xl, c])
    document_landings = [
        net.send(r.documents.at[t[3]], r.row_documents.at[z, xl, c], t) for t in seq_others
    ]
    document_landings_own = net.keep(r.documents.at[xl], r.row_documents.at[z, xl, c])
    upstream_landing = net.send(r.cotangent.at[1 - xl], r.upstream.at[xl], partner)
    upstream_own = net.keep(r.cotangent.at[xl], r.upstream.at[xl])

    forwarded = {}

    def forward_blocks(dz):
        source = (z - dz) % ZS
        for dx in range(2):
            if (dz, dx) == (0, 0):
                own_block.wait()
            else:
                direct[dz, dx].arrive()
            block = r.row.at[source, (xl + dx) % 2, c]
            forwarded[dz, dx] = net.send(block, block, sibling)

    def project(dz):
        source = (z - dz) % ZS
        for dx in range(2):
            forwarded[dz, dx].arrive()
        rows = aligned(source, BLOCK)
        product = dot_nn(r.row[source].reshape(BLOCK, 1024), r.head_weights[...])
        r.raw[rows, :] = product[:, :384]
        r.values[rows, :] = product[:, 384:].astype(BF16)
        for part in range(3):
            gain = r.query_gain[...] if part < 2 else r.key_gain[...]
            normed, inverse = normalize(product[:, part * HD : (part + 1) * HD], gain)
            r.inverses[rows, part : part + 1] = inverse
            turned = normed * r.cosines[rows, :] + pltpu.roll(normed, 64, 1) * r.sines[rows, :]
            if part < 2:
                r.queries[rows, part * HD : (part + 1) * HD] = turned.astype(BF16)
            else:
                r.keys[rows, :] = turned.astype(BF16)

    for load in loads:
        load.wait()
    forward_blocks(0)
    forward_blocks(1)
    project(0)
    forward_blocks(3)
    project(1)
    forward_blocks(2)
    project(3)
    for landing in document_landings:
        landing.arrive()
    document_landings_own.wait()
    lane = lax.broadcasted_iota(jnp.int32, (1, 128), 1)
    pieces = []
    for block in range(8):
        even = r.row_documents[block // 2, block % 2, 0, 0:1, :]
        odd = r.row_documents[block // 2, block % 2, 1, 0:1, :]
        piece = jnp.where(lane < 64, even, odd)
        pieces.append(piece)
        r.document_column[block * 128 : (block + 1) * 128, :] = jnp.broadcast_to(piece, (128, 128)).T
    document_row = jnp.concatenate(pieces, axis=1)
    project(2)

    def visible_in(block):
        count = (block + 1) * BLOCK
        rows = slice(block * BLOCK, count)
        same = r.document_column[rows, 0:1] == document_row[:, :count]
        row_at = block * BLOCK + lax.broadcasted_iota(jnp.int32, (BLOCK, count), 0)
        column_at = lax.broadcasted_iota(jnp.int32, (BLOCK, count), 1)
        return same & (row_at >= column_at)

    attn_landings = []
    for h in range(2):
        columns = slice(h * HD, (h + 1) * HD)
        for block in range(4):
            rows = slice(block * BLOCK, (block + 1) * BLOCK)
            count = (block + 1) * BLOCK
            scores = dot_nt(r.queries[rows, columns], r.keys[:count, :])
            scores = jnp.where(visible_in(block), scores * (SCALE * LOG2E), MASKED)
            top = jnp.max(scores, axis=-1, keepdims=True)
            soft = jnp.exp2(scores - top)
            total = jnp.sum(soft, axis=-1, keepdims=True)
            mixed = dot_nn(soft.astype(BF16), r.values[:count, :]) / total
            r.attended[rows, columns] = mixed
            r.attn_heads[block, :, :, :, columns] = mixed.astype(BF16).reshape(2, 2, 64, HD)
            r.log_total[rows, h : h + 1] = top + jnp.log2(total)
        here = pl.ds(pl.multiple_of(head * 256 + h * HD, HD), HD)
        for t in zc:
            attn_landings.append(
                net.send(r.attn_heads.at[t[2], :, t[4], :, pl.ds(h * HD, HD)], r.attn_tokens.at[:, :, here], t)
            )
        attn_landings.append(
            net.keep(r.attn_heads.at[z, :, c, :, pl.ds(h * HD, HD)], r.attn_tokens.at[:, :, here])
        )
    for landing in attn_landings:
        landing.arrive() if isinstance(landing, Landing) else landing.wait()

    def chain(axis, src, slot_of):
        steps = []
        for step in (1, 3, 2):
            shift = {"d" + axis: step}
            back = {"d" + axis: -step}
            source = shifted(at, **back)
            steps.append((net.send(src, slot_of(at), shifted(at, **shift)), slot_of(source)))
        last = [net.send(src, slot_of(at), sibling)]
        own = net.keep(src, slot_of(at))
        return (steps, last, own)

    def chain_forward(state):
        steps, last, own = state
        for landing, slot in steps:
            landing.arrive()
            last.append(net.send(slot, slot, sibling))

    def chain_arrive(state):
        steps, last, own = state
        for landing in last:
            landing.arrive()
        own.wait()

    load_wo.wait()
    branch = dot_nt(r.wo[...], r.attn_tokens[...].reshape(128, 2048)).T
    r.branch[...] = branch
    branch_normed, branch_inverse = normalize(branch, r.attention_gain[...])
    residual = r.row[z, :, c].reshape(128, 1024).astype(F32) + branch_normed
    r.residual[...] = residual
    r.residual_low[...] = residual.astype(BF16)
    residual_chain = chain(
        "y", r.residual_low, lambda who: r.residual_all.at[aligned(who[1] * 2 + who[4], 128), :]
    )
    for load in load_wgu:
        load.wait()
    for tile in range(6):
        columns = slice(tile * 512, (tile + 1) * 512)
        up_columns = slice(3072 + tile * 512, 3072 + (tile + 1) * 512)
        gate = dot_nn(r.residual_low[...], r.wgu[:, columns])
        up = dot_nn(r.residual_low[...], r.wgu[:, up_columns])
        sigmoid_gate = lax.logistic(gate)
        silu = gate * sigmoid_gate
        r.activated[:, columns] = (silu * up).astype(BF16)
        r.up_factor[:, columns] = silu
        r.gate_factor[:, columns] = up * sigmoid_gate * (1.0 + gate * (1.0 - sigmoid_gate))

    x_slot = aligned(x * 2 + c, 128)
    y_slot = aligned(y * 2 + c, 128)
    activated_landings = [
        net.send(
            r.activated.at[:, aligned((t[0] * 2 + t[3]) * 2 + t[4], 384)], r.activated_all.at[x_slot, :], t
        )
        for t in xc
    ]
    activated_own = net.keep(r.activated.at[:, aligned(x * 2 + c, 384)], r.activated_all.at[x_slot, :])
    load_wd.wait()
    down = dot_nt(r.wd[...], r.activated[...]).T
    upstream_landing.arrive()
    upstream_own.wait()
    down_normed, down_inverse = normalize(down, r.feedforward_gain[...])
    r.layer_output[...] = (r.residual[...] + down_normed).reshape(2, 64, 1024)
    upstream = r.upstream[...].reshape(128, 1024).astype(F32)
    down_grad, feedforward_gain_grad = norm_back(upstream, down, down_inverse, r.feedforward_gain[...])
    r.down_low[...] = down_grad.astype(BF16)
    down_chain = chain(
        "x", r.down_low, lambda who: r.down_all.at[aligned((who[0] * 2 + who[3]) * 2 + who[4], 128), :]
    )
    for tile in range(6):
        columns = slice(tile * 512, (tile + 1) * 512)
        up_columns = slice(3072 + tile * 512, 3072 + (tile + 1) * 512)
        act_grad = dot_nn(r.down_low[...], r.wd[:, columns])
        r.gate_up_low[:, columns] = (act_grad * r.gate_factor[:, columns]).astype(BF16)
        r.gate_up_low[:, up_columns] = (act_grad * r.up_factor[:, columns]).astype(BF16)
    chain_forward(residual_chain)
    gate_up_landings = []
    for part in range(2):
        for t in yc:
            gate_up_landings.append(
                net.send(
                    r.gate_up_low.at[:, aligned(part * 8 + t[1] * 2 + t[4], 384)],
                    r.gate_up_all.at[y_slot, pl.ds(part * 384, 384)],
                    t,
                )
            )
    gate_up_own = [
        net.keep(
            r.gate_up_low.at[:, aligned(part * 8 + y * 2 + c, 384)],
            r.gate_up_all.at[y_slot, pl.ds(part * 384, 384)],
        )
        for part in range(2)
    ]
    residual_grad = upstream + dot_nt(r.wgu[...], r.gate_up_low[...]).T
    r.residual_grad[...] = residual_grad
    branch_grad, attention_gain_grad = norm_back(
        residual_grad, r.branch[...], branch_inverse, r.attention_gain[...]
    )
    for i in range(8):
        r.gains_own[i : i + 1, :] = attention_gain_grad[:, i * 128 : (i + 1) * 128]
        r.gains_own[8 + i : 9 + i, :] = feedforward_gain_grad[:, i * 128 : (i + 1) * 128]
    branch_low = branch_grad.astype(BF16)
    r.branch_low[...] = branch_low.reshape(2, 64, 1024)
    r.attn_grad[...] = dot_nn(branch_low, r.wo[...]).astype(BF16).reshape(2, 64, 2048)
    attn_grad_landings = [
        net.send(r.attn_grad.at[:, :, aligned(t[2] * 2 + t[4], 256)], r.attn_grad_row.at[z, :, c], t)
        for t in zc
    ]
    attn_grad_own = net.keep(r.attn_grad.at[:, :, aligned(head, 256)], r.attn_grad_row.at[z, :, c])
    branch_chain = chain("z", r.branch_low, lambda who: r.branch_row.at[who[2], :, who[4]])
    out_landing = net.send(r.layer_output.at[1 - xl], r.out.at[xl], partner)
    out_own = net.keep(r.layer_output.at[xl], r.out.at[xl])
    head_loads = []
    for i in range(8):
        for ref, start, width in (
            (r.query_weight, 0, 256),
            (r.key_weight, 256, 128),
            (r.value_weight, 384, 128),
        ):
            head_loads.append(
                net.keep(ref.at[:, pl.ds(i * width, width)], r.wgu.at[:, pl.ds(i * 512 + start, width)])
            )
    chain_forward(down_chain)

    r.key_sum[...] = jnp.zeros_like(r.key_sum)
    r.value_sum[...] = jnp.zeros_like(r.value_sum)
    for landing in attn_grad_landings:
        landing.arrive()
    attn_grad_own.wait()

    def rope_norm_back(grad, part, rows, gain):
        turned = grad * r.cosines[rows, :] - pltpu.roll(grad, 64, 1) * r.sines[rows, :]
        vector = r.raw[rows, part * HD : (part + 1) * HD]
        result, gain_part = norm_back(turned, vector, r.inverses[rows, part : part + 1], gain)
        return (result.astype(BF16).reshape(2, 2, 64, HD), gain_part)

    query_total = jnp.zeros((1, HD), F32)
    for block in range(4):
        rows = slice(block * BLOCK, (block + 1) * BLOCK)
        count = (block + 1) * BLOCK
        visible = visible_in(block)
        for h in range(2):
            columns = slice(h * HD, (h + 1) * HD)
            query = r.queries[rows, columns]
            grad = r.attn_grad_row[block, :, :, :, columns].reshape(BLOCK, HD)
            delta = jnp.sum(grad.astype(F32) * r.attended[rows, columns], axis=-1, keepdims=True)
            scores = dot_nt(query, r.keys[:count, :]) * (SCALE * LOG2E)
            soft = jnp.exp2(jnp.where(visible, scores - r.log_total[rows, h : h + 1], MASKED))
            r.value_sum[:count, :] += dot_tn(soft.astype(BF16), grad)
            soft_grad = dot_nt(grad, r.values[:count, :])
            score_low = (soft * (soft_grad - delta)).astype(BF16)
            query_grad = dot_nn(score_low, r.keys[:count, :]) * SCALE
            r.key_sum[:count, :] += dot_tn(score_low, query)
            low, gain_part = rope_norm_back(query_grad, h, rows, r.query_gain[...])
            r.lows[block, :, :, :, columns] = low
            query_total = query_total + gain_part
    key_total = jnp.zeros((1, HD), F32)
    for block in range(4):
        rows = slice(block * BLOCK, (block + 1) * BLOCK)
        low, gain_part = rope_norm_back(r.key_sum[rows, :] * SCALE, 2, rows, r.key_gain[...])
        r.lows[block, :, :, :, 256:384] = low
        r.lows[block, :, :, :, 384:] = r.value_sum[rows, :].astype(BF16).reshape(2, 2, 64, HD)
        key_total = key_total + gain_part
    r.gains_own[16:17, :] = query_total
    r.gains_own[17:18, :] = key_total
    r.gains_own[18:24, :] = jnp.zeros((6, 128), F32)
    low_landings = [
        net.send(r.lows.at[t[2], :, t[4]], r.low_tokens.at[:, :, aligned(head, 512)], t) for t in zc
    ]
    low_own = net.keep(r.lows.at[z, :, c], r.low_tokens.at[:, :, aligned(head, 512)])
    gains_y = [net.send(r.gains_own, r.gains_y.at[i], ys[i]) for i in range(3)]

    chain_forward(branch_chain)
    row = r.row[...].reshape(1024, 1024)
    low_columns = dot_tn(row, r.lows[...].reshape(1024, 512)).astype(BF16)
    r.own_a[..., 0:384] = low_columns[:, :384].reshape(4, 2, 2, 4, 16, 384)
    r.own_a[..., 640:768] = low_columns[:, 384:].reshape(4, 2, 2, 4, 16, 128)
    chain_arrive(residual_chain)
    for landing in gate_up_landings:
        landing.arrive()
    for copy in gate_up_own:
        copy.wait()
    load_b = [
        net.keep(r.residual_all, r.wo.at[:, pl.ds(0, 1024)]),
        net.keep(r.gate_up_all, r.wd.at[:, pl.ds(0, 768)]),
    ]
    chain_arrive(branch_chain)
    output_columns = dot_tn(
        r.branch_row[...].reshape(1024, 1024), r.attn_heads[...].reshape(1024, 256)
    ).astype(BF16)
    r.own_a[..., 384:640] = output_columns.reshape(4, 2, 2, 4, 16, 256)
    first_a = [net.send(r.own_a.at[:, :, :, ys[i][1]], r.all_a.at[i], ys[i]) for i in range(3)]
    for load in load_b:
        load.wait()
    r.own_b[...] = dot_tn(r.wo[:, :1024], r.wd[:, :768]).astype(BF16).reshape(4, 2, 2, 64, 768)
    first_b = [
        net.send(r.own_b.at[:, t[3], :, :, aligned(t[0], 384)], r.all_b.at[i], t) for i, t in enumerate(xs)
    ]
    chain_arrive(down_chain)
    for landing in activated_landings:
        landing.arrive()
    activated_own.wait()
    load_c = [
        net.keep(r.down_all, r.wo.at[:, pl.ds(1024, 1024)]),
        net.keep(r.activated_all, r.wd.at[:, pl.ds(768, 384)]),
    ]
    for load in load_c:
        load.wait()
    r.own_c[...] = dot_tn(r.wo[:, 1024:], r.wd[:, 768:1152]).astype(BF16).reshape(4, 2, 2, 4, 16, 384)
    first_c = [net.send(r.own_c.at[t[2]], r.all_c.at[i], t) for i, t in enumerate(zs)]

    for load in head_loads:
        load.wait()
    for landing in low_landings:
        landing.arrive()
    low_own.wait()
    input_grad = r.residual_grad[...] + dot_nt(r.wgu[:, :4096], r.low_tokens[...].reshape(128, 4096)).T
    r.input_grad[...] = input_grad.reshape(2, 64, 1024)
    grad_landing = net.send(r.input_grad.at[1 - xl], r.grad.at[xl], partner)
    grad_own = net.keep(r.input_grad.at[xl], r.grad.at[xl])

    def total(own, others, landings):
        for landing in landings:
            landing.arrive()
        result = own.astype(F32)
        for i in range(len(landings)):
            result = result + others[i].astype(F32)
        return result

    r.gains_next[...] = total(r.gains_own[...], r.gains_y, gains_y)
    gains_x = [net.send(r.gains_next, r.gains_x.at[i], xs[i]) for i in range(3)]
    r.next_c[...] = total(r.own_c[z], r.all_c, first_c).astype(BF16)
    then_c = [net.send(r.next_c.at[:, :, t[1]], r.then_c.at[i], t) for i, t in enumerate(ys)]
    mine = aligned(xh, 384)
    r.next_b[...] = total(r.own_b[:, xl, :, :, mine], r.all_b, first_b).astype(BF16)
    then_b = [net.send(r.next_b.at[t[2]], r.then_b.at[i], t) for i, t in enumerate(zs)]
    r.next_a[...] = total(r.own_a[:, :, :, y], r.all_a, first_a).astype(BF16)
    then_a = [
        net.send(r.next_a.at[:, t[3], :, :, aligned(t[0], 384)], r.then_a.at[i], t) for i, t in enumerate(xs)
    ]

    r.done_c[...] = total(r.next_c[:, :, y], r.then_c, then_c).astype(BF16)
    quarter = aligned(xl * 2 + c, 384)
    pairs = [partner, shifted(at, flip_xl=1, dc=1), sibling]
    got_c = [net.send(r.done_c.at[t[3], t[4]], r.got_c.at[:, quarter], t) for t in pairs]
    got_c_own = net.keep(r.done_c.at[xl, c], r.got_c.at[:, quarter])
    r.done_b[...] = total(r.next_b[z], r.then_b, then_b).astype(BF16)
    got_b = net.send(r.done_b.at[1 - c], r.got_b.at[:, aligned(c, 384)], sibling)
    got_b_own = net.keep(r.done_b.at[c], r.got_b.at[:, aligned(c, 384)])
    r.gains_last[...] = total(r.gains_next[...], r.gains_x, gains_x)
    gains_zc = [net.send(r.gains_last, r.gains_zc.at[i], t) for i, t in enumerate(zc)]
    r.done_a[...] = total(r.next_a[:, xl, :, :, mine], r.then_a, then_a).astype(BF16)
    got_a = []
    for t in zc:
        got_a.append(net.send(r.done_a.at[t[2], t[4], :, pl.ds(0, 256)], r.got_wide.at[:, aligned(head, 256)], t))
        got_a.append(net.send(r.done_a.at[t[2], t[4], :, pl.ds(256, 128)], r.got_narrow.at[:, aligned(head, 128)], t))
    got_a_own = [
        net.keep(r.done_a.at[z, c, :, pl.ds(0, 256)], r.got_wide.at[:, aligned(head, 256)]),
        net.keep(r.done_a.at[z, c, :, pl.ds(256, 128)], r.got_narrow.at[:, aligned(head, 128)]),
    ]

    ending = []

    def spread(src, slot):
        for t in replicas:
            ending.append(net.send(src, slot, t))
        ending.append(net.keep(src, slot))

    got_b.arrive()
    got_b_own.wait()
    spread(r.got_b, r.gate_up_grad.at[xh, :, aligned(y, 768)])
    for landing in got_c:
        landing.arrive()
    got_c_own.wait()
    spread(r.got_c, r.down_grad.at[aligned(y, 16), aligned(xh, 1536)])
    for landing in got_a:
        landing.arrive()
    for copy in got_a_own:
        copy.wait()
    spread(r.got_wide, r.wide.at[xh, aligned(y, 16), :])
    spread(r.got_narrow, r.narrow.at[xh, aligned(y, 16), :])
    r.gains_final[...] = total(r.gains_last[...], r.gains_zc, gains_zc)
    gains_out = net.keep(r.gains_final, r.gains)
    for item in ending:
        if not isinstance(item, Landing):
            item.wait()
    for copy in (out_own, grad_own, gains_out):
        copy.wait()
    net.drain()


def layer(*arrays):
    return pl.pallas_call(
        layer_kernel,
        out_shape=[shape(dims, dtype) for _, dims, dtype in OUTPUTS],
        in_specs=[
            pl.BlockSpec(memory_space=pltpu.VMEM if name in IN_VMEM else pl.ANY) for name in INPUTS
        ],
        out_specs=[pl.BlockSpec(memory_space=pl.ANY)] * len(OUTPUTS),
        scratch_shapes=[pltpu.VMEM(dims, dtype) for _, dims, dtype in SCRATCH]
        + [
            pltpu.SemaphoreType.DMA((SENDS,)),
            pltpu.SemaphoreType.DMA((SENDS,)),
            pltpu.SemaphoreType.DMA((KEEPS,)),
        ],
        compiler_params=pltpu.CompilerParams(
            collective_id=0, has_side_effects=True, vmem_limit_bytes=VMEM_LIMIT
        ),
        name="layer",
    )(*arrays)


VMEM_LIMIT = 63 * 2**20


def per_device(
    hidden_in,
    query_weight,
    key_weight,
    value_weight,
    output_weight,
    gate_weight,
    up_weight,
    down_weight,
    query_gain,
    key_gain,
    attention_gain,
    feedforward_gain,
    document_ids,
    cotangent,
):
    documents = document_ids.astype(F32)
    documents = jnp.concatenate([documents, documents], axis=1)
    documents = jnp.broadcast_to(documents[:, None, :], (2, 8, 128))
    out, grad, wide, narrow, gate_up_grad, down_grad, gains = layer(
        hidden_in, cotangent, documents,
        query_weight, key_weight, value_weight, output_weight, gate_weight, up_weight, down_weight,
        *rope_tables(),
        query_gain[None, :], key_gain[None, :], attention_gain[None, :], feedforward_gain[None, :],
    )[:7]
    return (
        out,
        grad,
        wide[0].astype(F32),
        narrow[0].astype(F32),
        narrow[1].astype(F32),
        wide[1].astype(F32),
        gate_up_grad[0].astype(F32),
        gate_up_grad[1].astype(F32),
        down_grad.astype(F32),
        gains[16],
        gains[17],
        gains[:8].reshape(1024),
        gains[8:16].reshape(1024),
    )


def solution(mesh):
    tokens = P("rows", "seq", None)
    split = P("seq", None)
    return jax.shard_map(
        per_device,
        mesh=mesh,
        in_specs=(tokens,) + (P(),) * 11 + (P("rows", "seq"), tokens),
        out_specs=(tokens, tokens) + (split,) * 7 + (P(),) * 4,
        check_vma=False,
    )
```

```python
import functools

import jax
import jax.numpy as jnp
import numpy as np
from jax import lax
from jax.experimental import pallas as pl
from jax.experimental.pallas import tpu as pltpu
from jax.sharding import PartitionSpec as P

HD = 128
EPSILON = 1e-06
ROPE_BASE = 1000000.0
MASKED = -1e30
LOG2E = 1.4426950408889634
SCALE = HD ** (-0.5)
MESH = pl.DeviceIdType.MESH
F32 = jnp.float32
BF16 = jnp.bfloat16

YS = 4
ZS = 4
XS = 4


def place():
    rows, seq = lax.axis_index("rows"), lax.axis_index("seq")
    return (rows // YS, rows % YS, seq // 4, (seq // 2) % 2, seq % 2)


def device(xh, y, z, xl, c):
    return (xh * YS + y, z * 4 + xl * 2 + c)


def shifted(at, dx=0, dy=0, dz=0, dc=0, flip_xl=0, flip_xh=0):
    xh, y, z, xl, c = at
    if dx:
        x = (xh * 2 + xl + dx) % XS
        xh, xl = x // 2, x % 2
    if flip_xl:
        xl = 1 - xl
    if flip_xh:
        xh = 1 - xh
    if dc:
        c = 1 - c
    return (xh, (y + dy) % YS, (z + dz) % ZS, xl, c)


class Group:
    def __init__(self, net, index):
        self.net, self.index = net, index
        self.units, self.here = 0, False

    def add(self, src, dst, target, start=True):
        copy = self.net.remote(src, dst, target, self.index)
        if start:
            copy.start()
        self.units += units_of(dst)
        return self

    def wait(self):
        if not self.here:
            self.net.sized(self.units, self.net.recv_sems.at[self.index]).wait()
            self.here = True

    def drain(self):
        self.wait()
        self.net.sized(self.units, self.net.send_sems.at[self.index]).wait()


class LocalGroup:
    def __init__(self, net, index):
        self.net, self.index = net, index
        self.units, self.here, self.only = 0, False, None

    def add(self, src, dst):
        copy = pltpu.make_async_copy(src, dst, self.net.local_sems.at[self.index])
        copy.start()
        self.only = None if self.units else copy
        self.units += units_of(dst)
        return self

    def wait(self):
        if not self.here:
            if self.only is None:
                self.net.sized(self.units, self.net.local_sems.at[self.index]).wait()
            else:
                self.only.wait()
            self.here = True


def units_of(ref):
    return int(np.prod(ref.shape)) * (1 if ref.dtype == BF16 else 2)


class Net:
    def __init__(self, send_sems, recv_sems, local_sems, measures):
        self.send_sems, self.recv_sems, self.local_sems = send_sems, recv_sems, local_sems
        self.measures = measures
        self.groups, self.locals, self.next_send, self.next_keep = [], [], 0, 0

    def sized(self, units, sem):
        for ref in self.measures:
            columns = ref.shape[-1]
            while columns >= 128:
                rows = units // columns
                if rows * columns == units and rows % 16 == 0 and rows <= ref.shape[0] and columns % 128 == 0:
                    view = ref.at[pl.ds(0, rows), pl.ds(0, columns)]
                    return pltpu.make_async_copy(view, view, sem)
                columns -= 128
        raise ValueError(units)

    def barrier(self, targets):
        barrier = pltpu.get_barrier_semaphore()
        for target in targets:
            pl.semaphore_signal(barrier, inc=1, device_id=device(*target), device_id_type=MESH)
        pl.semaphore_wait(barrier, len(targets))

    def remote(self, src, dst, target, i):
        return pltpu.make_async_remote_copy(
            src_ref=src,
            dst_ref=dst,
            send_sem=self.send_sems.at[i],
            recv_sem=self.recv_sems.at[i],
            device_id=device(*target),
            device_id_type=MESH,
        )

    def group(self):
        self.groups.append(Group(self, self.next_send))
        self.next_send += 1
        return self.groups[-1]

    def local_group(self):
        self.locals.append(LocalGroup(self, self.next_keep))
        self.next_keep += 1
        return self.locals[-1]

    def send(self, src, dst, target):
        return self.group().add(src, dst, target)

    def together(self, items):
        result = self.group()
        for src, dst, target in items:
            result.add(src, dst, target)
        return result

    def keep(self, src, dst):
        return self.local_group().add(src, dst)

    def drain(self):
        for group in self.locals:
            group.wait()
        for group in self.groups:
            group.drain()


def shape(dims, dtype=BF16):
    return jax.ShapeDtypeStruct(dims, dtype)


ZC = [(dz, dc) for dz in range(ZS) for dc in range(2) if (dz, dc) != (0, 0)]
ORDER = (0, 1, 3, 2)
BLOCK = 256
SENDS = 87
KEEPS = 39


def rope_tables():
    half = HD // 2
    frequency = ROPE_BASE ** (-(np.arange(half, dtype=np.float64) * 2.0 / HD))
    angles = np.arange(1024, dtype=np.float64)[:, None] * frequency[None, :]
    cosines = np.concatenate([np.cos(angles)] * 2, axis=1)
    sines = np.concatenate([-np.sin(angles), np.sin(angles)], axis=1)
    return (cosines.astype(np.float32), sines.astype(np.float32))


def dot_nn(left, right):
    return jnp.dot(left, right, preferred_element_type=F32)


def dot_nt(left, right):
    return lax.dot_general(left, right, (((1,), (1,)), ((), ())), preferred_element_type=F32)


def dot_tn(left, right):
    return lax.dot_general(left, right, (((0,), (0,)), ((), ())), preferred_element_type=F32)


def normalize(vector, scales):
    inverse = lax.rsqrt(jnp.mean(vector * vector, axis=-1, keepdims=True) + EPSILON)
    return (vector * inverse * scales, inverse)


def norm_back(gradient, vector, inverse, scales):
    normed = vector * inverse
    scales_grad = jnp.sum(gradient * normed, axis=0, keepdims=True)
    scaled = gradient * scales
    vector_grad = inverse * (scaled - normed * jnp.mean(scaled * normed, axis=-1, keepdims=True))
    return (vector_grad, scales_grad)


def aligned(index, width):
    return pl.ds(pl.multiple_of(index * width, width), width)


class Refs:
    pass


INPUTS = dict(
    hidden=0,
    cotangent=0,
    query_weight=0,
    key_weight=0,
    value_weight=0,
    output_weight=0,
    gate_weight=0,
    up_weight=0,
    down_weight=0,
    document_ids_in=((2, 64), jnp.int32),
    cosines_in=((1024, 128), F32),
    sines_in=((1024, 128), F32),
    query_gain_in=((1, 128), F32),
    key_gain_in=((1, 128), F32),
    attention_gain_in=((1, 1024), F32),
    feedforward_gain_in=((1, 1024), F32),
)
SMALL = {name[:-3]: item for name, item in INPUTS.items() if item}
OUTPUTS = dict(
    out_own=((64, 1024), F32),
    grad_own=((64, 1024), F32),
    out_got=((64, 1024), BF16),
    grad_got=((64, 1024), BF16),
    query_weight_grad=((64, 2048), BF16),
    key_value_grad=((2, 64, 1024), BF16),
    output_weight_grad=((64, 2048), BF16),
    gate_grad=((64, 3072), BF16),
    up_grad=((64, 3072), BF16),
    down_grad=((64, 3072), BF16),
    gains=((24, 128), F32),
    residual_y=((1024, 1024), BF16),
    gate_all=((1024, 384), BF16),
    up_all=((1024, 384), BF16),
    down_all=((1024, 1024), BF16),
    activated_all=((1024, 384), BF16),
)
SCRATCH = dict(
    head_weights=((1024, 512), BF16),
    wo=((1024, 2048), BF16),
    wgu=((1024, 6144), BF16),
    wd=((1024, 3072), BF16),
    row=((4, 2, 2, 64, 1024), BF16),
    upstream=((2, 64, 1024), BF16),
    documents=((2, 16, 128), F32),
    row_documents=((16, 16, 128), F32),
    document_column=((1024, 128), F32),
    raw=((1024, 384), F32),
    inverses=((1024, 3), F32),
    queries=((1024, 256), BF16),
    keys=((1024, 128), BF16),
    values=((1024, 128), BF16),
    attended=((1024, 256), F32),
    attn_heads=((4, 2, 2, 64, 256), BF16),
    log_total=((2, 1024, 1), F32),
    attn_tokens=((2, 64, 2048), BF16),
    branch=((128, 1024), F32),
    down=((128, 1024), F32),
    residual=((128, 1024), F32),
    residual_low=((128, 1024), BF16),
    gate_factor=((128, 3072), F32),
    up_factor=((128, 3072), F32),
    activated=((128, 3072), BF16),
    layer_output=((2, 64, 1024), F32),
    down_low=((128, 1024), BF16),
    gate_up_low=((128, 6144), BF16),
    residual_grad=((128, 1024), F32),
    branch_low=((2, 64, 1024), BF16),
    attn_grad=((2, 64, 2048), BF16),
    attn_grad_row=((4, 2, 2, 64, 256), BF16),
    branch_row=((4, 2, 2, 64, 1024), BF16),
    lows=((4, 2, 2, 64, 512), BF16),
    key_sum=((1024, 128), F32),
    value_sum=((1024, 128), F32),
    low_tokens=((2, 64, 4096), BF16),
    input_grad=((2, 64, 1024), F32),
    out_low=((2, 64, 1024), BF16),
    grad_low=((2, 64, 1024), BF16),
    own_gate=((4, 2, 2, 2, 32, 384), BF16),
    all_gate=((3, 2, 2, 2, 32, 384), BF16),
    next_gate=((2, 2, 2, 32, 384), BF16),
    then_gate=((3, 2, 32, 384), BF16),
    done_gate=((2, 32, 384), BF16),
    got_gate=((32, 768), BF16),
    own_query=((4, 2, 2, 4, 16, 256), BF16),
    all_query=((3, 4, 2, 2, 16, 256), BF16),
    next_query=((4, 2, 2, 16, 256), BF16),
    then_query=((3, 4, 2, 16, 256), BF16),
    done_query=((4, 2, 16, 256), BF16),
    got_query=((16, 2048), BF16),
    own_kv=((4, 2, 2, 4, 16, 256), BF16),
    all_kv=((3, 4, 2, 4, 16, 128), BF16),
    next_kv=((4, 2, 4, 16, 128), BF16),
    then_kv=((3, 4, 2, 16, 128), BF16),
    done_kv=((4, 2, 16, 128), BF16),
    got_kv=((16, 1024), BF16),
    own_output=((4, 2, 2, 4, 16, 256), BF16),
    all_output=((3, 4, 2, 2, 16, 256), BF16),
    next_output=((4, 2, 2, 16, 256), BF16),
    then_output=((3, 4, 2, 16, 256), BF16),
    done_output=((4, 2, 16, 256), BF16),
    got_output=((16, 2048), BF16),
    own_up=((4, 2, 2, 2, 32, 384), BF16),
    all_up=((3, 4, 2, 32, 384), BF16),
    next_up=((4, 2, 32, 384), BF16),
    then_up=((3, 2, 32, 384), BF16),
    done_up=((2, 32, 384), BF16),
    got_up=((32, 768), BF16),
    own_down=((4, 2, 2, 4, 16, 384), BF16),
    all_down=((3, 4, 2, 2, 16, 384), BF16),
    next_down=((4, 2, 2, 16, 384), BF16),
    then_down=((3, 2, 2, 16, 384), BF16),
    done_down=((2, 2, 16, 384), BF16),
    got_down=((16, 1536), BF16),
    gains_own=((24, 128), F32),
    gains_next=((24, 128), F32),
    gains_last=((24, 128), F32),
    gains_final=((24, 128), F32),
    gains_y=((3, 24, 128), F32),
    gains_x=((3, 24, 128), F32),
    gains_zc=((7, 24, 128), F32),
)


def layer_kernel(*refs):
    names = [*INPUTS, *OUTPUTS, *SCRATCH, *SMALL]
    r = Refs()
    for name, ref in zip(names, refs):
        setattr(r, name, ref)
    net = Net(*refs[len(names) :], (r.wd, r.wgu))
    at = place()
    xh, y, z, xl, c = at
    x = xh * 2 + xl
    head = z * 2 + c
    sibling = shifted(at, dc=1)
    partner = shifted(at, flip_xl=1)
    seq_others = [
        shifted(at, dz=dz, dc=dc, flip_xl=dx)
        for dz in range(ZS)
        for dx in range(2)
        for dc in range(2)
        if (dz, dx, dc) != (0, 0, 0)
    ]
    zc = [shifted(at, dz=dz, dc=dc) for dz, dc in ZC]
    yc = [shifted(at, dy=dy, dc=dc) for dy, dc in ZC]
    xc = [shifted(at, dx=dx, dc=dc) for dx, dc in ZC]
    ys = [shifted(at, dy=step) for step in range(1, 4)]
    xs = [shifted(at, dx=step) for step in range(1, 4)]
    zs = [shifted(at, dz=step) for step in range(1, 4)]
    replicas = [
        shifted(at, dy=dy, flip_xh=dx) for dy in range(YS) for dx in range(2) if (dy, dx) != (0, 0)
    ]

    barrier_targets = list(seq_others) + yc[1:] + xc[1:] + replicas
    documents_load = net.keep(r.document_ids_in, r.document_ids)
    net.barrier(barrier_targets)
    up_z, down_z = shifted(at, dz=1), shifted(at, dz=-1)
    arrived = {}
    arrived[0, 1] = net.send(r.hidden.at[1 - xl], r.row.at[z, xl, c], partner)
    for dz, target in ((1, up_z), (3, down_z)):
        arrived[dz, 0] = net.send(r.hidden.at[xl], r.row.at[z, xl, c], target)
    own_block = net.keep(r.hidden.at[xl], r.row.at[z, xl, c])
    documents_load.wait()
    own_documents = r.document_ids[...].astype(F32)
    own_documents = jnp.concatenate([own_documents, own_documents], axis=1)
    for i in range(2):
        r.documents[i] = jnp.broadcast_to(own_documents[i : i + 1, :], (16, 128))
    document_slot = r.row_documents.at[z * 4 + xl * 2 + c]
    document_landings = net.together([(r.documents.at[t[3]], document_slot, t) for t in seq_others])
    document_landings_own = net.keep(r.documents.at[xl], document_slot)
    upstream_landing = net.send(r.cotangent.at[1 - xl], r.upstream.at[xl], partner)
    upstream_own = net.keep(r.cotangent.at[xl], r.upstream.at[xl])

    forwarded = {}

    def block_of(dz, dx):
        return r.row.at[(z - dz) % ZS, (xl + dx) % 2, c]

    def to_sibling(dz, dx):
        forwarded[dz, dx] = net.send(block_of(dz, dx), block_of(dz, dx), sibling)

    def project(dz):
        source = (z - dz) % ZS
        for dx in range(2):
            forwarded[dz, dx].wait()
        rows = aligned(source, BLOCK)
        product = dot_nn(r.row[source].reshape(BLOCK, 1024), r.head_weights[...])
        r.raw[rows, :] = product[:, :384]
        r.values[rows, :] = product[:, 384:].astype(BF16)
        for part in range(3):
            gain = r.query_gain[...] if part < 2 else r.key_gain[...]
            normed, inverse = normalize(product[:, part * HD : (part + 1) * HD], gain)
            r.inverses[rows, part : part + 1] = inverse
            turned = normed * r.cosines[rows, :] + pltpu.roll(normed, 64, 1) * r.sines[rows, :]
            if part < 2:
                r.queries[rows, part * HD : (part + 1) * HD] = turned.astype(BF16)
            else:
                r.keys[rows, :] = turned.astype(BF16)

    loads = net.local_group()
    for ref, start, width in (
        (r.query_weight, 0, 256),
        (r.key_weight, 256, 128),
        (r.value_weight, 384, 128),
    ):
        loads.add(ref.at[:, aligned(head, width)], r.head_weights.at[:, pl.ds(start, width)])
    small_loads = net.local_group()
    small_loads.add(r.cosines_in, r.cosines).add(r.sines_in, r.sines)
    gain_loads = [
        net.keep(r.query_gain_in, r.query_gain),
        net.keep(r.key_gain_in, r.key_gain),
        net.keep(r.attention_gain_in, r.attention_gain),
        net.keep(r.feedforward_gain_in, r.feedforward_gain),
    ]
    load_wo = net.keep(r.output_weight, r.wo)
    load_wgu = net.keep(r.gate_weight, r.wgu.at[:, pl.ds(0, 3072)])
    load_wgu.add(r.up_weight, r.wgu.at[:, pl.ds(3072, 3072)])
    load_wd = net.keep(r.down_weight, r.wd)

    loads.wait()
    small_loads.wait()
    for load in gain_loads:
        load.wait()
    own_block.wait()
    to_sibling(0, 0)
    arrived[0, 1].wait()
    for dz, target in ((1, up_z), (3, down_z)):
        arrived[dz, 1] = net.send(block_of(0, 1), block_of(0, 1), target)
    to_sibling(0, 1)
    arrived[1, 0].wait()
    arrived[2, 0] = net.send(block_of(1, 0), block_of(1, 0), up_z)
    to_sibling(1, 0)
    arrived[3, 0].wait()
    to_sibling(3, 0)
    arrived[3, 1].wait()
    arrived[2, 1] = net.send(block_of(3, 1), block_of(3, 1), down_z)
    to_sibling(3, 1)
    arrived[1, 1].wait()
    to_sibling(1, 1)
    project(0)
    project(1)
    project(3)
    for dx in range(2):
        arrived[2, dx].wait()
        to_sibling(2, dx)
    document_landings.wait()
    document_landings_own.wait()
    lane = lax.broadcasted_iota(jnp.int32, (1, 128), 1)
    pieces = []
    for block in range(8):
        even = r.row_documents[2 * block, 0:1, :]
        odd = r.row_documents[2 * block + 1, 0:1, :]
        piece = jnp.where(lane < 64, even, odd)
        pieces.append(piece)
        r.document_column[block * 128 : (block + 1) * 128, :] = jnp.broadcast_to(piece, (128, 128)).T
    document_row = jnp.concatenate(pieces, axis=1)
    project(2)

    def visible_in(block):
        count = (block + 1) * BLOCK
        rows = slice(block * BLOCK, count)
        same = r.document_column[rows, 0:1] == document_row[:, :count]
        row_at = block * BLOCK + lax.broadcasted_iota(jnp.int32, (BLOCK, count), 0)
        column_at = lax.broadcasted_iota(jnp.int32, (BLOCK, count), 1)
        return same & (row_at >= column_at)

    attn_landings = {dz: [] for dz in ORDER}
    by_source = [[net.group() for _ in ORDER] for _ in range(2)]
    by_core = [net.local_group() for _ in range(2)]
    first_send, first_keep = by_source[0][0].index, by_core[0].index

    def head_copies(h):
        columns = aligned(h, HD)
        slot = r.attn_tokens.at[:, :, aligned(head * 2 + h, HD)]
        copies = [
            net.remote(r.attn_heads.at[t[2], :, t[4], :, columns], slot, t, first_send + h * 4 + dz)
            for (dz, _), t in zip(ZC, zc)
        ]
        own = pltpu.make_async_copy(
            r.attn_heads.at[z, :, c, :, columns], slot, net.local_sems.at[first_keep + h]
        )
        return copies + [own]

    @pl.loop(0, 2)
    def _(h):
        columns = aligned(h, HD)
        for block in range(4):
            rows = slice(block * BLOCK, (block + 1) * BLOCK)
            count = (block + 1) * BLOCK
            scores = dot_nt(r.queries[rows, columns], r.keys[:count, :])
            scores = jnp.where(visible_in(block), scores * (SCALE * LOG2E), MASKED)
            top = jnp.max(scores, axis=-1, keepdims=True)
            soft = jnp.exp2(scores - top)
            total = jnp.sum(soft, axis=-1, keepdims=True)
            mixed = dot_nn(soft.astype(BF16), r.values[:count, :]) / total
            r.attended[rows, columns] = mixed
            r.attn_heads[block, :, :, :, columns] = mixed.astype(BF16).reshape(2, 2, 64, HD)
            r.log_total[h, rows, :] = top + jnp.log2(total)
        for copy in head_copies(h):
            copy.start()

    for h in range(2):
        by_core[h].units = 2 * 64 * HD
        attn_landings[0].append(by_core[h])
        for dz in ORDER:
            by_source[h][dz].units = 2 * 64 * HD * (1 if dz == 0 else 2)
            attn_landings[dz].append(by_source[h][dz])

    def chain(shift, src, slot_of, half_of):
        ahead, behind = shift(1), shift(-1)
        state = Refs()
        state.slot_of, state.half_of, state.ahead, state.behind = slot_of, half_of, ahead, behind
        state.far = shift(2)
        state.from_behind = net.send(src, slot_of(at), ahead)
        state.from_ahead = net.send(src, slot_of(at), behind)
        state.near = [net.send(src, slot_of(at), sibling), net.keep(src, slot_of(at))]
        return state

    def chain_middle(state):
        half_of, behind, ahead = state.half_of, state.behind, state.ahead
        state.from_behind.wait()
        state.beyond = [net.send(half_of(behind, 0), half_of(behind, 0), ahead)]
        state.from_ahead.wait()
        state.beyond.append(net.send(half_of(ahead, 1), half_of(ahead, 1), behind))
        for source in (behind, ahead):
            state.near.append(net.send(state.slot_of(source), state.slot_of(source), sibling))

    def chain_forward(state):
        for landing in state.beyond:
            landing.wait()
        state.last = net.send(state.slot_of(state.far), state.slot_of(state.far), sibling)

    def chain_near(state):
        for item in state.near:
            item.wait()

    def chain_wait(state):
        chain_near(state)
        state.last.wait()

    load_wo.wait()
    turned = jnp.zeros((1024, 128), F32)
    for dz in ORDER:
        for landing in attn_landings[dz]:
            landing.wait()
        columns = aligned((z - dz) % ZS, 512)
        turned = turned + dot_nt(r.wo[:, columns], r.attn_tokens[:, :, columns].reshape(128, 512))
    branch = turned.T
    r.branch[...] = branch
    branch_normed, branch_inverse = normalize(branch, r.attention_gain[...])
    residual = r.row[z, :, c].reshape(128, 1024).astype(F32) + branch_normed
    r.residual[...] = residual
    r.residual_low[...] = residual.astype(BF16)
    def rows_of(group, index):
        def slot_of(who):
            return group.at[aligned(index(who) * 2 + who[4], 128), :]

        def half_of(who, half):
            return group.at[aligned((index(who) * 2 + who[4]) * 2 + half, 64), :]

        return (slot_of, half_of)

    def y_of(who):
        return who[1]

    def x_of(who):
        return who[0] * 2 + who[3]

    residual_chain = chain(lambda step: shifted(at, dy=step), r.residual_low, *rows_of(r.residual_y, y_of))
    load_wgu.wait()

    @pl.loop(0, 3)
    def _(tile):
        columns, up_columns = aligned(tile, 1024), aligned(tile + 3, 1024)
        gate = dot_nn(r.residual_low[...], r.wgu[:, columns])
        up = dot_nn(r.residual_low[...], r.wgu[:, up_columns])
        sigmoid_gate = lax.logistic(gate)
        silu = gate * sigmoid_gate
        r.activated[:, columns] = (silu * up).astype(BF16)
        r.up_factor[:, columns] = silu
        r.gate_factor[:, columns] = up * sigmoid_gate * (1.0 + gate * (1.0 - sigmoid_gate))

    def to_columns(src, first, group, index, targets):
        slot = group.at[aligned(index(at) * 2 + c, 128), :]
        items = net.together(
            [(src.at[:, aligned(first + index(t) * 2 + t[4], 384)], slot, t) for t in targets]
        )
        return [items, net.keep(src.at[:, aligned(first + index(at) * 2 + c, 384)], slot)]

    activated_landings = to_columns(r.activated, 0, r.activated_all, x_of, xc)
    load_wd.wait()

    @pl.loop(0, 2)
    def _(part):
        rows = aligned(part, 512)
        r.down[:, rows] = dot_nt(r.wd[rows, :], r.activated[...]).T

    down = r.down[...]
    upstream_landing.wait()
    upstream_own.wait()
    down_normed, down_inverse = normalize(down, r.feedforward_gain[...])
    layer_output = (r.residual[...] + down_normed).reshape(2, 64, 1024)
    r.layer_output[...] = layer_output
    r.out_low[...] = layer_output.astype(BF16)
    upstream = r.upstream[...].reshape(128, 1024).astype(F32)
    down_grad, feedforward_gain_grad = norm_back(upstream, down, down_inverse, r.feedforward_gain[...])
    r.down_low[...] = down_grad.astype(BF16)
    down_chain = chain(lambda step: shifted(at, dx=step), r.down_low, *rows_of(r.down_all, x_of))

    @pl.loop(0, 3)
    def _(tile):
        columns, up_columns = aligned(tile, 1024), aligned(tile + 3, 1024)
        act_grad = dot_nn(r.down_low[...], r.wd[:, columns])
        r.gate_up_low[:, columns] = (act_grad * r.gate_factor[:, columns]).astype(BF16)
        r.gate_up_low[:, up_columns] = (act_grad * r.up_factor[:, columns]).astype(BF16)

    up_landings = to_columns(r.gate_up_low, 8, r.up_all, y_of, yc)

    @pl.loop(0, 2)
    def _(part):
        rows = aligned(part, 512)
        r.residual_grad[:, rows] = dot_nt(r.wgu[rows, :], r.gate_up_low[...]).T

    chain_middle(residual_chain)
    residual_grad = r.upstream[...].reshape(128, 1024).astype(F32) + r.residual_grad[...]
    r.residual_grad[...] = residual_grad
    branch_grad, attention_gain_grad = norm_back(
        residual_grad, r.branch[...], branch_inverse, r.attention_gain[...]
    )
    for i in range(8):
        r.gains_own[i : i + 1, :] = attention_gain_grad[:, i * 128 : (i + 1) * 128]
        r.gains_own[8 + i : 9 + i, :] = feedforward_gain_grad[:, i * 128 : (i + 1) * 128]
    branch_low = branch_grad.astype(BF16)
    r.branch_low[...] = branch_low.reshape(2, 64, 1024)

    @pl.loop(0, 2)
    def _(tile):
        columns = aligned(tile, 1024)
        product = dot_nn(r.branch_low[...].reshape(128, 1024), r.wo[:, columns])
        r.attn_grad[:, :, columns] = product.astype(BF16).reshape(2, 64, 1024)

    attn_grad_landings = net.together(
        [(r.attn_grad.at[:, :, aligned(t[2] * 2 + t[4], 256)], r.attn_grad_row.at[z, :, c], t) for t in zc]
    )
    attn_grad_own = net.keep(r.attn_grad.at[:, :, aligned(head, 256)], r.attn_grad_row.at[z, :, c])
    branch_chain = chain(
        lambda step: shifted(at, dz=step),
        r.branch_low,
        lambda who: r.branch_row.at[who[2], :, who[4]],
        lambda who, half: r.branch_row.at[who[2], half, who[4]],
    )
    gate_landings = to_columns(r.gate_up_low, 0, r.gate_all, y_of, yc)
    head_loads = net.local_group()
    for i in range(8):
        for ref, start, width in (
            (r.query_weight, 0, 256),
            (r.key_weight, 256, 128),
            (r.value_weight, 384, 128),
        ):
            head_loads.add(ref.at[:, pl.ds(i * width, width)], r.wgu.at[:, pl.ds(i * 512 + start, width)])
    def total(own, others, landings):
        for landing in landings:
            landing.wait()
        result = own.astype(F32)
        for i in range(3):
            result = result + others[i].astype(F32)
        return result

    def wait_all(items):
        for item in items:
            item.wait()

    across = shifted(at, flip_xh=1)
    ending = net.group()
    ending_own = net.local_group()

    def replicate(src, slot_of, y_first):
        ending_own.add(src, slot_of(at))
        if y_first:
            along = [net.send(src, slot_of(at), t) for t in ys]
            ending.add(src, slot_of(at), across)
        else:
            over = net.send(src, slot_of(at), across)
            for t in ys:
                ending.add(src, slot_of(at), t)

        def second():
            if y_first:
                for step, landing in enumerate(along):
                    landing.wait()
                    source = shifted(at, dy=-(step + 1))
                    ending.add(slot_of(source), slot_of(source), across)
            else:
                over.wait()
                for t in ys:
                    ending.add(slot_of(across), slot_of(across), t)

        return second

    def along_y(src, slot):
        ending_own.add(src, slot)
        for t in ys:
            ending.add(src, slot, t)

    def swap(own, low, own_to, got_to):
        ending.add(low.at[1 - xl], got_to, partner)
        ending_own.add(own.at[xl], own_to)

    r.key_sum[...] = jnp.zeros_like(r.key_sum)
    r.value_sum[...] = jnp.zeros_like(r.value_sum)
    attn_grad_landings.wait()
    attn_grad_own.wait()

    def rope_norm_back(grad, part, rows, gain):
        turned = grad * r.cosines[rows, :] - pltpu.roll(grad, 64, 1) * r.sines[rows, :]
        vector = r.raw[rows, part * HD : (part + 1) * HD]
        result, gain_part = norm_back(turned, vector, r.inverses[rows, part : part + 1], gain)
        return (result.astype(BF16).reshape(2, 2, 64, HD), gain_part)

    def backward_block(block):
        rows = slice(block * BLOCK, (block + 1) * BLOCK)
        count = (block + 1) * BLOCK
        visible = visible_in(block)
        for h in range(2):
            columns = slice(h * HD, (h + 1) * HD)
            query = r.queries[rows, columns]
            grad = r.attn_grad_row[block, :, :, :, columns].reshape(BLOCK, HD)
            delta = jnp.sum(grad.astype(F32) * r.attended[rows, columns], axis=-1, keepdims=True)
            scores = dot_nt(query, r.keys[:count, :]) * (SCALE * LOG2E)
            soft = jnp.exp2(jnp.where(visible, scores - r.log_total[h, rows, :], MASKED))
            r.value_sum[:count, :] += dot_tn(soft.astype(BF16), grad)
            soft_grad = dot_nt(grad, r.values[:count, :])
            score_low = (soft * (soft_grad - delta)).astype(BF16)
            query_grad = dot_nn(score_low, r.keys[:count, :]) * SCALE
            r.key_sum[:count, :] += dot_tn(score_low, query)
            low, gain_part = rope_norm_back(query_grad, h, rows, r.query_gain[...])
            r.lows[block, :, :, :, columns] = low
            r.gains_own[16:17, :] += gain_part

    def by_rows(product):
        return product.astype(BF16).reshape(4, 2, 2, 2, 32, 384)

    def to_heads(done, got, width):
        items = [net.together([(done.at[t[2], t[4]], got.at[:, aligned(head, width)], t) for t in zc])]
        return items + [net.keep(done.at[z, c], got.at[:, aligned(head, width)])]

    r.gains_own[16:24, :] = jnp.zeros((8, 128), F32)
    wait_all(activated_landings)
    load_activated = net.keep(r.activated_all, r.wd.at[:, pl.ds(768, 384)])
    backward_block(0)
    chain_near(residual_chain)
    near_up = net.local_group()
    for who in (at, residual_chain.behind, residual_chain.ahead):
        rows = aligned(y_of(who), 256)
        near_up.add(r.residual_y.at[rows, :], r.wo.at[rows, pl.ds(0, 1024)])
    chain_forward(residual_chain)
    backward_block(1)
    chain_wait(residual_chain)
    rows = aligned(y_of(residual_chain.far), 256)
    far_up = net.keep(r.residual_y.at[rows, :], r.wo.at[rows, pl.ds(0, 1024)])
    backward_block(2)
    chain_middle(down_chain)
    wait_all(up_landings)
    load_up = net.keep(r.up_all, r.wd.at[:, pl.ds(0, 384)])
    backward_block(3)
    chain_middle(branch_chain)
    wait_all([near_up, far_up, load_up])
    r.own_up[...] = by_rows(dot_tn(r.wo[:, :1024], r.wd[:, :384]))
    first_up = [net.together([(r.own_up.at[:, t[3], :, t[0]], r.all_up.at[i], t) for i, t in enumerate(xs)])]
    key_total = jnp.zeros((1, HD), F32)
    for block in range(4):
        rows = slice(block * BLOCK, (block + 1) * BLOCK)
        low, gain_part = rope_norm_back(r.key_sum[rows, :] * SCALE, 2, rows, r.key_gain[...])
        r.lows[block, :, :, :, 256:384] = low
        r.lows[block, :, :, :, 384:] = r.value_sum[rows, :].astype(BF16).reshape(2, 2, 64, HD)
        key_total = key_total + gain_part
    r.gains_own[17:18, :] = key_total
    low_landings = {dz: net.group() for dz in ORDER}

    def send_lows(dz_here):
        for (dz, dc), t in zip(ZC, zc):
            if dz == dz_here:
                low_landings[dz].add(r.lows.at[t[2], :, t[4]], r.low_tokens.at[:, :, aligned(head, 512)], t)

    low_own = net.keep(r.lows.at[z, :, c], r.low_tokens.at[:, :, aligned(head, 512)])
    send_lows(0)
    gains_y = [net.together([(r.gains_own, r.gains_y.at[i], ys[i]) for i in range(3)])]
    send_lows(1)
    row = r.row[...].reshape(1024, 1024)
    low_columns = dot_tn(row, r.lows[...].reshape(1024, 512)).astype(BF16)
    r.own_query[...] = low_columns[:, :256].reshape(4, 2, 2, 4, 16, 256)
    first_query = [net.together([(r.own_query.at[:, :, :, t[1]], r.all_query.at[i], t) for i, t in enumerate(ys)])]
    r.own_kv[...] = low_columns[:, 256:].reshape(4, 2, 2, 4, 16, 256)
    first_kv = [net.together([(r.own_kv.at[:, t[3], :, :, :, aligned(t[0], 128)], r.all_kv.at[i], t) for i, t in enumerate(xs)])]
    wait_all(gate_landings)
    load_gate = net.keep(r.gate_all, r.wd.at[:, pl.ds(384, 384)])
    chain_near(down_chain)
    near_down = net.local_group()
    for who in (at, down_chain.behind, down_chain.ahead):
        rows = aligned(x_of(who), 256)
        near_down.add(r.down_all.at[rows, :], r.wgu.at[rows, pl.ds(4096, 1024)])
    chain_forward(down_chain)
    load_gate.wait()
    r.own_gate[...] = by_rows(dot_tn(r.wo[:, :1024], r.wd[:, 384:768]))
    first_gate = [net.together([(r.own_gate.at[t[2]], r.all_gate.at[i], t) for i, t in enumerate(zs)])]
    chain_wait(down_chain)
    rows = aligned(x_of(down_chain.far), 256)
    load_down = net.keep(r.down_all.at[rows, :], r.wgu.at[rows, pl.ds(4096, 1024)])
    wait_all([near_down, load_down, load_activated])
    product = dot_tn(r.wgu[:, 4096:5120], r.wd[:, 768:1152])
    r.own_down[...] = product.astype(BF16).reshape(4, 2, 2, 4, 16, 384)
    first_down = [net.together([(r.own_down.at[:, :, :, t[1]], r.all_down.at[i], t) for i, t in enumerate(ys)])]
    chain_forward(branch_chain)
    r.next_up[...] = total(r.own_up[:, at[3], :, at[0]], r.all_up, first_up).astype(BF16)
    then_up = [net.together([(r.next_up.at[t[2]], r.then_up.at[i], t) for i, t in enumerate(zs)])]
    r.gains_next[...] = total(r.gains_own[...], r.gains_y, gains_y)
    gains_x = [net.together([(r.gains_next, r.gains_x.at[i], xs[i]) for i in range(3)])]
    r.next_query[...] = total(r.own_query[:, :, :, at[1]], r.all_query, first_query).astype(BF16)
    then_query = [net.together([(r.next_query.at[:, t[3]], r.then_query.at[i], t) for i, t in enumerate(xs)])]
    chain_wait(branch_chain)
    output_columns = dot_tn(r.branch_row[...].reshape(1024, 1024), r.attn_heads[...].reshape(1024, 256))
    r.own_output[...] = output_columns.astype(BF16).reshape(4, 2, 2, 4, 16, 256)
    first_output = [net.together([(r.own_output.at[:, :, :, t[1]], r.all_output.at[i], t) for i, t in enumerate(ys)])]
    send_lows(3)
    r.next_kv[...] = total(r.own_kv[:, at[3], :, :, :, aligned(at[0], 128)], r.all_kv, first_kv).astype(BF16)
    then_kv = [net.together([(r.next_kv.at[:, :, t[1]], r.then_kv.at[i], t) for i, t in enumerate(ys)])]
    r.next_gate[...] = total(r.own_gate[at[2]], r.all_gate, first_gate).astype(BF16)
    then_gate = [net.together([(r.next_gate.at[t[3], :, t[0]], r.then_gate.at[i], t) for i, t in enumerate(xs)])]
    swap(r.layer_output, r.out_low, r.out_own, r.out_got)
    r.done_up[...] = total(r.next_up[z], r.then_up, then_up).astype(BF16)
    got_up = [
        net.send(r.done_up.at[1 - c], r.got_up.at[:, aligned(c, 384)], sibling),
        net.keep(r.done_up.at[c], r.got_up.at[:, aligned(c, 384)]),
    ]
    r.next_down[...] = total(r.own_down[:, :, :, at[1]], r.all_down, first_down).astype(BF16)
    then_down = [net.together([(r.next_down.at[t[2]], r.then_down.at[i], t) for i, t in enumerate(zs)])]
    r.gains_last[...] = total(r.gains_next[...], r.gains_x, gains_x)
    gains_zc = [net.together([(r.gains_last, r.gains_zc.at[i], t) for i, t in enumerate(zc)])]
    wait_all(got_up)
    second_up = replicate(r.got_up, lambda who: r.up_grad.at[aligned(who[0], 32), aligned(who[1], 768)], True)
    r.done_query[...] = total(r.next_query[:, xl], r.then_query, then_query).astype(BF16)
    got_query = to_heads(r.done_query, r.got_query, 256)
    send_lows(2)
    r.done_gate[...] = total(r.next_gate[xl, :, xh], r.then_gate, then_gate).astype(BF16)
    got_gate = [
        net.send(r.done_gate.at[1 - c], r.got_gate.at[:, aligned(c, 384)], sibling),
        net.keep(r.done_gate.at[c], r.got_gate.at[:, aligned(c, 384)]),
    ]
    r.done_down[...] = total(r.next_down[z], r.then_down, then_down).astype(BF16)
    quarter = aligned(xl * 2 + c, 384)
    pairs = [partner, shifted(at, flip_xl=1, dc=1), sibling]
    got_down = [net.together([(r.done_down.at[t[3], t[4]], r.got_down.at[:, quarter], t) for t in pairs])]
    got_down.append(net.keep(r.done_down.at[xl, c], r.got_down.at[:, quarter]))
    wait_all(got_gate)
    second_gate = replicate(r.got_gate, lambda who: r.gate_grad.at[aligned(who[0], 32), aligned(who[1], 768)], False)
    r.next_output[...] = total(r.own_output[:, :, :, at[1]], r.all_output, first_output).astype(BF16)
    then_output = [net.together([(r.next_output.at[:, t[3]], r.then_output.at[i], t) for i, t in enumerate(xs)])]
    r.done_kv[...] = total(r.next_kv[:, :, y], r.then_kv, then_kv).astype(BF16)
    got_kv = to_heads(r.done_kv, r.got_kv, 128)
    wait_all(got_query)
    along_y(r.got_query, r.query_weight_grad.at[aligned(y, 16), :])
    wait_all(got_down)
    second_down = replicate(r.got_down, lambda who: r.down_grad.at[aligned(who[1], 16), aligned(who[0], 1536)], True)
    second_gate()
    wait_all(got_kv)
    second_kv = replicate(r.got_kv, lambda who: r.key_value_grad.at[who[0], aligned(who[1], 16), :], False)
    second_up()
    head_loads.wait()
    low_own.wait()
    for dz in ORDER:
        low_landings[dz].wait()

    @pl.loop(0, 2)
    def _(part):
        rows = aligned(part, 512)
        r.down[:, rows] = dot_nt(r.wgu[rows, pl.ds(0, 4096)], r.low_tokens[...].reshape(128, 4096)).T

    input_grad = (r.residual_grad[...] + r.down[...]).reshape(2, 64, 1024)
    r.input_grad[...] = input_grad
    r.grad_low[...] = input_grad.astype(BF16)
    swap(r.input_grad, r.grad_low, r.grad_own, r.grad_got)
    r.done_output[...] = total(r.next_output[:, xl], r.then_output, then_output).astype(BF16)
    got_output = to_heads(r.done_output, r.got_output, 256)
    second_kv()
    second_down()
    wait_all(got_output)
    along_y(r.got_output, r.output_weight_grad.at[aligned(y, 16), :])
    wait_all(gains_zc)
    gains = r.gains_last[...]
    for i in range(7):
        gains = gains + r.gains_zc[i]
    r.gains_final[...] = gains
    net.keep(r.gains_final, r.gains)
    assert (net.next_send, net.next_keep) == (SENDS, KEEPS), (net.next_send, net.next_keep)
    net.drain()


def layer(*arrays):
    return pl.pallas_call(
        layer_kernel,
        out_shape=[shape(*item) for item in OUTPUTS.values()],
        in_specs=[pl.BlockSpec(memory_space=pl.ANY)] * len(INPUTS),
        out_specs=[pl.BlockSpec(memory_space=pl.ANY)] * len(OUTPUTS),
        scratch_shapes=[pltpu.VMEM(*item) for item in [*SCRATCH.values(), *SMALL.values()]]
        + [
            pltpu.SemaphoreType.DMA((SENDS,)),
            pltpu.SemaphoreType.DMA((SENDS,)),
            pltpu.SemaphoreType.DMA((KEEPS,)),
        ],
        compiler_params=pltpu.CompilerParams(
            collective_id=0, has_side_effects=True, vmem_limit_bytes=VMEM_LIMIT
        ),
        name="layer",
    )(*arrays)


def widen_kernel(
    out_own, grad_own, out_got, grad_got, query, key_value, output, gate, up, down, gains,
    out_to, grad_to, query_to, key_to, value_to, output_to, gate_to, up_to, down_to,
    query_gain, key_gain, attention_gain, feedforward_gain,
):
    lower = (lax.axis_index("seq") // 2) % 2 == 0
    for own, got, to in ((out_own, out_got, out_to), (grad_own, grad_got, grad_to)):
        mine, other = own[...], got[...].astype(F32)
        to[0] = jnp.where(lower, mine, other)
        to[1] = jnp.where(lower, other, mine)
    query_to[...] = query[...].astype(F32)
    key_to[...] = key_value[0].astype(F32)
    value_to[...] = key_value[1].astype(F32)
    output_to[...] = output[...].astype(F32)
    gate_to[...] = gate[...].astype(F32)
    up_to[...] = up[...].astype(F32)
    down_to[...] = down[...].astype(F32)
    attention_gain[...] = gains[0:8, :]
    feedforward_gain[...] = gains[8:16, :]
    query_gain[...] = gains[16:17, :]
    key_gain[...] = gains[17:18, :]


def widen(*arrays):
    steps = 2
    rows = 64 // steps

    def flat(columns):
        return pl.BlockSpec((rows, columns), lambda i: (i, 0))

    def paired(columns):
        return pl.BlockSpec((2, rows, columns), lambda i: (0, i, 0))

    def whole(count):
        return pl.BlockSpec((count, 128), lambda i: (0, 0))

    return pl.pallas_call(
        widen_kernel,
        grid=(steps,),
        out_shape=[shape((2, 64, 1024), F32)] * 2
        + [shape((64, n), F32) for n in (2048, 1024, 1024, 2048, 3072, 3072, 3072)]
        + [shape((n, 128), F32) for n in (1, 1, 8, 8)],
        in_specs=[flat(1024)] * 4
        + [flat(2048), paired(1024), flat(2048)]
        + [flat(3072)] * 3
        + [whole(24)],
        out_specs=[paired(1024)] * 2
        + [flat(n) for n in (2048, 1024, 1024, 2048, 3072, 3072, 3072)]
        + [whole(n) for n in (1, 1, 8, 8)],
        name="widen",
    )(*arrays)


VMEM_LIMIT = 63 * 2**20


def per_device(
    hidden_in,
    query_weight,
    key_weight,
    value_weight,
    output_weight,
    gate_weight,
    up_weight,
    down_weight,
    query_gain,
    key_gain,
    attention_gain,
    feedforward_gain,
    document_ids,
    cotangent,
):
    results = layer(
        hidden_in, cotangent,
        query_weight, key_weight, value_weight, output_weight, gate_weight, up_weight, down_weight,
        document_ids, *rope_tables(),
        query_gain[None, :], key_gain[None, :], attention_gain[None, :], feedforward_gain[None, :],
    )[:11]
    results = widen(*results)
    return tuple(results[:9]) + (results[9][0], results[10][0], results[11].reshape(1024), results[12].reshape(1024))


def solution(mesh):
    tokens = P("rows", "seq", None)
    split = P("seq", None)
    return jax.shard_map(
        per_device,
        mesh=mesh,
        in_specs=(tokens,) + (P(),) * 11 + (P("rows", "seq"), tokens),
        out_specs=(tokens, tokens) + (split,) * 7 + (P(),) * 4,
        check_vma=False,
    )
```

```python
import functools

import jax
import jax.numpy as jnp
import numpy as np
from jax import lax
from jax.experimental import pallas as pl
from jax.experimental.pallas import tpu as pltpu
from jax.sharding import PartitionSpec as P

HD = 128
EPSILON = 1e-06
ROPE_BASE = 1000000.0
MASKED = -1e30
LOG2E = 1.4426950408889634
SCALE = HD ** (-0.5)
MESH = pl.DeviceIdType.MESH
F32 = jnp.float32
BF16 = jnp.bfloat16

YS = 4
ZS = 4
XS = 4


def place():
    rows, seq = lax.axis_index("rows"), lax.axis_index("seq")
    return (rows // YS, rows % YS, seq // 4, (seq // 2) % 2, seq % 2)


def device(xh, y, z, xl, c):
    return (xh * YS + y, z * 4 + xl * 2 + c)


def shifted(at, dx=0, dy=0, dz=0, dc=0, flip_xl=0, flip_xh=0):
    xh, y, z, xl, c = at
    if dx:
        x = (xh * 2 + xl + dx) % XS
        xh, xl = x // 2, x % 2
    if flip_xl:
        xl = 1 - xl
    if flip_xh:
        xh = 1 - xh
    if dc:
        c = 1 - c
    return (xh, (y + dy) % YS, (z + dz) % ZS, xl, c)


class Group:
    def __init__(self, net, index):
        self.net, self.index = net, index
        self.units, self.here = 0, False

    def add(self, src, dst, target, start=True):
        copy = self.net.remote(src, dst, target, self.index)
        if start:
            copy.start()
        self.units += units_of(dst)
        return self

    def wait(self):
        if not self.here:
            self.net.sized(self.units, self.net.recv_sems.at[self.index]).wait()
            self.here = True

    def drain(self):
        self.wait()
        self.net.sized(self.units, self.net.send_sems.at[self.index]).wait()


class LocalGroup:
    def __init__(self, net, index):
        self.net, self.index = net, index
        self.units, self.here, self.only = 0, False, None

    def add(self, src, dst):
        copy = pltpu.make_async_copy(src, dst, self.net.local_sems.at[self.index])
        copy.start()
        self.only = None if self.units else copy
        self.units += units_of(dst)
        return self

    def wait(self):
        if not self.here:
            if self.only is None:
                self.net.sized(self.units, self.net.local_sems.at[self.index]).wait()
            else:
                self.only.wait()
            self.here = True


def units_of(ref):
    return int(np.prod(ref.shape)) * (1 if ref.dtype == BF16 else 2)


class Net:
    def __init__(self, send_sems, recv_sems, local_sems, measures):
        self.send_sems, self.recv_sems, self.local_sems = send_sems, recv_sems, local_sems
        self.measures = measures
        self.groups, self.locals, self.next_send, self.next_keep = [], [], 0, 0

    def sized(self, units, sem):
        for ref in self.measures:
            columns = ref.shape[-1]
            while columns >= 128:
                rows = units // columns
                if rows * columns == units and rows % 16 == 0 and rows <= ref.shape[0] and columns % 128 == 0:
                    view = ref.at[pl.ds(0, rows), pl.ds(0, columns)]
                    return pltpu.make_async_copy(view, view, sem)
                columns -= 128
        raise ValueError(units)

    def barrier(self, targets):
        barrier = pltpu.get_barrier_semaphore()
        for target in targets:
            pl.semaphore_signal(barrier, inc=1, device_id=device(*target), device_id_type=MESH)
        pl.semaphore_wait(barrier, len(targets))

    def remote(self, src, dst, target, i):
        return pltpu.make_async_remote_copy(
            src_ref=src,
            dst_ref=dst,
            send_sem=self.send_sems.at[i],
            recv_sem=self.recv_sems.at[i],
            device_id=device(*target),
            device_id_type=MESH,
        )

    def group(self):
        self.groups.append(Group(self, self.next_send))
        self.next_send += 1
        return self.groups[-1]

    def local_group(self):
        self.locals.append(LocalGroup(self, self.next_keep))
        self.next_keep += 1
        return self.locals[-1]

    def send(self, src, dst, target):
        return self.group().add(src, dst, target)

    def together(self, items):
        result = self.group()
        for src, dst, target in items:
            result.add(src, dst, target)
        return result

    def keep(self, src, dst):
        return self.local_group().add(src, dst)

    def drain(self):
        for group in self.locals:
            group.wait()
        for group in self.groups:
            group.drain()


def shape(dims, dtype=BF16):
    return jax.ShapeDtypeStruct(dims, dtype)


ZC = [(dz, dc) for dz in range(ZS) for dc in range(2) if (dz, dc) != (0, 0)]
ORDER = (0, 1, 3, 2)
BLOCK = 256
SENDS = 91
KEEPS = 36


def rope_tables():
    half = HD // 2
    frequency = ROPE_BASE ** (-(np.arange(half, dtype=np.float64) * 2.0 / HD))
    angles = np.arange(1024, dtype=np.float64)[:, None] * frequency[None, :]
    cosines = np.concatenate([np.cos(angles)] * 2, axis=1)
    sines = np.concatenate([-np.sin(angles), np.sin(angles)], axis=1)
    return (cosines.astype(np.float32), sines.astype(np.float32))


def dot_nn(left, right):
    return jnp.dot(left, right, preferred_element_type=F32)


def dot_nt(left, right):
    return lax.dot_general(left, right, (((1,), (1,)), ((), ())), preferred_element_type=F32)


def dot_tn(left, right):
    return lax.dot_general(left, right, (((0,), (0,)), ((), ())), preferred_element_type=F32)


def normalize(vector, scales):
    inverse = lax.rsqrt(jnp.mean(vector * vector, axis=-1, keepdims=True) + EPSILON)
    return (vector * inverse * scales, inverse)


def norm_back(gradient, vector, inverse, scales):
    normed = vector * inverse
    scales_grad = jnp.sum(gradient * normed, axis=0, keepdims=True)
    scaled = gradient * scales
    vector_grad = inverse * (scaled - normed * jnp.mean(scaled * normed, axis=-1, keepdims=True))
    return (vector_grad, scales_grad)


def aligned(index, width):
    return pl.ds(pl.multiple_of(index * width, width), width)


class Refs:
    pass


INPUTS = dict(
    hidden=0,
    cotangent=0,
    query_weight=0,
    key_weight=0,
    value_weight=0,
    output_weight=0,
    gate_weight=0,
    up_weight=0,
    down_weight=0,
    document_ids_in=((2, 64), jnp.int32),
    cosines_in=((1024, 128), F32),
    sines_in=((1024, 128), F32),
    query_gain_in=((1, 128), F32),
    key_gain_in=((1, 128), F32),
    attention_gain_in=((1, 1024), F32),
    feedforward_gain_in=((1, 1024), F32),
)
SMALL = {name[:-3]: item for name, item in INPUTS.items() if item}
OUTPUTS = dict(
    out_own=((64, 1024), F32),
    grad_own=((64, 1024), F32),
    out_got=((64, 1024), BF16),
    grad_got=((64, 1024), BF16),
    query_weight_grad=((64, 2048), BF16),
    key_value_grad=((2, 64, 1024), BF16),
    output_weight_grad=((64, 2048), BF16),
    gate_grad=((64, 3072), BF16),
    up_grad=((64, 3072), BF16),
    down_grad=((64, 3072), BF16),
    gains=((24, 128), F32),
    residual_y=((1024, 1024), BF16),
    gate_all=((1024, 384), BF16),
    up_all=((1024, 384), BF16),
    down_all=((1024, 1024), BF16),
    activated_all=((1024, 384), BF16),
)
SCRATCH = dict(
    head_weights=((1024, 512), BF16),
    wo=((1024, 2048), BF16),
    wgu=((1024, 6144), BF16),
    wd=((1024, 3072), BF16),
    row=((4, 2, 2, 64, 1024), BF16),
    upstream=((2, 64, 1024), BF16),
    documents=((2, 16, 128), F32),
    row_documents=((16, 16, 128), F32),
    document_column=((1024, 128), F32),
    raw=((1024, 384), F32),
    inverses=((1024, 3), F32),
    queries=((1024, 256), BF16),
    keys=((1024, 128), BF16),
    values=((1024, 128), BF16),
    attended=((1024, 256), F32),
    attn_heads=((4, 2, 2, 64, 256), BF16),
    log_total=((2, 1024, 1), F32),
    attn_tokens=((2, 64, 2048), BF16),
    branch=((128, 1024), F32),
    down=((128, 1024), F32),
    residual=((128, 1024), F32),
    residual_low=((128, 1024), BF16),
    gate_factor=((128, 3072), F32),
    up_factor=((128, 3072), F32),
    activated=((128, 3072), BF16),
    layer_output=((2, 64, 1024), F32),
    down_low=((128, 1024), BF16),
    gate_up_low=((128, 6144), BF16),
    residual_grad=((128, 1024), F32),
    branch_low=((2, 64, 1024), BF16),
    attn_grad=((2, 64, 2048), BF16),
    attn_grad_row=((4, 2, 2, 64, 256), BF16),
    branch_row=((4, 2, 2, 64, 1024), BF16),
    lows=((4, 2, 2, 64, 512), BF16),
    key_sum=((1024, 128), F32),
    value_sum=((1024, 128), F32),
    low_tokens=((2, 64, 4096), BF16),
    input_grad=((2, 64, 1024), F32),
    out_low=((2, 64, 1024), BF16),
    grad_low=((2, 64, 1024), BF16),
    own_gate=((4, 2, 2, 2, 32, 384), BF16),
    all_gate=((3, 2, 2, 2, 32, 384), BF16),
    next_gate=((2, 2, 2, 32, 384), BF16),
    then_gate=((3, 2, 32, 384), BF16),
    done_gate=((2, 32, 384), BF16),
    own_query=((4, 2, 2, 4, 16, 256), BF16),
    all_query=((2, 4, 2, 2, 16, 256), BF16),
    far_query=((2, 2, 2, 2, 16, 256), BF16),
    mid_query=((2, 2, 2, 2, 16, 256), BF16),
    next_query=((4, 2, 2, 16, 256), BF16),
    then_query=((3, 4, 2, 16, 256), BF16),
    done_query=((4, 2, 16, 256), BF16),
    got_query=((16, 2048), BF16),
    own_kv=((4, 2, 2, 4, 16, 256), BF16),
    all_kv=((3, 4, 2, 4, 16, 128), BF16),
    next_kv=((4, 2, 4, 16, 128), BF16),
    then_kv=((3, 4, 2, 16, 128), BF16),
    done_kv=((4, 2, 16, 128), BF16),
    got_kv=((16, 1024), BF16),
    own_output=((4, 2, 2, 4, 16, 256), BF16),
    all_output=((2, 4, 2, 2, 16, 256), BF16),
    far_output=((2, 2, 2, 2, 16, 256), BF16),
    mid_output=((2, 2, 2, 2, 16, 256), BF16),
    next_output=((4, 2, 2, 16, 256), BF16),
    then_output=((3, 4, 2, 16, 256), BF16),
    done_output=((4, 2, 16, 256), BF16),
    got_output=((16, 2048), BF16),
    own_up=((4, 2, 2, 2, 32, 384), BF16),
    all_up=((3, 4, 2, 32, 384), BF16),
    next_up=((4, 2, 32, 384), BF16),
    then_up=((3, 2, 32, 384), BF16),
    done_up=((2, 32, 384), BF16),
    own_down=((4, 2, 2, 4, 16, 384), BF16),
    all_down=((2, 4, 2, 2, 16, 384), BF16),
    far_down=((2, 2, 2, 2, 16, 384), BF16),
    mid_down=((2, 2, 2, 2, 16, 384), BF16),
    next_down=((4, 2, 2, 16, 384), BF16),
    then_down=((3, 2, 2, 16, 384), BF16),
    done_down=((2, 2, 16, 384), BF16),
    gains_own=((24, 128), F32),
    gains_next=((24, 128), F32),
    gains_last=((24, 128), F32),
    gains_final=((24, 128), F32),
    gains_y=((3, 24, 128), F32),
    gains_x=((3, 24, 128), F32),
    gains_zc=((7, 24, 128), F32),
)


def layer_kernel(*refs):
    names = [*INPUTS, *OUTPUTS, *SCRATCH, *SMALL]
    r = Refs()
    for name, ref in zip(names, refs):
        setattr(r, name, ref)
    net = Net(*refs[len(names) :], (r.wd, r.wgu))
    at = place()
    xh, y, z, xl, c = at
    x = xh * 2 + xl
    head = z * 2 + c
    sibling = shifted(at, dc=1)
    partner = shifted(at, flip_xl=1)
    seq_others = [
        shifted(at, dz=dz, dc=dc, flip_xl=dx)
        for dz in range(ZS)
        for dx in range(2)
        for dc in range(2)
        if (dz, dx, dc) != (0, 0, 0)
    ]
    zc = [shifted(at, dz=dz, dc=dc) for dz, dc in ZC]
    yc = [shifted(at, dy=dy, dc=dc) for dy, dc in ZC]
    xc = [shifted(at, dx=dx, dc=dc) for dx, dc in ZC]
    ys = [shifted(at, dy=step) for step in range(1, 4)]
    xs = [shifted(at, dx=step) for step in range(1, 4)]
    zs = [shifted(at, dz=step) for step in range(1, 4)]
    replicas = [
        shifted(at, dy=dy, flip_xh=dx) for dy in range(YS) for dx in range(2) if (dy, dx) != (0, 0)
    ]

    crossed = [shifted(at, dy=dy, dc=dc, flip_xl=1) for dy in range(1, YS) for dc in range(2)]
    barrier_targets = list(seq_others) + yc[1:] + xc[1:] + replicas + crossed
    documents_load = net.keep(r.document_ids_in, r.document_ids)
    net.barrier(barrier_targets)
    up_z, down_z = shifted(at, dz=1), shifted(at, dz=-1)
    arrived = {}
    arrived[0, 1] = net.send(r.hidden.at[1 - xl], r.row.at[z, xl, c], partner)
    for dz, target in ((1, up_z), (3, down_z)):
        arrived[dz, 0] = net.send(r.hidden.at[xl], r.row.at[z, xl, c], target)
    own_block = net.keep(r.hidden.at[xl], r.row.at[z, xl, c])
    documents_load.wait()
    own_documents = r.document_ids[...].astype(F32)
    own_documents = jnp.concatenate([own_documents, own_documents], axis=1)
    for i in range(2):
        r.documents[i] = jnp.broadcast_to(own_documents[i : i + 1, :], (16, 128))
    document_slot = r.row_documents.at[z * 4 + xl * 2 + c]
    document_landings = net.together([(r.documents.at[t[3]], document_slot, t) for t in seq_others])
    document_landings_own = net.keep(r.documents.at[xl], document_slot)
    upstream_landing = net.send(r.cotangent.at[1 - xl], r.upstream.at[xl], partner)
    upstream_own = net.keep(r.cotangent.at[xl], r.upstream.at[xl])

    forwarded = {}

    def block_of(dz, dx):
        return r.row.at[(z - dz) % ZS, (xl + dx) % 2, c]

    def to_sibling(dz, dx):
        forwarded[dz, dx] = net.send(block_of(dz, dx), block_of(dz, dx), sibling)

    def project(dz):
        source = (z - dz) % ZS
        for dx in range(2):
            forwarded[dz, dx].wait()
        rows = aligned(source, BLOCK)
        product = dot_nn(r.row[source].reshape(BLOCK, 1024), r.head_weights[...])
        r.raw[rows, :] = product[:, :384]
        r.values[rows, :] = product[:, 384:].astype(BF16)
        for part in range(3):
            gain = r.query_gain[...] if part < 2 else r.key_gain[...]
            normed, inverse = normalize(product[:, part * HD : (part + 1) * HD], gain)
            r.inverses[rows, part : part + 1] = inverse
            turned = normed * r.cosines[rows, :] + pltpu.roll(normed, 64, 1) * r.sines[rows, :]
            if part < 2:
                r.queries[rows, part * HD : (part + 1) * HD] = turned.astype(BF16)
            else:
                r.keys[rows, :] = turned.astype(BF16)

    loads = net.local_group()
    for ref, start, width in (
        (r.query_weight, 0, 256),
        (r.key_weight, 256, 128),
        (r.value_weight, 384, 128),
    ):
        loads.add(ref.at[:, aligned(head, width)], r.head_weights.at[:, pl.ds(start, width)])
    small_loads = net.local_group()
    small_loads.add(r.cosines_in, r.cosines).add(r.sines_in, r.sines)
    gain_loads = [
        net.keep(r.query_gain_in, r.query_gain),
        net.keep(r.key_gain_in, r.key_gain),
        net.keep(r.attention_gain_in, r.attention_gain),
        net.keep(r.feedforward_gain_in, r.feedforward_gain),
    ]
    load_wo = net.keep(r.output_weight, r.wo)
    load_wgu = net.keep(r.gate_weight, r.wgu.at[:, pl.ds(0, 3072)])
    load_wgu.add(r.up_weight, r.wgu.at[:, pl.ds(3072, 3072)])
    load_wd = net.keep(r.down_weight, r.wd)

    loads.wait()
    small_loads.wait()
    for load in gain_loads:
        load.wait()
    own_block.wait()
    to_sibling(0, 0)
    arrived[0, 1].wait()
    for dz, target in ((1, up_z), (3, down_z)):
        arrived[dz, 1] = net.send(block_of(0, 1), block_of(0, 1), target)
    to_sibling(0, 1)
    arrived[1, 0].wait()
    arrived[2, 0] = net.send(block_of(1, 0), block_of(1, 0), up_z)
    to_sibling(1, 0)
    arrived[3, 0].wait()
    to_sibling(3, 0)
    arrived[3, 1].wait()
    arrived[2, 1] = net.send(block_of(3, 1), block_of(3, 1), down_z)
    to_sibling(3, 1)
    arrived[1, 1].wait()
    to_sibling(1, 1)
    project(0)
    project(1)
    project(3)
    for dx in range(2):
        arrived[2, dx].wait()
        to_sibling(2, dx)
    document_landings.wait()
    document_landings_own.wait()
    lane = lax.broadcasted_iota(jnp.int32, (1, 128), 1)
    pieces = []
    for block in range(8):
        even = r.row_documents[2 * block, 0:1, :]
        odd = r.row_documents[2 * block + 1, 0:1, :]
        piece = jnp.where(lane < 64, even, odd)
        pieces.append(piece)
        r.document_column[block * 128 : (block + 1) * 128, :] = jnp.broadcast_to(piece, (128, 128)).T
    document_row = jnp.concatenate(pieces, axis=1)
    project(2)

    def visible_in(block):
        count = (block + 1) * BLOCK
        rows = slice(block * BLOCK, count)
        same = r.document_column[rows, 0:1] == document_row[:, :count]
        row_at = block * BLOCK + lax.broadcasted_iota(jnp.int32, (BLOCK, count), 0)
        column_at = lax.broadcasted_iota(jnp.int32, (BLOCK, count), 1)
        return same & (row_at >= column_at)

    attn_landings = {dz: [] for dz in ORDER}
    by_source = [[net.group() for _ in ORDER] for _ in range(2)]
    by_core = [net.local_group() for _ in range(2)]
    first_send, first_keep = by_source[0][0].index, by_core[0].index

    def head_copies(h):
        columns = aligned(h, HD)
        slot = r.attn_tokens.at[:, :, aligned(head * 2 + h, HD)]
        copies = [
            net.remote(r.attn_heads.at[t[2], :, t[4], :, columns], slot, t, first_send + h * 4 + dz)
            for (dz, _), t in zip(ZC, zc)
        ]
        own = pltpu.make_async_copy(
            r.attn_heads.at[z, :, c, :, columns], slot, net.local_sems.at[first_keep + h]
        )
        return copies + [own]

    @pl.loop(0, 2)
    def _(h):
        columns = aligned(h, HD)
        for block in range(4):
            rows = slice(block * BLOCK, (block + 1) * BLOCK)
            count = (block + 1) * BLOCK
            scores = dot_nt(r.queries[rows, columns], r.keys[:count, :])
            scores = jnp.where(visible_in(block), scores * (SCALE * LOG2E), MASKED)
            top = jnp.max(scores, axis=-1, keepdims=True)
            soft = jnp.exp2(scores - top)
            total = jnp.sum(soft, axis=-1, keepdims=True)
            mixed = dot_nn(soft.astype(BF16), r.values[:count, :]) / total
            r.attended[rows, columns] = mixed
            r.attn_heads[block, :, :, :, columns] = mixed.astype(BF16).reshape(2, 2, 64, HD)
            r.log_total[h, rows, :] = top + jnp.log2(total)
        for copy in head_copies(h):
            copy.start()

    for h in range(2):
        by_core[h].units = 2 * 64 * HD
        attn_landings[0].append(by_core[h])
        for dz in ORDER:
            by_source[h][dz].units = 2 * 64 * HD * (1 if dz == 0 else 2)
            attn_landings[dz].append(by_source[h][dz])

    def chain(shift, src, slot_of, half_of):
        ahead, behind = shift(1), shift(-1)
        state = Refs()
        state.slot_of, state.half_of, state.ahead, state.behind = slot_of, half_of, ahead, behind
        state.far = shift(2)
        state.from_behind = net.send(src, slot_of(at), ahead)
        state.from_ahead = net.send(src, slot_of(at), behind)
        state.near = [net.send(src, slot_of(at), sibling), net.keep(src, slot_of(at))]
        return state

    def chain_middle(state):
        half_of, behind, ahead = state.half_of, state.behind, state.ahead
        state.from_behind.wait()
        state.beyond = [net.send(half_of(behind, 0), half_of(behind, 0), ahead)]
        state.from_ahead.wait()
        state.beyond.append(net.send(half_of(ahead, 1), half_of(ahead, 1), behind))
        for source in (behind, ahead):
            state.near.append(net.send(state.slot_of(source), state.slot_of(source), sibling))

    def chain_forward(state):
        for landing in state.beyond:
            landing.wait()
        state.last = net.send(state.slot_of(state.far), state.slot_of(state.far), sibling)

    def chain_near(state):
        for item in state.near:
            item.wait()

    def chain_wait(state):
        chain_near(state)
        state.last.wait()

    load_wo.wait()
    turned = jnp.zeros((1024, 128), F32)
    for dz in ORDER:
        for landing in attn_landings[dz]:
            landing.wait()
        columns = aligned((z - dz) % ZS, 512)
        turned = turned + dot_nt(r.wo[:, columns], r.attn_tokens[:, :, columns].reshape(128, 512))
    branch = turned.T
    r.branch[...] = branch
    branch_normed, branch_inverse = normalize(branch, r.attention_gain[...])
    residual = r.row[z, :, c].reshape(128, 1024).astype(F32) + branch_normed
    r.residual[...] = residual
    r.residual_low[...] = residual.astype(BF16)
    def rows_of(group, index):
        def slot_of(who):
            return group.at[aligned(index(who) * 2 + who[4], 128), :]

        def half_of(who, half):
            return group.at[aligned((index(who) * 2 + who[4]) * 2 + half, 64), :]

        return (slot_of, half_of)

    def y_of(who):
        return who[1]

    def x_of(who):
        return who[0] * 2 + who[3]

    residual_chain = chain(lambda step: shifted(at, dy=step), r.residual_low, *rows_of(r.residual_y, y_of))
    load_wgu.wait()

    @pl.loop(0, 3)
    def _(tile):
        columns, up_columns = aligned(tile, 1024), aligned(tile + 3, 1024)
        gate = dot_nn(r.residual_low[...], r.wgu[:, columns])
        up = dot_nn(r.residual_low[...], r.wgu[:, up_columns])
        sigmoid_gate = lax.logistic(gate)
        silu = gate * sigmoid_gate
        r.activated[:, columns] = (silu * up).astype(BF16)
        r.up_factor[:, columns] = silu
        r.gate_factor[:, columns] = up * sigmoid_gate * (1.0 + gate * (1.0 - sigmoid_gate))

    def to_columns(src, first, group, index, targets):
        slot = group.at[aligned(index(at) * 2 + c, 128), :]
        items = net.together(
            [(src.at[:, aligned(first + index(t) * 2 + t[4], 384)], slot, t) for t in targets]
        )
        return [items, net.keep(src.at[:, aligned(first + index(at) * 2 + c, 384)], slot)]

    activated_landings = to_columns(r.activated, 0, r.activated_all, x_of, xc)
    load_wd.wait()

    @pl.loop(0, 2)
    def _(part):
        rows = aligned(part, 512)
        r.down[:, rows] = dot_nt(r.wd[rows, :], r.activated[...]).T

    down = r.down[...]
    upstream_landing.wait()
    upstream_own.wait()
    down_normed, down_inverse = normalize(down, r.feedforward_gain[...])
    layer_output = (r.residual[...] + down_normed).reshape(2, 64, 1024)
    r.layer_output[...] = layer_output
    r.out_low[...] = layer_output.astype(BF16)
    upstream = r.upstream[...].reshape(128, 1024).astype(F32)
    down_grad, feedforward_gain_grad = norm_back(upstream, down, down_inverse, r.feedforward_gain[...])
    r.down_low[...] = down_grad.astype(BF16)
    down_chain = chain(lambda step: shifted(at, dx=step), r.down_low, *rows_of(r.down_all, x_of))

    @pl.loop(0, 3)
    def _(tile):
        columns, up_columns = aligned(tile, 1024), aligned(tile + 3, 1024)
        act_grad = dot_nn(r.down_low[...], r.wd[:, columns])
        r.gate_up_low[:, columns] = (act_grad * r.gate_factor[:, columns]).astype(BF16)
        r.gate_up_low[:, up_columns] = (act_grad * r.up_factor[:, columns]).astype(BF16)

    up_landings = to_columns(r.gate_up_low, 8, r.up_all, y_of, yc)

    @pl.loop(0, 2)
    def _(part):
        rows = aligned(part, 512)
        r.residual_grad[:, rows] = dot_nt(r.wgu[rows, :], r.gate_up_low[...]).T

    chain_middle(residual_chain)
    residual_grad = r.upstream[...].reshape(128, 1024).astype(F32) + r.residual_grad[...]
    r.residual_grad[...] = residual_grad
    branch_grad, attention_gain_grad = norm_back(
        residual_grad, r.branch[...], branch_inverse, r.attention_gain[...]
    )
    for i in range(8):
        r.gains_own[i : i + 1, :] = attention_gain_grad[:, i * 128 : (i + 1) * 128]
        r.gains_own[8 + i : 9 + i, :] = feedforward_gain_grad[:, i * 128 : (i + 1) * 128]
    branch_low = branch_grad.astype(BF16)
    r.branch_low[...] = branch_low.reshape(2, 64, 1024)
    attn_grad_landings = net.group()
    for dz in (2, 1, 3, 0):
        columns = aligned((z + dz) % ZS, 512)
        product = dot_nn(r.branch_low[...].reshape(128, 1024), r.wo[:, columns])
        r.attn_grad[:, :, columns] = product.astype(BF16).reshape(2, 64, 512)
        for (step, _), t in zip(ZC, zc):
            if step == dz:
                attn_grad_landings.add(
                    r.attn_grad.at[:, :, aligned(t[2] * 2 + t[4], 256)], r.attn_grad_row.at[z, :, c], t
                )
    attn_grad_own = net.keep(r.attn_grad.at[:, :, aligned(head, 256)], r.attn_grad_row.at[z, :, c])
    branch_chain = chain(
        lambda step: shifted(at, dz=step),
        r.branch_low,
        lambda who: r.branch_row.at[who[2], :, who[4]],
        lambda who, half: r.branch_row.at[who[2], half, who[4]],
    )
    gate_landings = to_columns(r.gate_up_low, 0, r.gate_all, y_of, yc)
    head_loads = net.local_group()
    for i in range(8):
        for ref, start, width in (
            (r.query_weight, 0, 256),
            (r.key_weight, 256, 128),
            (r.value_weight, 384, 128),
        ):
            head_loads.add(ref.at[:, pl.ds(i * width, width)], r.wgu.at[:, pl.ds(i * 512 + start, width)])
    def total(own, others, landings):
        for landing in landings:
            landing.wait()
        result = own.astype(F32)
        for i in range(others.shape[0]):
            result = result + others[i].astype(F32)
        return result

    def wait_all(items):
        for item in items:
            item.wait()

    across = shifted(at, flip_xh=1)
    ending, swaps = net.group(), net.group()
    ending_own = net.local_group()

    def replicate(pieces, slot_of, wide_of, y_first):
        along = [net.group() if y_first else ending for _ in ys]
        over = ending if y_first else net.group()
        for src, (xl_to, c_to), mine in pieces:
            if mine:
                ending_own.add(src, slot_of(at))
            else:
                ending.add(src, slot_of(at), (xh, y, z, xl_to, c_to))
            over.add(src, slot_of(at), (1 - xh, y, z, xl_to, c_to))
            for group, t in zip(along, ys):
                group.add(src, slot_of(at), (xh, t[1], z, xl_to, c_to))

        def second():
            if y_first:
                for step, group in enumerate(along):
                    group.wait()
                    source = shifted(at, dy=-(step + 1))
                    ending.add(wide_of(source), wide_of(source), across)
            else:
                over.wait()
                for t in ys:
                    ending.add(wide_of(across), wide_of(across), t)

        return second

    def both_cores(done):
        return [(done.at[c], (xl, c), True), (done.at[1 - c], (xl, 1 - c), False)]

    def four_devices(done):
        return [
            (done.at[xl_to, c_to], (xl_to, c_to), (same_xl, same_c) == (True, True))
            for xl_to, same_xl in ((xl, True), (1 - xl, False))
            for c_to, same_c in ((c, True), (1 - c, False))
        ]

    def one_device(got):
        return [(got, (xl, c), True)]

    def ring_start(piece_of, far, landed, targets):
        ahead, opposite, behind = targets
        half = far.shape[1]
        first, last = pl.ds(0, half), pl.ds(half, half)
        state = Refs()
        state.targets, state.far, state.landed = targets, far, landed
        state.from_far = net.together(
            [
                (piece_of(opposite).at[first], far.at[0], ahead),
                (piece_of(opposite).at[last], far.at[1], behind),
            ]
        )
        state.near = net.together(
            [
                (piece_of(ahead).at[last], landed.at[0, last], ahead),
                (piece_of(behind).at[first], landed.at[1, first], behind),
            ]
        )
        state.wait = lambda: (state.near.wait(), state.summed.wait())
        return [state]

    def ring_middle(states, value_of, middle):
        (state,) = states
        ahead, _, behind = state.targets
        half = state.far.shape[1]
        first, last = pl.ds(0, half), pl.ds(half, half)
        state.from_far.wait()
        middle[0] = (value_of(ahead)[:half].astype(F32) + state.far[0].astype(F32)).astype(BF16)
        middle[1] = (value_of(behind)[half:].astype(F32) + state.far[1].astype(F32)).astype(BF16)
        state.summed = net.together(
            [
                (middle.at[0], state.landed.at[0, first], ahead),
                (middle.at[1], state.landed.at[1, last], behind),
            ]
        )

    def along_y(src, slot):
        ending_own.add(src, slot)
        for t in ys:
            ending.add(src, slot, t)

    def swap(own, low, own_to, got_to):
        swaps.add(low.at[1 - xl], got_to, partner)
        ending_own.add(own.at[xl], own_to)

    r.key_sum[...] = jnp.zeros_like(r.key_sum)
    r.value_sum[...] = jnp.zeros_like(r.value_sum)
    attn_grad_landings.wait()
    attn_grad_own.wait()

    def rope_norm_back(grad, part, rows, gain):
        turned = grad * r.cosines[rows, :] - pltpu.roll(grad, 64, 1) * r.sines[rows, :]
        vector = r.raw[rows, part * HD : (part + 1) * HD]
        result, gain_part = norm_back(turned, vector, r.inverses[rows, part : part + 1], gain)
        return (result.astype(BF16).reshape(2, 2, 64, HD), gain_part)

    def backward_block(block):
        rows = slice(block * BLOCK, (block + 1) * BLOCK)
        count = (block + 1) * BLOCK
        visible = visible_in(block)
        for h in range(2):
            columns = slice(h * HD, (h + 1) * HD)
            query = r.queries[rows, columns]
            grad = r.attn_grad_row[block, :, :, :, columns].reshape(BLOCK, HD)
            delta = jnp.sum(grad.astype(F32) * r.attended[rows, columns], axis=-1, keepdims=True)
            scores = dot_nt(query, r.keys[:count, :]) * (SCALE * LOG2E)
            soft = jnp.exp2(jnp.where(visible, scores - r.log_total[h, rows, :], MASKED))
            r.value_sum[:count, :] += dot_tn(soft.astype(BF16), grad)
            soft_grad = dot_nt(grad, r.values[:count, :])
            score_low = (soft * (soft_grad - delta)).astype(BF16)
            query_grad = dot_nn(score_low, r.keys[:count, :]) * SCALE
            r.key_sum[:count, :] += dot_tn(score_low, query)
            low, gain_part = rope_norm_back(query_grad, h, rows, r.query_gain[...])
            r.lows[block, :, :, :, columns] = low
            r.gains_own[16:17, :] += gain_part

    def by_rows(product):
        return product.astype(BF16).reshape(4, 2, 2, 2, 32, 384)

    def to_heads(done, got, width):
        items = [net.together([(done.at[t[2], t[4]], got.at[:, aligned(head, width)], t) for t in zc])]
        return items + [net.keep(done.at[z, c], got.at[:, aligned(head, width)])]

    r.gains_own[16:24, :] = jnp.zeros((8, 128), F32)
    wait_all(activated_landings)
    load_activated = net.keep(r.activated_all, r.wd.at[:, pl.ds(768, 384)])
    backward_block(0)
    chain_middle(down_chain)
    swap(r.layer_output, r.out_low, r.out_own, r.out_got)
    chain_near(residual_chain)
    near_up = net.local_group()
    for who in (at, residual_chain.behind, residual_chain.ahead):
        rows = aligned(y_of(who), 256)
        near_up.add(r.residual_y.at[rows, :], r.wo.at[rows, pl.ds(0, 1024)])
    chain_forward(residual_chain)
    backward_block(1)
    backward_block(2)
    chain_wait(residual_chain)
    rows = aligned(y_of(residual_chain.far), 256)
    far_up = net.keep(r.residual_y.at[rows, :], r.wo.at[rows, pl.ds(0, 1024)])
    wait_all(up_landings)
    load_up = net.keep(r.up_all, r.wd.at[:, pl.ds(0, 384)])
    backward_block(3)
    wait_all([near_up, far_up, load_up])
    r.own_up[...] = by_rows(dot_tn(r.wo[:, :1024], r.wd[:, :384]))
    first_up = [net.together([(r.own_up.at[:, t[3], :, t[0]], r.all_up.at[i], t) for i, t in enumerate(xs)])]
    chain_middle(branch_chain)
    chain_near(down_chain)
    near_down = net.local_group()
    for who in (at, down_chain.behind, down_chain.ahead):
        rows = aligned(x_of(who), 256)
        near_down.add(r.down_all.at[rows, :], r.wgu.at[rows, pl.ds(4096, 1024)])
    chain_forward(down_chain)
    key_total = jnp.zeros((1, HD), F32)
    for block in range(4):
        rows = slice(block * BLOCK, (block + 1) * BLOCK)
        low, gain_part = rope_norm_back(r.key_sum[rows, :] * SCALE, 2, rows, r.key_gain[...])
        r.lows[block, :, :, :, 256:384] = low
        r.lows[block, :, :, :, 384:] = r.value_sum[rows, :].astype(BF16).reshape(2, 2, 64, HD)
        key_total = key_total + gain_part
    r.gains_own[17:18, :] = key_total
    low_landings = {dz: net.group() for dz in ORDER}

    def send_lows(dz_here):
        for (dz, dc), t in zip(ZC, zc):
            if dz == dz_here:
                low_landings[dz].add(r.lows.at[t[2], :, t[4]], r.low_tokens.at[:, :, aligned(head, 512)], t)

    low_own = net.keep(r.lows.at[z, :, c], r.low_tokens.at[:, :, aligned(head, 512)])
    send_lows(0)
    gains_y = [net.together([(r.gains_own, r.gains_y.at[i], ys[i]) for i in range(3)])]
    row = r.row[...].reshape(1024, 1024)
    low_columns = dot_tn(row, r.lows[...].reshape(1024, 512)).astype(BF16)
    r.own_query[...] = low_columns[:, :256].reshape(4, 2, 2, 4, 16, 256)
    first_query = ring_start(lambda t: r.own_query.at[:, :, :, t[1]], r.far_query, r.all_query, ys)
    r.own_kv[...] = low_columns[:, 256:].reshape(4, 2, 2, 4, 16, 256)
    first_kv = [net.together([(r.own_kv.at[:, t[3], :, :, :, aligned(t[0], 128)], r.all_kv.at[i], t) for i, t in enumerate(xs)])]
    send_lows(1)
    wait_all(gate_landings)
    load_gate = net.keep(r.gate_all, r.wd.at[:, pl.ds(384, 384)])
    chain_wait(down_chain)
    rows = aligned(x_of(down_chain.far), 256)
    load_down = net.keep(r.down_all.at[rows, :], r.wgu.at[rows, pl.ds(4096, 1024)])
    wait_all([near_down, load_down, load_activated])
    product = dot_tn(r.wgu[:, 4096:5120], r.wd[:, 768:1152])
    r.own_down[...] = product.astype(BF16).reshape(4, 2, 2, 4, 16, 384)
    first_down = ring_start(lambda t: r.own_down.at[:, :, :, t[1]], r.far_down, r.all_down, ys)
    load_gate.wait()
    r.own_gate[...] = by_rows(dot_tn(r.wo[:, :1024], r.wd[:, 384:768]))
    first_gate = [net.together([(r.own_gate.at[t[2]], r.all_gate.at[i], t) for i, t in enumerate(zs)])]
    chain_forward(branch_chain)
    ring_middle(first_query, lambda t: r.own_query[:, :, :, t[1]], r.mid_query)
    ring_middle(first_down, lambda t: r.own_down[:, :, :, t[1]], r.mid_down)
    chain_wait(branch_chain)
    output_columns = dot_tn(r.branch_row[...].reshape(1024, 1024), r.attn_heads[...].reshape(1024, 256))
    r.own_output[...] = output_columns.astype(BF16).reshape(4, 2, 2, 4, 16, 256)
    first_output = ring_start(lambda t: r.own_output.at[:, :, :, t[1]], r.far_output, r.all_output, ys)
    r.next_up[...] = total(r.own_up[:, at[3], :, at[0]], r.all_up, first_up).astype(BF16)
    then_up = [net.together([(r.next_up.at[t[2]], r.then_up.at[i], t) for i, t in enumerate(zs)])]
    r.gains_next[...] = total(r.gains_own[...], r.gains_y, gains_y)
    gains_x = [net.together([(r.gains_next, r.gains_x.at[i], xs[i]) for i in range(3)])]
    r.next_query[...] = total(r.own_query[:, :, :, at[1]], r.all_query, first_query).astype(BF16)
    then_query = [net.together([(r.next_query.at[:, t[3]], r.then_query.at[i], t) for i, t in enumerate(xs)])]
    r.next_down[...] = total(r.own_down[:, :, :, at[1]], r.all_down, first_down).astype(BF16)
    then_down = [net.together([(r.next_down.at[t[2]], r.then_down.at[i], t) for i, t in enumerate(zs)])]
    r.next_kv[...] = total(r.own_kv[:, at[3], :, :, :, aligned(at[0], 128)], r.all_kv, first_kv).astype(BF16)
    then_kv = [net.together([(r.next_kv.at[:, :, t[1]], r.then_kv.at[i], t) for i, t in enumerate(ys)])]
    ring_middle(first_output, lambda t: r.own_output[:, :, :, t[1]], r.mid_output)
    send_lows(3)
    r.next_gate[...] = total(r.own_gate[at[2]], r.all_gate, first_gate).astype(BF16)
    then_gate = [net.together([(r.next_gate.at[t[3], :, t[0]], r.then_gate.at[i], t) for i, t in enumerate(xs)])]
    r.gains_last[...] = total(r.gains_next[...], r.gains_x, gains_x)
    gains_zc = [net.together([(r.gains_last, r.gains_zc.at[i], t) for i, t in enumerate(zc)])]
    r.done_up[...] = total(r.next_up[z], r.then_up, then_up).astype(BF16)
    second_up = replicate(
        both_cores(r.done_up),
        lambda who: r.up_grad.at[aligned(who[0], 32), aligned(who[1] * 2 + who[4], 384)],
        lambda who: r.up_grad.at[aligned(who[0], 32), aligned(who[1], 768)],
        True,
    )
    r.done_kv[...] = total(r.next_kv[:, :, y], r.then_kv, then_kv).astype(BF16)
    got_kv = to_heads(r.done_kv, r.got_kv, 128)
    r.done_down[...] = total(r.next_down[z], r.then_down, then_down).astype(BF16)
    second_down = replicate(
        four_devices(r.done_down),
        lambda who: r.down_grad.at[aligned(who[1], 16), aligned((who[0] * 2 + who[3]) * 2 + who[4], 384)],
        lambda who: r.down_grad.at[aligned(who[1], 16), aligned(who[0], 1536)],
        False,
    )
    r.next_output[...] = total(r.own_output[:, :, :, at[1]], r.all_output, first_output).astype(BF16)
    then_output = [net.together([(r.next_output.at[:, t[3]], r.then_output.at[i], t) for i, t in enumerate(xs)])]
    r.done_query[...] = total(r.next_query[:, xl], r.then_query, then_query).astype(BF16)
    got_query = to_heads(r.done_query, r.got_query, 256)
    send_lows(2)
    r.done_gate[...] = total(r.next_gate[xl, :, xh], r.then_gate, then_gate).astype(BF16)
    second_gate = replicate(
        both_cores(r.done_gate),
        lambda who: r.gate_grad.at[aligned(who[0], 32), aligned(who[1] * 2 + who[4], 384)],
        lambda who: r.gate_grad.at[aligned(who[0], 32), aligned(who[1], 768)],
        True,
    )
    wait_all(got_kv)
    second_kv = replicate(
        one_device(r.got_kv),
        lambda who: r.key_value_grad.at[who[0], aligned(who[1], 16), :],
        lambda who: r.key_value_grad.at[who[0], aligned(who[1], 16), :],
        False,
    )
    second_down()
    second_up()
    r.done_output[...] = total(r.next_output[:, xl], r.then_output, then_output).astype(BF16)
    got_output = to_heads(r.done_output, r.got_output, 256)
    wait_all(got_query)
    along_y(r.got_query, r.query_weight_grad.at[aligned(y, 16), :])
    second_gate()
    second_kv()
    head_loads.wait()
    low_own.wait()
    for dz in ORDER:
        low_landings[dz].wait()

    @pl.loop(0, 2)
    def _(part):
        rows = aligned(part, 512)
        r.down[:, rows] = dot_nt(r.wgu[rows, pl.ds(0, 4096)], r.low_tokens[...].reshape(128, 4096)).T

    input_grad = (r.residual_grad[...] + r.down[...]).reshape(2, 64, 1024)
    r.input_grad[...] = input_grad
    r.grad_low[...] = input_grad.astype(BF16)
    swap(r.input_grad, r.grad_low, r.grad_own, r.grad_got)
    wait_all(got_output)
    along_y(r.got_output, r.output_weight_grad.at[aligned(y, 16), :])
    wait_all(gains_zc)
    gains = r.gains_last[...]
    for i in range(7):
        gains = gains + r.gains_zc[i]
    r.gains_final[...] = gains
    net.keep(r.gains_final, r.gains)
    assert (net.next_send, net.next_keep) == (SENDS, KEEPS), (net.next_send, net.next_keep)
    net.drain()


def layer(*arrays):
    return pl.pallas_call(
        layer_kernel,
        out_shape=[shape(*item) for item in OUTPUTS.values()],
        in_specs=[pl.BlockSpec(memory_space=pl.ANY)] * len(INPUTS),
        out_specs=[pl.BlockSpec(memory_space=pl.ANY)] * len(OUTPUTS),
        scratch_shapes=[pltpu.VMEM(*item) for item in [*SCRATCH.values(), *SMALL.values()]]
        + [
            pltpu.SemaphoreType.DMA((SENDS,)),
            pltpu.SemaphoreType.DMA((SENDS,)),
            pltpu.SemaphoreType.DMA((KEEPS,)),
        ],
        compiler_params=pltpu.CompilerParams(
            collective_id=0, has_side_effects=True, vmem_limit_bytes=VMEM_LIMIT
        ),
        name="layer",
    )(*arrays)


def widen_kernel(
    out_own, grad_own, out_got, grad_got, query, key_value, output, gate, up, down, gains,
    out_to, grad_to, query_to, key_to, value_to, output_to, gate_to, up_to, down_to,
    query_gain, key_gain, attention_gain, feedforward_gain,
):
    lower = (lax.axis_index("seq") // 2) % 2 == 0
    for own, got, to in ((out_own, out_got, out_to), (grad_own, grad_got, grad_to)):
        mine, other = own[...], got[...].astype(F32)
        to[0] = jnp.where(lower, mine, other)
        to[1] = jnp.where(lower, other, mine)
    query_to[...] = query[...].astype(F32)
    key_to[...] = key_value[0].astype(F32)
    value_to[...] = key_value[1].astype(F32)
    output_to[...] = output[...].astype(F32)
    gate_to[...] = gate[...].astype(F32)
    up_to[...] = up[...].astype(F32)
    down_to[...] = down[...].astype(F32)
    attention_gain[...] = gains[0:8, :]
    feedforward_gain[...] = gains[8:16, :]
    query_gain[...] = gains[16:17, :]
    key_gain[...] = gains[17:18, :]


def widen(*arrays):
    steps = 2
    rows = 64 // steps

    def flat(columns):
        return pl.BlockSpec((rows, columns), lambda i: (i, 0))

    def paired(columns):
        return pl.BlockSpec((2, rows, columns), lambda i: (0, i, 0))

    def whole(count):
        return pl.BlockSpec((count, 128), lambda i: (0, 0))

    return pl.pallas_call(
        widen_kernel,
        grid=(steps,),
        out_shape=[shape((2, 64, 1024), F32)] * 2
        + [shape((64, n), F32) for n in (2048, 1024, 1024, 2048, 3072, 3072, 3072)]
        + [shape((n, 128), F32) for n in (1, 1, 8, 8)],
        in_specs=[flat(1024)] * 4
        + [flat(2048), paired(1024), flat(2048)]
        + [flat(3072)] * 3
        + [whole(24)],
        out_specs=[paired(1024)] * 2
        + [flat(n) for n in (2048, 1024, 1024, 2048, 3072, 3072, 3072)]
        + [whole(n) for n in (1, 1, 8, 8)],
        name="widen",
    )(*arrays)


VMEM_LIMIT = 63 * 2**20


def per_device(
    hidden_in,
    query_weight,
    key_weight,
    value_weight,
    output_weight,
    gate_weight,
    up_weight,
    down_weight,
    query_gain,
    key_gain,
    attention_gain,
    feedforward_gain,
    document_ids,
    cotangent,
):
    results = layer(
        hidden_in, cotangent,
        query_weight, key_weight, value_weight, output_weight, gate_weight, up_weight, down_weight,
        document_ids, *rope_tables(),
        query_gain[None, :], key_gain[None, :], attention_gain[None, :], feedforward_gain[None, :],
    )[:11]
    results = widen(*results)
    return tuple(results[:9]) + (results[9][0], results[10][0], results[11].reshape(1024), results[12].reshape(1024))


def solution(mesh):
    tokens = P("rows", "seq", None)
    split = P("seq", None)
    return jax.shard_map(
        per_device,
        mesh=mesh,
        in_specs=(tokens,) + (P(),) * 11 + (P("rows", "seq"), tokens),
        out_specs=(tokens, tokens) + (split,) * 7 + (P(),) * 4,
        check_vma=False,
    )
```

```python
import functools

import jax
import jax.numpy as jnp
import numpy as np
from jax import lax
from jax.experimental import pallas as pl
from jax.experimental.pallas import tpu as pltpu
from jax.sharding import PartitionSpec as P

HD = 128
EPSILON = 1e-06
ROPE_BASE = 1000000.0
MASKED = -1e30
LOG2E = 1.4426950408889634
SCALE = HD ** (-0.5)
MESH = pl.DeviceIdType.MESH
F32 = jnp.float32
BF16 = jnp.bfloat16

YS = 4
ZS = 4
XS = 4


def place():
    rows, seq = lax.axis_index("rows"), lax.axis_index("seq")
    return (rows // YS, rows % YS, seq // 4, (seq // 2) % 2, seq % 2)


def device(xh, y, z, xl, c):
    return (xh * YS + y, z * 4 + xl * 2 + c)


def shifted(at, dx=0, dy=0, dz=0, dc=0, flip_xl=0, flip_xh=0):
    xh, y, z, xl, c = at
    if dx:
        x = (xh * 2 + xl + dx) % XS
        xh, xl = x // 2, x % 2
    if flip_xl:
        xl = 1 - xl
    if flip_xh:
        xh = 1 - xh
    if dc:
        c = 1 - c
    return (xh, (y + dy) % YS, (z + dz) % ZS, xl, c)


class Group:
    def __init__(self, net, index):
        self.net, self.index, self.sender = net, index, index // BUCKET
        self.units, self.here = 0, False

    def add(self, src, dst, target, start=True):
        copy = self.net.remote(src, dst, target, self.sender, self.index)
        if start:
            copy.start()
        self.units += units_of(dst)
        return self

    def wait(self):
        if not self.here:
            self.net.sized(self.units, self.net.recv_sems.at[self.index]).wait()
            self.here = True


class LocalGroup:
    def __init__(self, net, index):
        self.net, self.index = net, index
        self.units, self.here, self.only = 0, False, None

    def add(self, src, dst):
        copy = pltpu.make_async_copy(src, dst, self.net.local_sems.at[self.index])
        copy.start()
        self.only = None if self.units else copy
        self.units += units_of(dst)
        return self

    def wait(self):
        if not self.here:
            if self.only is None:
                self.net.sized(self.units, self.net.local_sems.at[self.index]).wait()
            else:
                self.only.wait()
            self.here = True


def units_of(ref):
    return int(np.prod(ref.shape)) * (1 if ref.dtype == BF16 else 2)


class Net:
    def __init__(self, send_sems, recv_sems, local_sems, measures):
        self.send_sems, self.recv_sems, self.local_sems = send_sems, recv_sems, local_sems
        self.measures = measures
        self.groups, self.locals, self.next_send, self.next_keep = [], [], 0, 0

    def sized(self, units, sem):
        for ref in self.measures:
            columns = ref.shape[-1]
            while columns >= 128:
                rows = units // columns
                if rows * columns == units and rows % 16 == 0 and rows <= ref.shape[0] and columns % 128 == 0:
                    view = ref.at[pl.ds(0, rows), pl.ds(0, columns)]
                    return pltpu.make_async_copy(view, view, sem)
                columns -= 128
        raise ValueError(units)

    def barrier(self, targets):
        barrier = pltpu.get_barrier_semaphore()
        for target in targets:
            pl.semaphore_signal(barrier, inc=1, device_id=device(*target), device_id_type=MESH)
        pl.semaphore_wait(barrier, len(targets))

    def remote(self, src, dst, target, sender, i):
        return pltpu.make_async_remote_copy(
            src_ref=src,
            dst_ref=dst,
            send_sem=self.send_sems.at[sender],
            recv_sem=self.recv_sems.at[i],
            device_id=device(*target),
            device_id_type=MESH,
        )

    def group(self):
        self.groups.append(Group(self, self.next_send))
        self.next_send += 1
        return self.groups[-1]

    def local_group(self):
        self.locals.append(LocalGroup(self, self.next_keep))
        self.next_keep += 1
        return self.locals[-1]

    def send(self, src, dst, target):
        return self.group().add(src, dst, target)

    def together(self, items):
        result = self.group()
        for src, dst, target in items:
            result.add(src, dst, target)
        return result

    def keep(self, src, dst):
        return self.local_group().add(src, dst)

    def drain(self):
        for group in self.locals:
            group.wait()
        sent = {}
        for group in self.groups:
            group.wait()
            sent[group.sender] = sent.get(group.sender, 0) + group.units
        for sender, units in sent.items():
            self.sized(units, self.send_sems.at[sender]).wait()


def shape(dims, dtype=BF16):
    return jax.ShapeDtypeStruct(dims, dtype)


ZC = [(dz, dc) for dz in range(ZS) for dc in range(2) if (dz, dc) != (0, 0)]
ORDER = (0, 1, 3, 2)
BLOCK = 256
BUCKET = 15
SENDS = 93
KEEPS = 36


def rope_tables():
    half = HD // 2
    frequency = ROPE_BASE ** (-(np.arange(half, dtype=np.float64) * 2.0 / HD))
    angles = np.arange(1024, dtype=np.float64)[:, None] * frequency[None, :]
    cosines = np.concatenate([np.cos(angles)] * 2, axis=1)
    sines = np.concatenate([-np.sin(angles), np.sin(angles)], axis=1)
    return (cosines.astype(np.float32), sines.astype(np.float32))


def dot_nn(left, right):
    return jnp.dot(left, right, preferred_element_type=F32)


def dot_nt(left, right):
    return lax.dot_general(left, right, (((1,), (1,)), ((), ())), preferred_element_type=F32)


def dot_tn(left, right):
    return lax.dot_general(left, right, (((0,), (0,)), ((), ())), preferred_element_type=F32)


def normalize(vector, scales):
    inverse = lax.rsqrt(jnp.mean(vector * vector, axis=-1, keepdims=True) + EPSILON)
    return (vector * inverse * scales, inverse)


def norm_back(gradient, vector, inverse, scales):
    normed = vector * inverse
    scales_grad = jnp.sum(gradient * normed, axis=0, keepdims=True)
    scaled = gradient * scales
    vector_grad = inverse * (scaled - normed * jnp.mean(scaled * normed, axis=-1, keepdims=True))
    return (vector_grad, scales_grad)


def aligned(index, width):
    return pl.ds(pl.multiple_of(index * width, width), width)


class Refs:
    pass


INPUTS = dict(
    hidden=0,
    cotangent=0,
    query_weight=0,
    key_weight=0,
    value_weight=0,
    output_weight=0,
    gate_weight=0,
    up_weight=0,
    down_weight=0,
    document_ids_in=((2, 64), jnp.int32),
    cosines_in=((1024, 128), F32),
    sines_in=((1024, 128), F32),
    query_gain_in=((1, 128), F32),
    key_gain_in=((1, 128), F32),
    attention_gain_in=((1, 1024), F32),
    feedforward_gain_in=((1, 1024), F32),
)
SMALL = {name[:-3]: item for name, item in INPUTS.items() if item}
OUTPUTS = dict(
    out_own=((64, 1024), F32),
    grad_own=((64, 1024), F32),
    out_got=((64, 1024), BF16),
    grad_got=((64, 1024), BF16),
    query_weight_grad=((64, 2048), BF16),
    key_value_grad=((2, 64, 1024), BF16),
    output_weight_grad=((64, 2048), BF16),
    gate_grad=((64, 3072), BF16),
    up_grad=((64, 3072), BF16),
    down_grad=((64, 3072), BF16),
    gains=((24, 128), F32),
    residual_y=((1024, 1024), BF16),
    gate_all=((1024, 384), BF16),
    up_all=((1024, 384), BF16),
    down_all=((1024, 1024), BF16),
    activated_all=((1024, 384), BF16),
)
SCRATCH = dict(
    head_weights=((1024, 512), BF16),
    wo=((1024, 2048), BF16),
    wgu=((1024, 6144), BF16),
    wd=((1024, 3072), BF16),
    row=((4, 2, 2, 64, 1024), BF16),
    upstream=((2, 64, 1024), BF16),
    documents=((2, 16, 128), F32),
    row_documents=((16, 16, 128), F32),
    document_column=((1024, 128), F32),
    raw=((1024, 384), F32),
    inverses=((1024, 3), F32),
    queries=((1024, 256), BF16),
    keys=((1024, 128), BF16),
    values=((1024, 128), BF16),
    attended=((1024, 256), F32),
    attn_heads=((4, 2, 2, 64, 256), BF16),
    log_total=((2, 1024, 1), F32),
    attn_tokens=((2, 64, 2048), BF16),
    branch=((128, 1024), F32),
    down=((128, 1024), F32),
    residual=((128, 1024), F32),
    residual_low=((128, 1024), BF16),
    gate_factor=((128, 3072), F32),
    up_factor=((128, 3072), F32),
    activated=((128, 3072), BF16),
    layer_output=((2, 64, 1024), F32),
    down_low=((128, 1024), BF16),
    gate_up_low=((128, 6144), BF16),
    residual_grad=((128, 1024), F32),
    branch_low=((2, 64, 1024), BF16),
    attn_grad=((2, 64, 2048), BF16),
    attn_grad_row=((4, 2, 2, 64, 256), BF16),
    branch_row=((4, 2, 2, 64, 1024), BF16),
    lows=((4, 2, 2, 64, 512), BF16),
    key_sum=((1024, 128), F32),
    value_sum=((1024, 128), F32),
    low_tokens=((2, 64, 4096), BF16),
    input_grad=((2, 64, 1024), F32),
    out_low=((2, 64, 1024), BF16),
    grad_low=((2, 64, 1024), BF16),
    own_gate=((4, 2, 2, 2, 32, 384), BF16),
    all_gate=((3, 2, 2, 2, 32, 384), BF16),
    next_gate=((2, 2, 2, 32, 384), BF16),
    then_gate=((3, 2, 32, 384), BF16),
    done_gate=((2, 32, 384), BF16),
    own_query=((4, 2, 2, 4, 16, 256), BF16),
    all_query=((2, 4, 2, 2, 16, 256), BF16),
    far_query=((2, 2, 2, 2, 16, 256), BF16),
    mid_query=((2, 2, 2, 2, 16, 256), BF16),
    next_query=((4, 2, 2, 16, 256), BF16),
    then_query=((3, 4, 2, 16, 256), BF16),
    done_query=((4, 2, 16, 256), BF16),
    got_query=((16, 2048), BF16),
    own_kv=((4, 2, 2, 4, 16, 256), BF16),
    all_kv=((3, 4, 2, 4, 16, 128), BF16),
    next_kv=((4, 2, 4, 16, 128), BF16),
    then_kv=((3, 4, 2, 16, 128), BF16),
    done_kv=((4, 2, 16, 128), BF16),
    got_kv=((16, 1024), BF16),
    own_output=((4, 2, 2, 4, 16, 256), BF16),
    all_output=((2, 4, 2, 2, 16, 256), BF16),
    far_output=((2, 2, 2, 2, 16, 256), BF16),
    mid_output=((2, 2, 2, 2, 16, 256), BF16),
    next_output=((4, 2, 2, 16, 256), BF16),
    then_output=((3, 4, 2, 16, 256), BF16),
    done_output=((4, 2, 16, 256), BF16),
    got_output=((16, 2048), BF16),
    own_up=((4, 2, 2, 2, 32, 384), BF16),
    all_up=((3, 4, 2, 32, 384), BF16),
    next_up=((4, 2, 32, 384), BF16),
    then_up=((3, 2, 32, 384), BF16),
    done_up=((2, 32, 384), BF16),
    own_down=((4, 2, 2, 4, 16, 384), BF16),
    all_down=((2, 4, 2, 2, 16, 384), BF16),
    far_down=((2, 2, 2, 2, 16, 384), BF16),
    mid_down=((2, 2, 2, 2, 16, 384), BF16),
    next_down=((4, 2, 2, 16, 384), BF16),
    then_down=((3, 2, 2, 16, 384), BF16),
    done_down=((2, 2, 16, 384), BF16),
    gains_own=((24, 128), F32),
    gains_next=((24, 128), F32),
    gains_last=((24, 128), F32),
    gains_final=((24, 128), F32),
    gains_y=((3, 24, 128), F32),
    gains_x=((3, 24, 128), F32),
    gains_zc=((7, 24, 128), F32),
)


def layer_kernel(*refs):
    names = [*INPUTS, *OUTPUTS, *SCRATCH, *SMALL]
    r = Refs()
    for name, ref in zip(names, refs):
        setattr(r, name, ref)
    net = Net(*refs[len(names) :], (r.wd, r.wgu))
    at = place()
    xh, y, z, xl, c = at
    x = xh * 2 + xl
    head = z * 2 + c
    sibling = shifted(at, dc=1)
    partner = shifted(at, flip_xl=1)
    seq_others = [
        shifted(at, dz=dz, dc=dc, flip_xl=dx)
        for dz in range(ZS)
        for dx in range(2)
        for dc in range(2)
        if (dz, dx, dc) != (0, 0, 0)
    ]
    zc = [shifted(at, dz=dz, dc=dc) for dz, dc in ZC]
    yc = [shifted(at, dy=dy, dc=dc) for dy, dc in ZC]
    xc = [shifted(at, dx=dx, dc=dc) for dx, dc in ZC]
    ys = [shifted(at, dy=step) for step in range(1, 4)]
    xs = [shifted(at, dx=step) for step in range(1, 4)]
    zs = [shifted(at, dz=step) for step in range(1, 4)]
    replicas = [
        shifted(at, dy=dy, flip_xh=dx) for dy in range(YS) for dx in range(2) if (dy, dx) != (0, 0)
    ]

    crossed = [shifted(at, dy=dy, dc=dc, flip_xl=1) for dy in range(1, YS) for dc in range(2)]
    barrier_targets = list(seq_others) + yc[1:] + xc[1:] + replicas + crossed
    documents_load = net.keep(r.document_ids_in, r.document_ids)
    net.barrier(barrier_targets)
    up_z, down_z = shifted(at, dz=1), shifted(at, dz=-1)
    parts = [pl.ds(0, 32), pl.ds(32, 32)]
    arrived = {(dz, dx): net.group() for dz, dx in ((1, 0), (3, 0), (1, 1))}
    from_partner = [
        net.send(r.hidden.at[1 - xl, part], r.row.at[z, xl, c, part], partner) for part in parts
    ]
    for dz, target in ((1, up_z), (3, down_z)):
        arrived[dz, 0].add(r.hidden.at[xl], r.row.at[z, xl, c], target)
    own_block = net.keep(r.hidden.at[xl], r.row.at[z, xl, c])
    documents_load.wait()
    own_documents = r.document_ids[...].astype(F32)
    own_documents = jnp.concatenate([own_documents, own_documents], axis=1)
    for i in range(2):
        r.documents[i] = jnp.broadcast_to(own_documents[i : i + 1, :], (16, 128))
    document_slot = r.row_documents.at[z * 4 + xl * 2 + c]
    document_landings = net.together([(r.documents.at[t[3]], document_slot, t) for t in seq_others])
    document_landings_own = net.keep(r.documents.at[xl], document_slot)
    upstream_landing = net.send(r.cotangent.at[1 - xl], r.upstream.at[xl], partner)
    upstream_own = net.keep(r.cotangent.at[xl], r.upstream.at[xl])

    forwarded = {}

    def block_of(dz, dx):
        return r.row.at[(z - dz) % ZS, (xl + dx) % 2, c]

    def to_sibling(dz, dx):
        forwarded[dz, dx] = net.send(block_of(dz, dx), block_of(dz, dx), sibling)

    def project(dz):
        source = (z - dz) % ZS
        for dx in range(2):
            forwarded[dz, dx].wait()
        rows = aligned(source, BLOCK)
        product = dot_nn(r.row[source].reshape(BLOCK, 1024), r.head_weights[...])
        r.raw[rows, :] = product[:, :384]
        r.values[rows, :] = product[:, 384:].astype(BF16)
        for part in range(3):
            gain = r.query_gain[...] if part < 2 else r.key_gain[...]
            normed, inverse = normalize(product[:, part * HD : (part + 1) * HD], gain)
            r.inverses[rows, part : part + 1] = inverse
            turned = normed * r.cosines[rows, :] + pltpu.roll(normed, 64, 1) * r.sines[rows, :]
            if part < 2:
                r.queries[rows, part * HD : (part + 1) * HD] = turned.astype(BF16)
            else:
                r.keys[rows, :] = turned.astype(BF16)

    loads = net.local_group()
    for ref, start, width in (
        (r.query_weight, 0, 256),
        (r.key_weight, 256, 128),
        (r.value_weight, 384, 128),
    ):
        loads.add(ref.at[:, aligned(head, width)], r.head_weights.at[:, pl.ds(start, width)])
    small_loads = net.local_group()
    small_loads.add(r.cosines_in, r.cosines).add(r.sines_in, r.sines)
    gain_loads = [
        net.keep(r.query_gain_in, r.query_gain),
        net.keep(r.key_gain_in, r.key_gain),
        net.keep(r.attention_gain_in, r.attention_gain),
        net.keep(r.feedforward_gain_in, r.feedforward_gain),
    ]
    load_wo = net.keep(r.output_weight, r.wo)
    load_wgu = net.keep(r.gate_weight, r.wgu.at[:, pl.ds(0, 3072)])
    load_wgu.add(r.up_weight, r.wgu.at[:, pl.ds(3072, 3072)])
    load_wd = net.keep(r.down_weight, r.wd)

    loads.wait()
    small_loads.wait()
    for load in gain_loads:
        load.wait()
    own_block.wait()
    to_sibling(0, 0)
    below = [net.group() for _ in parts]
    for landing, part, second in zip(from_partner, parts, below):
        landing.wait()
        piece = r.row.at[z, 1 - xl, c, part]
        arrived[1, 1].add(piece, piece, up_z)
        second.add(piece, piece, down_z)
    to_sibling(0, 1)
    arrived[1, 0].wait()
    arrived[2, 0] = net.send(block_of(1, 0), block_of(1, 0), up_z)
    to_sibling(1, 0)
    arrived[3, 0].wait()
    to_sibling(3, 0)
    arrived[2, 1] = net.group()
    for landing, part in zip(below, parts):
        landing.wait()
        piece = r.row.at[(z + 1) % ZS, 1 - xl, c, part]
        arrived[2, 1].add(piece, piece, down_z)
    to_sibling(3, 1)
    arrived[1, 1].wait()
    to_sibling(1, 1)
    project(0)
    project(1)
    project(3)
    for dx in range(2):
        arrived[2, dx].wait()
        to_sibling(2, dx)
    document_landings.wait()
    document_landings_own.wait()
    lane = lax.broadcasted_iota(jnp.int32, (1, 128), 1)
    pieces = []
    for block in range(8):
        even = r.row_documents[2 * block, 0:1, :]
        odd = r.row_documents[2 * block + 1, 0:1, :]
        piece = jnp.where(lane < 64, even, odd)
        pieces.append(piece)
        r.document_column[block * 128 : (block + 1) * 128, :] = jnp.broadcast_to(piece, (128, 128)).T
    document_row = jnp.concatenate(pieces, axis=1)
    project(2)

    def visible_in(block):
        count = (block + 1) * BLOCK
        rows = slice(block * BLOCK, count)
        same = r.document_column[rows, 0:1] == document_row[:, :count]
        row_at = block * BLOCK + lax.broadcasted_iota(jnp.int32, (BLOCK, count), 0)
        column_at = lax.broadcasted_iota(jnp.int32, (BLOCK, count), 1)
        return same & (row_at >= column_at)

    attn_landings = {dz: [] for dz in ORDER}
    by_source = [[net.group() for _ in ORDER] for _ in range(2)]
    sender = by_source[0][0].sender
    for groups in by_source:
        for group in groups:
            group.sender = sender
    by_core = [net.local_group() for _ in range(2)]
    first_send, first_keep = by_source[0][0].index, by_core[0].index

    def head_copies(h):
        columns = aligned(h, HD)
        slot = r.attn_tokens.at[:, :, aligned(head * 2 + h, HD)]
        copies = [
            net.remote(r.attn_heads.at[t[2], :, t[4], :, columns], slot, t, sender, first_send + h * 4 + dz)
            for (dz, _), t in zip(ZC, zc)
        ]
        own = pltpu.make_async_copy(
            r.attn_heads.at[z, :, c, :, columns], slot, net.local_sems.at[first_keep + h]
        )
        return copies + [own]

    @pl.loop(0, 2)
    def _(h):
        columns = aligned(h, HD)
        for block in range(4):
            rows = slice(block * BLOCK, (block + 1) * BLOCK)
            count = (block + 1) * BLOCK
            scores = dot_nt(r.queries[rows, columns], r.keys[:count, :])
            scores = jnp.where(visible_in(block), scores * (SCALE * LOG2E), MASKED)
            top = jnp.max(scores, axis=-1, keepdims=True)
            soft = jnp.exp2(scores - top)
            total = jnp.sum(soft, axis=-1, keepdims=True)
            mixed = dot_nn(soft.astype(BF16), r.values[:count, :]) / total
            r.attended[rows, columns] = mixed
            r.attn_heads[block, :, :, :, columns] = mixed.astype(BF16).reshape(2, 2, 64, HD)
            r.log_total[h, rows, :] = top + jnp.log2(total)
        for copy in head_copies(h):
            copy.start()

    for h in range(2):
        by_core[h].units = 2 * 64 * HD
        attn_landings[0].append(by_core[h])
        for dz in ORDER:
            by_source[h][dz].units = 2 * 64 * HD * (1 if dz == 0 else 2)
            attn_landings[dz].append(by_source[h][dz])

    def chain(shift, src, slot_of, half_of):
        ahead, behind = shift(1), shift(-1)
        state = Refs()
        state.slot_of, state.half_of, state.ahead, state.behind = slot_of, half_of, ahead, behind
        state.far = shift(2)
        state.from_behind = net.send(src, slot_of(at), ahead)
        state.from_ahead = net.send(src, slot_of(at), behind)
        state.near = [net.send(src, slot_of(at), sibling), net.keep(src, slot_of(at))]
        return state

    def chain_middle(state):
        half_of, behind, ahead = state.half_of, state.behind, state.ahead
        state.from_behind.wait()
        state.beyond = [net.send(half_of(behind, 0), half_of(behind, 0), ahead)]
        state.from_ahead.wait()
        state.beyond.append(net.send(half_of(ahead, 1), half_of(ahead, 1), behind))
        for source in (behind, ahead):
            state.near.append(net.send(state.slot_of(source), state.slot_of(source), sibling))

    def chain_forward(state):
        for landing in state.beyond:
            landing.wait()
        state.last = net.send(state.slot_of(state.far), state.slot_of(state.far), sibling)

    def chain_near(state):
        for item in state.near:
            item.wait()

    def chain_wait(state):
        chain_near(state)
        state.last.wait()

    load_wo.wait()
    turned = jnp.zeros((1024, 128), F32)
    for dz in ORDER:
        for landing in attn_landings[dz]:
            landing.wait()
        columns = aligned((z - dz) % ZS, 512)
        turned = turned + dot_nt(r.wo[:, columns], r.attn_tokens[:, :, columns].reshape(128, 512))
    branch = turned.T
    r.branch[...] = branch
    branch_normed, branch_inverse = normalize(branch, r.attention_gain[...])
    residual = r.row[z, :, c].reshape(128, 1024).astype(F32) + branch_normed
    r.residual[...] = residual
    r.residual_low[...] = residual.astype(BF16)
    def rows_of(group, index):
        def slot_of(who):
            return group.at[aligned(index(who) * 2 + who[4], 128), :]

        def half_of(who, half):
            return group.at[aligned((index(who) * 2 + who[4]) * 2 + half, 64), :]

        return (slot_of, half_of)

    def y_of(who):
        return who[1]

    def x_of(who):
        return who[0] * 2 + who[3]

    residual_chain = chain(lambda step: shifted(at, dy=step), r.residual_low, *rows_of(r.residual_y, y_of))
    load_wgu.wait()

    @pl.loop(0, 3)
    def _(tile):
        columns, up_columns = aligned(tile, 1024), aligned(tile + 3, 1024)
        gate = dot_nn(r.residual_low[...], r.wgu[:, columns])
        up = dot_nn(r.residual_low[...], r.wgu[:, up_columns])
        sigmoid_gate = lax.logistic(gate)
        silu = gate * sigmoid_gate
        r.activated[:, columns] = (silu * up).astype(BF16)
        r.up_factor[:, columns] = silu
        r.gate_factor[:, columns] = up * sigmoid_gate * (1.0 + gate * (1.0 - sigmoid_gate))

    def to_columns(src, first, group, index, targets):
        slot = group.at[aligned(index(at) * 2 + c, 128), :]
        items = net.together(
            [(src.at[:, aligned(first + index(t) * 2 + t[4], 384)], slot, t) for t in targets]
        )
        return [items, net.keep(src.at[:, aligned(first + index(at) * 2 + c, 384)], slot)]

    activated_landings = to_columns(r.activated, 0, r.activated_all, x_of, xc)
    load_wd.wait()

    @pl.loop(0, 2)
    def _(part):
        rows = aligned(part, 512)
        r.down[:, rows] = dot_nt(r.wd[rows, :], r.activated[...]).T

    down = r.down[...]
    upstream_landing.wait()
    upstream_own.wait()
    down_normed, down_inverse = normalize(down, r.feedforward_gain[...])
    layer_output = (r.residual[...] + down_normed).reshape(2, 64, 1024)
    r.layer_output[...] = layer_output
    r.out_low[...] = layer_output.astype(BF16)
    upstream = r.upstream[...].reshape(128, 1024).astype(F32)
    down_grad, feedforward_gain_grad = norm_back(upstream, down, down_inverse, r.feedforward_gain[...])
    r.down_low[...] = down_grad.astype(BF16)
    down_chain = chain(lambda step: shifted(at, dx=step), r.down_low, *rows_of(r.down_all, x_of))

    @pl.loop(0, 3)
    def _(tile):
        columns, up_columns = aligned(tile, 1024), aligned(tile + 3, 1024)
        act_grad = dot_nn(r.down_low[...], r.wd[:, columns])
        r.gate_up_low[:, columns] = (act_grad * r.gate_factor[:, columns]).astype(BF16)
        r.gate_up_low[:, up_columns] = (act_grad * r.up_factor[:, columns]).astype(BF16)

    up_landings = to_columns(r.gate_up_low, 8, r.up_all, y_of, yc)

    @pl.loop(0, 2)
    def _(part):
        rows = aligned(part, 512)
        r.residual_grad[:, rows] = dot_nt(r.wgu[rows, :], r.gate_up_low[...]).T

    chain_middle(residual_chain)
    residual_grad = r.upstream[...].reshape(128, 1024).astype(F32) + r.residual_grad[...]
    r.residual_grad[...] = residual_grad
    branch_grad, attention_gain_grad = norm_back(
        residual_grad, r.branch[...], branch_inverse, r.attention_gain[...]
    )
    for i in range(8):
        r.gains_own[i : i + 1, :] = attention_gain_grad[:, i * 128 : (i + 1) * 128]
        r.gains_own[8 + i : 9 + i, :] = feedforward_gain_grad[:, i * 128 : (i + 1) * 128]
    branch_low = branch_grad.astype(BF16)
    r.branch_low[...] = branch_low.reshape(2, 64, 1024)
    attn_grad_landings = net.group()
    for dz in (2, 1, 3, 0):
        columns = aligned((z + dz) % ZS, 512)
        product = dot_nn(r.branch_low[...].reshape(128, 1024), r.wo[:, columns])
        r.attn_grad[:, :, columns] = product.astype(BF16).reshape(2, 64, 512)
        for (step, _), t in zip(ZC, zc):
            if step == dz:
                attn_grad_landings.add(
                    r.attn_grad.at[:, :, aligned(t[2] * 2 + t[4], 256)], r.attn_grad_row.at[z, :, c], t
                )
    attn_grad_own = net.keep(r.attn_grad.at[:, :, aligned(head, 256)], r.attn_grad_row.at[z, :, c])
    branch_chain = chain(
        lambda step: shifted(at, dz=step),
        r.branch_low,
        lambda who: r.branch_row.at[who[2], :, who[4]],
        lambda who, half: r.branch_row.at[who[2], half, who[4]],
    )
    gate_landings = to_columns(r.gate_up_low, 0, r.gate_all, y_of, yc)
    head_loads = net.local_group()
    for i in range(8):
        for ref, start, width in (
            (r.query_weight, 0, 256),
            (r.key_weight, 256, 128),
            (r.value_weight, 384, 128),
        ):
            head_loads.add(ref.at[:, pl.ds(i * width, width)], r.wgu.at[:, pl.ds(i * 512 + start, width)])
    def total(own, others, landings):
        for landing in landings:
            landing.wait()
        result = own.astype(F32)
        for i in range(others.shape[0]):
            result = result + others[i].astype(F32)
        return result

    def wait_all(items):
        for item in items:
            item.wait()

    across = shifted(at, flip_xh=1)
    ending, swaps = net.group(), net.group()
    ending_own = net.local_group()

    def replicate(pieces, slot_of, wide_of, y_first):
        along = [net.group() if y_first else ending for _ in ys]
        over = ending if y_first else net.group()
        for src, (xl_to, c_to), mine in pieces:
            if mine:
                ending_own.add(src, slot_of(at))
            else:
                ending.add(src, slot_of(at), (xh, y, z, xl_to, c_to))
            over.add(src, slot_of(at), (1 - xh, y, z, xl_to, c_to))
            for group, t in zip(along, ys):
                group.add(src, slot_of(at), (xh, t[1], z, xl_to, c_to))

        def second():
            if y_first:
                for step, group in enumerate(along):
                    group.wait()
                    source = shifted(at, dy=-(step + 1))
                    ending.add(wide_of(source), wide_of(source), across)
            else:
                over.wait()
                for t in ys:
                    ending.add(wide_of(across), wide_of(across), t)

        return second

    def both_cores(done):
        return [(done.at[c], (xl, c), True), (done.at[1 - c], (xl, 1 - c), False)]

    def four_devices(done):
        return [
            (done.at[xl_to, c_to], (xl_to, c_to), (same_xl, same_c) == (True, True))
            for xl_to, same_xl in ((xl, True), (1 - xl, False))
            for c_to, same_c in ((c, True), (1 - c, False))
        ]

    def one_device(got):
        return [(got, (xl, c), True)]

    def ring_start(piece_of, far, landed, targets):
        ahead, opposite, behind = targets
        half = far.shape[1]
        first, last = pl.ds(0, half), pl.ds(half, half)
        state = Refs()
        state.targets, state.far, state.landed = targets, far, landed
        state.from_far = net.together(
            [
                (piece_of(opposite).at[first], far.at[0], ahead),
                (piece_of(opposite).at[last], far.at[1], behind),
            ]
        )
        state.near = net.together(
            [
                (piece_of(ahead).at[last], landed.at[0, last], ahead),
                (piece_of(behind).at[first], landed.at[1, first], behind),
            ]
        )
        state.wait = lambda: (state.near.wait(), state.summed.wait())
        return [state]

    def ring_middle(states, value_of, middle):
        (state,) = states
        ahead, _, behind = state.targets
        half = state.far.shape[1]
        first, last = pl.ds(0, half), pl.ds(half, half)
        state.from_far.wait()
        middle[0] = (value_of(ahead)[:half].astype(F32) + state.far[0].astype(F32)).astype(BF16)
        middle[1] = (value_of(behind)[half:].astype(F32) + state.far[1].astype(F32)).astype(BF16)
        state.summed = net.together(
            [
                (middle.at[0], state.landed.at[0, first], ahead),
                (middle.at[1], state.landed.at[1, last], behind),
            ]
        )

    def along_y(src, slot):
        ending_own.add(src, slot)
        for t in ys:
            ending.add(src, slot, t)

    def swap(own, low, own_to, got_to):
        swaps.add(low.at[1 - xl], got_to, partner)
        ending_own.add(own.at[xl], own_to)

    r.key_sum[...] = jnp.zeros_like(r.key_sum)
    r.value_sum[...] = jnp.zeros_like(r.value_sum)
    attn_grad_landings.wait()
    attn_grad_own.wait()

    def rope_norm_back(grad, part, rows, gain):
        turned = grad * r.cosines[rows, :] - pltpu.roll(grad, 64, 1) * r.sines[rows, :]
        vector = r.raw[rows, part * HD : (part + 1) * HD]
        result, gain_part = norm_back(turned, vector, r.inverses[rows, part : part + 1], gain)
        return (result.astype(BF16).reshape(2, 2, 64, HD), gain_part)

    def backward_block(block):
        rows = slice(block * BLOCK, (block + 1) * BLOCK)
        count = (block + 1) * BLOCK
        visible = visible_in(block)
        for h in range(2):
            columns = slice(h * HD, (h + 1) * HD)
            query = r.queries[rows, columns]
            grad = r.attn_grad_row[block, :, :, :, columns].reshape(BLOCK, HD)
            delta = jnp.sum(grad.astype(F32) * r.attended[rows, columns], axis=-1, keepdims=True)
            scores = dot_nt(query, r.keys[:count, :]) * (SCALE * LOG2E)
            soft = jnp.exp2(jnp.where(visible, scores - r.log_total[h, rows, :], MASKED))
            r.value_sum[:count, :] += dot_tn(soft.astype(BF16), grad)
            soft_grad = dot_nt(grad, r.values[:count, :])
            score_low = (soft * (soft_grad - delta)).astype(BF16)
            query_grad = dot_nn(score_low, r.keys[:count, :]) * SCALE
            r.key_sum[:count, :] += dot_tn(score_low, query)
            low, gain_part = rope_norm_back(query_grad, h, rows, r.query_gain[...])
            r.lows[block, :, :, :, columns] = low
            r.gains_own[16:17, :] += gain_part

    def by_rows(product):
        return product.astype(BF16).reshape(4, 2, 2, 2, 32, 384)

    def to_heads(done, got, width):
        items = [net.together([(done.at[t[2], t[4]], got.at[:, aligned(head, width)], t) for t in zc])]
        return items + [net.keep(done.at[z, c], got.at[:, aligned(head, width)])]

    r.gains_own[16:24, :] = jnp.zeros((8, 128), F32)
    wait_all(activated_landings)
    load_activated = net.keep(r.activated_all, r.wd.at[:, pl.ds(768, 384)])
    backward_block(0)
    chain_middle(down_chain)
    swap(r.layer_output, r.out_low, r.out_own, r.out_got)
    chain_near(residual_chain)
    near_up = net.local_group()
    for who in (at, residual_chain.behind, residual_chain.ahead):
        rows = aligned(y_of(who), 256)
        near_up.add(r.residual_y.at[rows, :], r.wo.at[rows, pl.ds(0, 1024)])
    chain_forward(residual_chain)
    backward_block(1)
    backward_block(2)
    chain_wait(residual_chain)
    rows = aligned(y_of(residual_chain.far), 256)
    far_up = net.keep(r.residual_y.at[rows, :], r.wo.at[rows, pl.ds(0, 1024)])
    wait_all(up_landings)
    load_up = net.keep(r.up_all, r.wd.at[:, pl.ds(0, 384)])
    backward_block(3)
    wait_all([near_up, far_up, load_up])
    r.own_up[...] = by_rows(dot_tn(r.wo[:, :1024], r.wd[:, :384]))
    first_up = [net.together([(r.own_up.at[:, t[3], :, t[0]], r.all_up.at[i], t) for i, t in enumerate(xs)])]
    chain_middle(branch_chain)
    chain_near(down_chain)
    near_down = net.local_group()
    for who in (at, down_chain.behind, down_chain.ahead):
        rows = aligned(x_of(who), 256)
        near_down.add(r.down_all.at[rows, :], r.wgu.at[rows, pl.ds(4096, 1024)])
    chain_forward(down_chain)
    key_total = jnp.zeros((1, HD), F32)
    for block in range(4):
        rows = slice(block * BLOCK, (block + 1) * BLOCK)
        low, gain_part = rope_norm_back(r.key_sum[rows, :] * SCALE, 2, rows, r.key_gain[...])
        r.lows[block, :, :, :, 256:384] = low
        r.lows[block, :, :, :, 384:] = r.value_sum[rows, :].astype(BF16).reshape(2, 2, 64, HD)
        key_total = key_total + gain_part
    r.gains_own[17:18, :] = key_total
    low_landings = {dz: net.group() for dz in ORDER}

    def send_lows(dz_here):
        for (dz, dc), t in zip(ZC, zc):
            if dz == dz_here:
                low_landings[dz].add(r.lows.at[t[2], :, t[4]], r.low_tokens.at[:, :, aligned(head, 512)], t)

    low_own = net.keep(r.lows.at[z, :, c], r.low_tokens.at[:, :, aligned(head, 512)])
    send_lows(0)
    gains_y = [net.together([(r.gains_own, r.gains_y.at[i], ys[i]) for i in range(3)])]
    row = r.row[...].reshape(1024, 1024)
    low_columns = dot_tn(row, r.lows[...].reshape(1024, 512)).astype(BF16)
    r.own_query[...] = low_columns[:, :256].reshape(4, 2, 2, 4, 16, 256)
    first_query = ring_start(lambda t: r.own_query.at[:, :, :, t[1]], r.far_query, r.all_query, ys)
    r.own_kv[...] = low_columns[:, 256:].reshape(4, 2, 2, 4, 16, 256)
    first_kv = [net.together([(r.own_kv.at[:, t[3], :, :, :, aligned(t[0], 128)], r.all_kv.at[i], t) for i, t in enumerate(xs)])]
    send_lows(1)
    wait_all(gate_landings)
    load_gate = net.keep(r.gate_all, r.wd.at[:, pl.ds(384, 384)])
    chain_wait(down_chain)
    rows = aligned(x_of(down_chain.far), 256)
    load_down = net.keep(r.down_all.at[rows, :], r.wgu.at[rows, pl.ds(4096, 1024)])
    wait_all([near_down, load_down, load_activated])
    product = dot_tn(r.wgu[:, 4096:5120], r.wd[:, 768:1152])
    r.own_down[...] = product.astype(BF16).reshape(4, 2, 2, 4, 16, 384)
    first_down = ring_start(lambda t: r.own_down.at[:, :, :, t[1]], r.far_down, r.all_down, ys)
    load_gate.wait()
    r.own_gate[...] = by_rows(dot_tn(r.wo[:, :1024], r.wd[:, 384:768]))
    first_gate = [net.together([(r.own_gate.at[t[2]], r.all_gate.at[i], t) for i, t in enumerate(zs)])]
    chain_forward(branch_chain)
    ring_middle(first_query, lambda t: r.own_query[:, :, :, t[1]], r.mid_query)
    ring_middle(first_down, lambda t: r.own_down[:, :, :, t[1]], r.mid_down)
    chain_wait(branch_chain)
    output_columns = dot_tn(r.branch_row[...].reshape(1024, 1024), r.attn_heads[...].reshape(1024, 256))
    r.own_output[...] = output_columns.astype(BF16).reshape(4, 2, 2, 4, 16, 256)
    first_output = ring_start(lambda t: r.own_output.at[:, :, :, t[1]], r.far_output, r.all_output, ys)
    r.next_up[...] = total(r.own_up[:, at[3], :, at[0]], r.all_up, first_up).astype(BF16)
    then_up = [net.together([(r.next_up.at[t[2]], r.then_up.at[i], t) for i, t in enumerate(zs)])]
    r.gains_next[...] = total(r.gains_own[...], r.gains_y, gains_y)
    gains_x = [net.together([(r.gains_next, r.gains_x.at[i], xs[i]) for i in range(3)])]
    r.next_query[...] = total(r.own_query[:, :, :, at[1]], r.all_query, first_query).astype(BF16)
    then_query = [net.together([(r.next_query.at[:, t[3]], r.then_query.at[i], t) for i, t in enumerate(xs)])]
    r.next_down[...] = total(r.own_down[:, :, :, at[1]], r.all_down, first_down).astype(BF16)
    then_down = [net.together([(r.next_down.at[t[2]], r.then_down.at[i], t) for i, t in enumerate(zs)])]
    r.next_kv[...] = total(r.own_kv[:, at[3], :, :, :, aligned(at[0], 128)], r.all_kv, first_kv).astype(BF16)
    then_kv = [net.together([(r.next_kv.at[:, :, t[1]], r.then_kv.at[i], t) for i, t in enumerate(ys)])]
    ring_middle(first_output, lambda t: r.own_output[:, :, :, t[1]], r.mid_output)
    send_lows(3)
    r.next_gate[...] = total(r.own_gate[at[2]], r.all_gate, first_gate).astype(BF16)
    then_gate = [net.together([(r.next_gate.at[t[3], :, t[0]], r.then_gate.at[i], t) for i, t in enumerate(xs)])]
    r.gains_last[...] = total(r.gains_next[...], r.gains_x, gains_x)
    gains_zc = [net.together([(r.gains_last, r.gains_zc.at[i], t) for i, t in enumerate(zc)])]
    r.done_up[...] = total(r.next_up[z], r.then_up, then_up).astype(BF16)
    second_up = replicate(
        both_cores(r.done_up),
        lambda who: r.up_grad.at[aligned(who[0], 32), aligned(who[1] * 2 + who[4], 384)],
        lambda who: r.up_grad.at[aligned(who[0], 32), aligned(who[1], 768)],
        True,
    )
    r.done_kv[...] = total(r.next_kv[:, :, y], r.then_kv, then_kv).astype(BF16)
    got_kv = to_heads(r.done_kv, r.got_kv, 128)
    r.done_down[...] = total(r.next_down[z], r.then_down, then_down).astype(BF16)
    second_down = replicate(
        four_devices(r.done_down),
        lambda who: r.down_grad.at[aligned(who[1], 16), aligned((who[0] * 2 + who[3]) * 2 + who[4], 384)],
        lambda who: r.down_grad.at[aligned(who[1], 16), aligned(who[0], 1536)],
        False,
    )
    r.next_output[...] = total(r.own_output[:, :, :, at[1]], r.all_output, first_output).astype(BF16)
    then_output = [net.together([(r.next_output.at[:, t[3]], r.then_output.at[i], t) for i, t in enumerate(xs)])]
    r.done_query[...] = total(r.next_query[:, xl], r.then_query, then_query).astype(BF16)
    got_query = to_heads(r.done_query, r.got_query, 256)
    send_lows(2)
    r.done_gate[...] = total(r.next_gate[xl, :, xh], r.then_gate, then_gate).astype(BF16)
    second_gate = replicate(
        both_cores(r.done_gate),
        lambda who: r.gate_grad.at[aligned(who[0], 32), aligned(who[1] * 2 + who[4], 384)],
        lambda who: r.gate_grad.at[aligned(who[0], 32), aligned(who[1], 768)],
        True,
    )
    wait_all(got_kv)
    second_kv = replicate(
        one_device(r.got_kv),
        lambda who: r.key_value_grad.at[who[0], aligned(who[1], 16), :],
        lambda who: r.key_value_grad.at[who[0], aligned(who[1], 16), :],
        False,
    )
    second_down()
    second_up()
    r.done_output[...] = total(r.next_output[:, xl], r.then_output, then_output).astype(BF16)
    got_output = to_heads(r.done_output, r.got_output, 256)
    wait_all(got_query)
    along_y(r.got_query, r.query_weight_grad.at[aligned(y, 16), :])
    second_gate()
    second_kv()
    head_loads.wait()
    low_own.wait()
    for dz in ORDER:
        low_landings[dz].wait()

    @pl.loop(0, 2)
    def _(part):
        rows = aligned(part, 512)
        r.down[:, rows] = dot_nt(r.wgu[rows, pl.ds(0, 4096)], r.low_tokens[...].reshape(128, 4096)).T

    input_grad = (r.residual_grad[...] + r.down[...]).reshape(2, 64, 1024)
    r.input_grad[...] = input_grad
    r.grad_low[...] = input_grad.astype(BF16)
    swap(r.input_grad, r.grad_low, r.grad_own, r.grad_got)
    wait_all(got_output)
    along_y(r.got_output, r.output_weight_grad.at[aligned(y, 16), :])
    wait_all(gains_zc)
    gains = r.gains_last[...]
    for i in range(7):
        gains = gains + r.gains_zc[i]
    r.gains_final[...] = gains
    net.keep(r.gains_final, r.gains)
    assert (net.next_send, net.next_keep) == (SENDS, KEEPS), (net.next_send, net.next_keep)
    net.drain()


def layer(*arrays):
    return pl.pallas_call(
        layer_kernel,
        out_shape=[shape(*item) for item in OUTPUTS.values()],
        in_specs=[pl.BlockSpec(memory_space=pl.ANY)] * len(INPUTS),
        out_specs=[pl.BlockSpec(memory_space=pl.ANY)] * len(OUTPUTS),
        scratch_shapes=[pltpu.VMEM(*item) for item in [*SCRATCH.values(), *SMALL.values()]]
        + [
            pltpu.SemaphoreType.DMA((-(-SENDS // BUCKET),)),
            pltpu.SemaphoreType.DMA((SENDS,)),
            pltpu.SemaphoreType.DMA((KEEPS,)),
        ],
        compiler_params=pltpu.CompilerParams(
            collective_id=0, has_side_effects=True, vmem_limit_bytes=VMEM_LIMIT
        ),
        name="layer",
    )(*arrays)


def widen_kernel(
    out_own, grad_own, out_got, grad_got, query, key_value, output, gate, up, down, gains,
    out_to, grad_to, query_to, key_to, value_to, output_to, gate_to, up_to, down_to,
    query_gain, key_gain, attention_gain, feedforward_gain,
):
    lower = (lax.axis_index("seq") // 2) % 2 == 0
    for own, got, to in ((out_own, out_got, out_to), (grad_own, grad_got, grad_to)):
        mine, other = own[...], got[...].astype(F32)
        to[0] = jnp.where(lower, mine, other)
        to[1] = jnp.where(lower, other, mine)
    query_to[...] = query[...].astype(F32)
    key_to[...] = key_value[0].astype(F32)
    value_to[...] = key_value[1].astype(F32)
    output_to[...] = output[...].astype(F32)
    gate_to[...] = gate[...].astype(F32)
    up_to[...] = up[...].astype(F32)
    down_to[...] = down[...].astype(F32)
    attention_gain[...] = gains[0:8, :]
    feedforward_gain[...] = gains[8:16, :]
    query_gain[...] = gains[16:17, :]
    key_gain[...] = gains[17:18, :]


def widen(*arrays):
    steps = 2
    rows = 64 // steps

    def flat(columns):
        return pl.BlockSpec((rows, columns), lambda i: (i, 0))

    def paired(columns):
        return pl.BlockSpec((2, rows, columns), lambda i: (0, i, 0))

    def whole(count):
        return pl.BlockSpec((count, 128), lambda i: (0, 0))

    return pl.pallas_call(
        widen_kernel,
        grid=(steps,),
        out_shape=[shape((2, 64, 1024), F32)] * 2
        + [shape((64, n), F32) for n in (2048, 1024, 1024, 2048, 3072, 3072, 3072)]
        + [shape((n, 128), F32) for n in (1, 1, 8, 8)],
        in_specs=[flat(1024)] * 4
        + [flat(2048), paired(1024), flat(2048)]
        + [flat(3072)] * 3
        + [whole(24)],
        out_specs=[paired(1024)] * 2
        + [flat(n) for n in (2048, 1024, 1024, 2048, 3072, 3072, 3072)]
        + [whole(n) for n in (1, 1, 8, 8)],
        name="widen",
    )(*arrays)


VMEM_LIMIT = 63 * 2**20


def per_device(
    hidden_in,
    query_weight,
    key_weight,
    value_weight,
    output_weight,
    gate_weight,
    up_weight,
    down_weight,
    query_gain,
    key_gain,
    attention_gain,
    feedforward_gain,
    document_ids,
    cotangent,
):
    results = layer(
        hidden_in, cotangent,
        query_weight, key_weight, value_weight, output_weight, gate_weight, up_weight, down_weight,
        document_ids, *rope_tables(),
        query_gain[None, :], key_gain[None, :], attention_gain[None, :], feedforward_gain[None, :],
    )[:11]
    results = widen(*results)
    return tuple(results[:9]) + (results[9][0], results[10][0], results[11].reshape(1024), results[12].reshape(1024))


def solution(mesh):
    tokens = P("rows", "seq", None)
    split = P("seq", None)
    return jax.shard_map(
        per_device,
        mesh=mesh,
        in_specs=(tokens,) + (P(),) * 11 + (P("rows", "seq"), tokens),
        out_specs=(tokens, tokens) + (split,) * 7 + (P(),) * 4,
        check_vma=False,
    )
```

```python
import functools

import jax
import jax.numpy as jnp
import numpy as np
from jax import lax
from jax.experimental import pallas as pl
from jax.experimental.pallas import tpu as pltpu
from jax.sharding import PartitionSpec as P

HD = 128
EPSILON = 1e-06
ROPE_BASE = 1000000.0
MASKED = -1e30
LOG2E = 1.4426950408889634
SCALE = HD ** (-0.5)
MESH = pl.DeviceIdType.MESH
F32 = jnp.float32
BF16 = jnp.bfloat16

YS = 4
ZS = 4
XS = 4


def place():
    rows, seq = lax.axis_index("rows"), lax.axis_index("seq")
    return (rows // YS, rows % YS, seq // 4, (seq // 2) % 2, seq % 2)


def device(xh, y, z, xl, c):
    return (xh * YS + y, z * 4 + xl * 2 + c)


def shifted(at, dx=0, dy=0, dz=0, dc=0, flip_xl=0, flip_xh=0):
    xh, y, z, xl, c = at
    if dx:
        x = (xh * 2 + xl + dx) % XS
        xh, xl = x // 2, x % 2
    if flip_xl:
        xl = 1 - xl
    if flip_xh:
        xh = 1 - xh
    if dc:
        c = 1 - c
    return (xh, (y + dy) % YS, (z + dz) % ZS, xl, c)


class Group:
    def __init__(self, net, index):
        self.net, self.index, self.sender = net, index, sum(index >= start for start in BUCKETS)
        self.units, self.here = 0, False

    def add(self, src, dst, target, start=True):
        copy = self.net.remote(src, dst, target, self.sender, self.index)
        if start:
            copy.start()
        self.units += units_of(dst)
        return self

    def wait(self):
        if not self.here:
            self.net.sized(self.units, self.net.recv_sems.at[self.index]).wait()
            self.here = True


class LocalGroup:
    def __init__(self, net, index):
        self.net, self.index = net, index
        self.units, self.here, self.only = 0, False, None

    def add(self, src, dst):
        copy = pltpu.make_async_copy(src, dst, self.net.local_sems.at[self.index])
        copy.start()
        self.only = None if self.units else copy
        self.units += units_of(dst)
        return self

    def wait(self):
        if not self.here:
            if self.only is None:
                self.net.sized(self.units, self.net.local_sems.at[self.index]).wait()
            else:
                self.only.wait()
            self.here = True


def units_of(ref):
    return int(np.prod(ref.shape)) * (1 if ref.dtype == BF16 else 2)


class Net:
    def __init__(self, send_sems, recv_sems, local_sems, measures):
        self.send_sems, self.recv_sems, self.local_sems = send_sems, recv_sems, local_sems
        self.measures = measures
        self.groups, self.locals, self.next_send, self.next_keep = [], [], 0, 0

    def sized(self, units, sem):
        for ref in self.measures:
            columns = ref.shape[-1]
            while columns >= 128:
                rows = units // columns
                if rows * columns == units and rows % 16 == 0 and rows <= ref.shape[0] and columns % 128 == 0:
                    view = ref.at[pl.ds(0, rows), pl.ds(0, columns)]
                    return pltpu.make_async_copy(view, view, sem)
                columns -= 128
        raise ValueError(units)

    def barrier(self, targets):
        barrier = pltpu.get_barrier_semaphore()
        for target in targets:
            pl.semaphore_signal(barrier, inc=1, device_id=device(*target), device_id_type=MESH)
        pl.semaphore_wait(barrier, len(targets))

    def remote(self, src, dst, target, sender, i):
        return pltpu.make_async_remote_copy(
            src_ref=src,
            dst_ref=dst,
            send_sem=self.send_sems.at[sender],
            recv_sem=self.recv_sems.at[i],
            device_id=device(*target),
            device_id_type=MESH,
        )

    def group(self):
        self.groups.append(Group(self, self.next_send))
        self.next_send += 1
        return self.groups[-1]

    def local_group(self):
        self.locals.append(LocalGroup(self, self.next_keep))
        self.next_keep += 1
        return self.locals[-1]

    def send(self, src, dst, target):
        return self.group().add(src, dst, target)

    def together(self, items):
        result = self.group()
        for src, dst, target in items:
            result.add(src, dst, target)
        return result

    def keep(self, src, dst):
        return self.local_group().add(src, dst)

    def drain(self):
        for group in self.locals:
            group.wait()
        sent = {}
        for group in self.groups:
            group.wait()
            sent[group.sender] = sent.get(group.sender, 0) + group.units
        for sender, units in sent.items():
            self.sized(units, self.send_sems.at[sender]).wait()


def shape(dims, dtype=BF16):
    return jax.ShapeDtypeStruct(dims, dtype)


ZC = [(dz, dc) for dz in range(ZS) for dc in range(2) if (dz, dc) != (0, 0)]
ORDER = (0, 1, 3, 2)
BLOCK = 256
BUCKETS = (53,)
SENDS = 93
KEEPS = 36


def rope_tables():
    half = HD // 2
    frequency = ROPE_BASE ** (-(np.arange(half, dtype=np.float64) * 2.0 / HD))
    angles = np.arange(1024, dtype=np.float64)[:, None] * frequency[None, :]
    cosines = np.concatenate([np.cos(angles)] * 2, axis=1)
    sines = np.concatenate([-np.sin(angles), np.sin(angles)], axis=1)
    return (cosines.astype(np.float32), sines.astype(np.float32))


def dot_nn(left, right):
    return jnp.dot(left, right, preferred_element_type=F32)


def dot_nt(left, right):
    return lax.dot_general(left, right, (((1,), (1,)), ((), ())), preferred_element_type=F32)


def dot_tn(left, right):
    return lax.dot_general(left, right, (((0,), (0,)), ((), ())), preferred_element_type=F32)


def normalize(vector, scales):
    inverse = lax.rsqrt(jnp.mean(vector * vector, axis=-1, keepdims=True) + EPSILON)
    return (vector * inverse * scales, inverse)


def norm_back(gradient, vector, inverse, scales):
    normed = vector * inverse
    scales_grad = jnp.sum(gradient * normed, axis=0, keepdims=True)
    scaled = gradient * scales
    vector_grad = inverse * (scaled - normed * jnp.mean(scaled * normed, axis=-1, keepdims=True))
    return (vector_grad, scales_grad)


def aligned(index, width):
    return pl.ds(pl.multiple_of(index * width, width), width)


class Refs:
    pass


INPUTS = dict(
    hidden=0,
    cotangent=0,
    query_weight=0,
    key_weight=0,
    value_weight=0,
    output_weight=0,
    gate_weight=0,
    up_weight=0,
    down_weight=0,
    document_ids_in=((2, 64), jnp.int32),
    cosines_in=((1024, 128), F32),
    sines_in=((1024, 128), F32),
    query_gain_in=((1, 128), F32),
    key_gain_in=((1, 128), F32),
    attention_gain_in=((1, 1024), F32),
    feedforward_gain_in=((1, 1024), F32),
)
SMALL = {name[:-3]: item for name, item in INPUTS.items() if item}
OUTPUTS = dict(
    out_own=((64, 1024), F32),
    grad_own=((64, 1024), F32),
    out_got=((64, 1024), BF16),
    grad_got=((64, 1024), BF16),
    query_weight_grad=((64, 2048), BF16),
    key_value_grad=((2, 64, 1024), BF16),
    output_weight_grad=((64, 2048), BF16),
    gate_grad=((64, 3072), BF16),
    up_grad=((64, 3072), BF16),
    down_grad=((64, 3072), BF16),
    gains=((24, 128), F32),
    residual_y=((1024, 1024), BF16),
    gate_all=((1024, 384), BF16),
    up_all=((1024, 384), BF16),
    down_all=((1024, 1024), BF16),
    activated_all=((1024, 384), BF16),
)
SCRATCH = dict(
    head_weights=((1024, 512), BF16),
    wo=((1024, 2048), BF16),
    wgu=((1024, 6144), BF16),
    wd=((1024, 3072), BF16),
    row=((4, 2, 2, 64, 1024), BF16),
    upstream=((2, 64, 1024), BF16),
    documents=((2, 16, 128), F32),
    row_documents=((16, 16, 128), F32),
    document_column=((1024, 128), F32),
    raw=((1024, 384), F32),
    inverses=((1024, 3), F32),
    queries=((1024, 256), BF16),
    keys=((1024, 128), BF16),
    values=((1024, 128), BF16),
    attended=((1024, 256), F32),
    attn_heads=((4, 2, 2, 64, 256), BF16),
    log_total=((2, 1024, 1), F32),
    attn_tokens=((2, 64, 2048), BF16),
    branch=((128, 1024), F32),
    down=((128, 1024), F32),
    residual=((128, 1024), F32),
    residual_low=((128, 1024), BF16),
    gate_factor=((128, 3072), F32),
    up_factor=((128, 3072), F32),
    activated=((128, 3072), BF16),
    layer_output=((2, 64, 1024), F32),
    down_low=((128, 1024), BF16),
    gate_up_low=((128, 6144), BF16),
    residual_grad=((128, 1024), F32),
    branch_low=((2, 64, 1024), BF16),
    attn_grad=((2, 64, 2048), BF16),
    attn_grad_row=((4, 2, 2, 64, 256), BF16),
    branch_row=((4, 2, 2, 64, 1024), BF16),
    lows=((4, 2, 2, 64, 512), BF16),
    key_sum=((1024, 128), F32),
    value_sum=((1024, 128), F32),
    low_tokens=((2, 64, 4096), BF16),
    input_grad=((2, 64, 1024), F32),
    out_low=((2, 64, 1024), BF16),
    grad_low=((2, 64, 1024), BF16),
    own_gate=((4, 2, 2, 2, 32, 384), BF16),
    all_gate=((3, 2, 2, 2, 32, 384), BF16),
    next_gate=((2, 2, 2, 32, 384), BF16),
    then_gate=((3, 2, 32, 384), BF16),
    done_gate=((2, 32, 384), BF16),
    own_query=((4, 2, 2, 4, 16, 256), BF16),
    all_query=((2, 4, 2, 2, 16, 256), BF16),
    far_query=((2, 2, 2, 2, 16, 256), BF16),
    mid_query=((2, 2, 2, 2, 16, 256), BF16),
    next_query=((4, 2, 2, 16, 256), BF16),
    then_query=((3, 4, 2, 16, 256), BF16),
    done_query=((4, 2, 16, 256), BF16),
    got_query=((16, 2048), BF16),
    own_kv=((4, 2, 2, 4, 16, 256), BF16),
    all_kv=((3, 4, 2, 4, 16, 128), BF16),
    next_kv=((4, 2, 4, 16, 128), BF16),
    then_kv=((3, 4, 2, 16, 128), BF16),
    done_kv=((4, 2, 16, 128), BF16),
    got_kv=((16, 1024), BF16),
    own_output=((4, 2, 2, 4, 16, 256), BF16),
    all_output=((2, 4, 2, 2, 16, 256), BF16),
    far_output=((2, 2, 2, 2, 16, 256), BF16),
    mid_output=((2, 2, 2, 2, 16, 256), BF16),
    next_output=((4, 2, 2, 16, 256), BF16),
    then_output=((3, 4, 2, 16, 256), BF16),
    done_output=((4, 2, 16, 256), BF16),
    got_output=((16, 2048), BF16),
    own_up=((4, 2, 2, 2, 32, 384), BF16),
    all_up=((3, 4, 2, 32, 384), BF16),
    next_up=((4, 2, 32, 384), BF16),
    then_up=((3, 2, 32, 384), BF16),
    done_up=((2, 32, 384), BF16),
    own_down=((4, 2, 2, 4, 16, 384), BF16),
    all_down=((2, 4, 2, 2, 16, 384), BF16),
    far_down=((2, 2, 2, 2, 16, 384), BF16),
    mid_down=((2, 2, 2, 2, 16, 384), BF16),
    next_down=((4, 2, 2, 16, 384), BF16),
    then_down=((3, 2, 2, 16, 384), BF16),
    done_down=((2, 2, 16, 384), BF16),
    gains_own=((24, 128), F32),
    gains_next=((24, 128), F32),
    gains_last=((24, 128), F32),
    gains_final=((24, 128), F32),
    gains_y=((3, 24, 128), F32),
    gains_x=((3, 24, 128), F32),
    gains_zc=((7, 24, 128), F32),
)


def layer_kernel(*refs):
    names = [*INPUTS, *OUTPUTS, *SCRATCH, *SMALL]
    r = Refs()
    for name, ref in zip(names, refs):
        setattr(r, name, ref)
    net = Net(*refs[len(names) :], (r.wd, r.wgu))
    at = place()
    xh, y, z, xl, c = at
    x = xh * 2 + xl
    head = z * 2 + c
    sibling = shifted(at, dc=1)
    partner = shifted(at, flip_xl=1)
    seq_others = [
        shifted(at, dz=dz, dc=dc, flip_xl=dx)
        for dz in range(ZS)
        for dx in range(2)
        for dc in range(2)
        if (dz, dx, dc) != (0, 0, 0)
    ]
    zc = [shifted(at, dz=dz, dc=dc) for dz, dc in ZC]
    yc = [shifted(at, dy=dy, dc=dc) for dy, dc in ZC]
    xc = [shifted(at, dx=dx, dc=dc) for dx, dc in ZC]
    ys = [shifted(at, dy=step) for step in range(1, 4)]
    xs = [shifted(at, dx=step) for step in range(1, 4)]
    zs = [shifted(at, dz=step) for step in range(1, 4)]
    replicas = [
        shifted(at, dy=dy, flip_xh=dx) for dy in range(YS) for dx in range(2) if (dy, dx) != (0, 0)
    ]

    crossed = [shifted(at, dy=dy, dc=dc, flip_xl=1) for dy in range(1, YS) for dc in range(2)]
    barrier_targets = list(seq_others) + yc[1:] + xc[1:] + replicas + crossed
    documents_load = net.keep(r.document_ids_in, r.document_ids)
    net.barrier(barrier_targets)
    up_z, down_z = shifted(at, dz=1), shifted(at, dz=-1)
    parts = [pl.ds(0, 32), pl.ds(32, 32)]
    arrived = {(dz, dx): net.group() for dz, dx in ((1, 0), (3, 0), (1, 1))}
    from_partner = [
        net.send(r.hidden.at[1 - xl, part], r.row.at[z, xl, c, part], partner) for part in parts
    ]
    for dz, target in ((1, up_z), (3, down_z)):
        arrived[dz, 0].add(r.hidden.at[xl], r.row.at[z, xl, c], target)
    own_block = net.keep(r.hidden.at[xl], r.row.at[z, xl, c])
    documents_load.wait()
    own_documents = r.document_ids[...].astype(F32)
    own_documents = jnp.concatenate([own_documents, own_documents], axis=1)
    for i in range(2):
        r.documents[i] = jnp.broadcast_to(own_documents[i : i + 1, :], (16, 128))
    document_slot = r.row_documents.at[z * 4 + xl * 2 + c]
    document_landings = net.together([(r.documents.at[t[3]], document_slot, t) for t in seq_others])
    document_landings_own = net.keep(r.documents.at[xl], document_slot)
    upstream_landing = net.send(r.cotangent.at[1 - xl], r.upstream.at[xl], partner)
    upstream_own = net.keep(r.cotangent.at[xl], r.upstream.at[xl])

    forwarded = {}

    def block_of(dz, dx):
        return r.row.at[(z - dz) % ZS, (xl + dx) % 2, c]

    def to_sibling(dz, dx):
        forwarded[dz, dx] = net.send(block_of(dz, dx), block_of(dz, dx), sibling)

    def project(dz):
        source = (z - dz) % ZS
        for dx in range(2):
            forwarded[dz, dx].wait()
        rows = aligned(source, BLOCK)
        product = dot_nn(r.row[source].reshape(BLOCK, 1024), r.head_weights[...])
        r.raw[rows, :] = product[:, :384]
        r.values[rows, :] = product[:, 384:].astype(BF16)
        for part in range(3):
            gain = r.query_gain[...] if part < 2 else r.key_gain[...]
            normed, inverse = normalize(product[:, part * HD : (part + 1) * HD], gain)
            r.inverses[rows, part : part + 1] = inverse
            turned = normed * r.cosines[rows, :] + pltpu.roll(normed, 64, 1) * r.sines[rows, :]
            if part < 2:
                r.queries[rows, part * HD : (part + 1) * HD] = turned.astype(BF16)
            else:
                r.keys[rows, :] = turned.astype(BF16)

    loads = net.local_group()
    for ref, start, width in (
        (r.query_weight, 0, 256),
        (r.key_weight, 256, 128),
        (r.value_weight, 384, 128),
    ):
        loads.add(ref.at[:, aligned(head, width)], r.head_weights.at[:, pl.ds(start, width)])
    small_loads = net.local_group()
    small_loads.add(r.cosines_in, r.cosines).add(r.sines_in, r.sines)
    gain_loads = [
        net.keep(r.query_gain_in, r.query_gain),
        net.keep(r.key_gain_in, r.key_gain),
        net.keep(r.attention_gain_in, r.attention_gain),
        net.keep(r.feedforward_gain_in, r.feedforward_gain),
    ]
    load_wo = net.keep(r.output_weight, r.wo)
    load_wgu = net.keep(r.gate_weight, r.wgu.at[:, pl.ds(0, 3072)])
    load_wgu.add(r.up_weight, r.wgu.at[:, pl.ds(3072, 3072)])
    load_wd = net.keep(r.down_weight, r.wd)

    loads.wait()
    small_loads.wait()
    for load in gain_loads:
        load.wait()
    own_block.wait()
    to_sibling(0, 0)
    below = [net.group() for _ in parts]
    for landing, part, second in zip(from_partner, parts, below):
        landing.wait()
        piece = r.row.at[z, 1 - xl, c, part]
        arrived[1, 1].add(piece, piece, up_z)
        second.add(piece, piece, down_z)
    to_sibling(0, 1)
    arrived[1, 0].wait()
    arrived[2, 0] = net.send(block_of(1, 0), block_of(1, 0), up_z)
    to_sibling(1, 0)
    arrived[3, 0].wait()
    to_sibling(3, 0)
    arrived[2, 1] = net.group()
    for landing, part in zip(below, parts):
        landing.wait()
        piece = r.row.at[(z + 1) % ZS, 1 - xl, c, part]
        arrived[2, 1].add(piece, piece, down_z)
    to_sibling(3, 1)
    arrived[1, 1].wait()
    to_sibling(1, 1)
    project(0)
    project(1)
    project(3)
    for dx in range(2):
        arrived[2, dx].wait()
        to_sibling(2, dx)
    document_landings.wait()
    document_landings_own.wait()
    lane = lax.broadcasted_iota(jnp.int32, (1, 128), 1)
    pieces = []
    for block in range(8):
        even = r.row_documents[2 * block, 0:1, :]
        odd = r.row_documents[2 * block + 1, 0:1, :]
        piece = jnp.where(lane < 64, even, odd)
        pieces.append(piece)
        r.document_column[block * 128 : (block + 1) * 128, :] = jnp.broadcast_to(piece, (128, 128)).T
    document_row = jnp.concatenate(pieces, axis=1)
    project(2)

    def visible_in(block):
        count = (block + 1) * BLOCK
        rows = slice(block * BLOCK, count)
        same = r.document_column[rows, 0:1] == document_row[:, :count]
        row_at = block * BLOCK + lax.broadcasted_iota(jnp.int32, (BLOCK, count), 0)
        column_at = lax.broadcasted_iota(jnp.int32, (BLOCK, count), 1)
        return same & (row_at >= column_at)

    attn_landings = {dz: [] for dz in ORDER}
    by_source = [[net.group() for _ in ORDER] for _ in range(2)]
    sender = by_source[0][0].sender
    for groups in by_source:
        for group in groups:
            group.sender = sender
    by_core = [net.local_group() for _ in range(2)]
    first_send, first_keep = by_source[0][0].index, by_core[0].index

    def head_copies(h):
        columns = aligned(h, HD)
        slot = r.attn_tokens.at[:, :, aligned(head * 2 + h, HD)]
        copies = [
            net.remote(r.attn_heads.at[t[2], :, t[4], :, columns], slot, t, sender, first_send + h * 4 + dz)
            for (dz, _), t in zip(ZC, zc)
        ]
        own = pltpu.make_async_copy(
            r.attn_heads.at[z, :, c, :, columns], slot, net.local_sems.at[first_keep + h]
        )
        return copies + [own]

    @pl.loop(0, 2)
    def _(h):
        columns = aligned(h, HD)
        for block in range(4):
            rows = slice(block * BLOCK, (block + 1) * BLOCK)
            count = (block + 1) * BLOCK
            scores = dot_nt(r.queries[rows, columns], r.keys[:count, :])
            scores = jnp.where(visible_in(block), scores * (SCALE * LOG2E), MASKED)
            top = jnp.max(scores, axis=-1, keepdims=True)
            soft = jnp.exp2(scores - top)
            total = jnp.sum(soft, axis=-1, keepdims=True)
            mixed = dot_nn(soft.astype(BF16), r.values[:count, :]) / total
            r.attended[rows, columns] = mixed
            r.attn_heads[block, :, :, :, columns] = mixed.astype(BF16).reshape(2, 2, 64, HD)
            r.log_total[h, rows, :] = top + jnp.log2(total)
        for copy in head_copies(h):
            copy.start()

    for h in range(2):
        by_core[h].units = 2 * 64 * HD
        attn_landings[0].append(by_core[h])
        for dz in ORDER:
            by_source[h][dz].units = 2 * 64 * HD * (1 if dz == 0 else 2)
            attn_landings[dz].append(by_source[h][dz])

    def chain(shift, src, slot_of, half_of):
        ahead, behind = shift(1), shift(-1)
        state = Refs()
        state.slot_of, state.half_of, state.ahead, state.behind = slot_of, half_of, ahead, behind
        state.far = shift(2)
        state.from_behind = net.send(src, slot_of(at), ahead)
        state.from_ahead = net.send(src, slot_of(at), behind)
        state.near = [net.send(src, slot_of(at), sibling), net.keep(src, slot_of(at))]
        return state

    def chain_middle(state):
        half_of, behind, ahead = state.half_of, state.behind, state.ahead
        state.from_behind.wait()
        state.beyond = [net.send(half_of(behind, 0), half_of(behind, 0), ahead)]
        state.from_ahead.wait()
        state.beyond.append(net.send(half_of(ahead, 1), half_of(ahead, 1), behind))
        for source in (behind, ahead):
            state.near.append(net.send(state.slot_of(source), state.slot_of(source), sibling))

    def chain_forward(state):
        for landing in state.beyond:
            landing.wait()
        state.last = net.send(state.slot_of(state.far), state.slot_of(state.far), sibling)

    def chain_near(state):
        for item in state.near:
            item.wait()

    def chain_wait(state):
        chain_near(state)
        state.last.wait()

    load_wo.wait()
    turned = jnp.zeros((1024, 128), F32)
    for dz in ORDER:
        for landing in attn_landings[dz]:
            landing.wait()
        columns = aligned((z - dz) % ZS, 512)
        turned = turned + dot_nt(r.wo[:, columns], r.attn_tokens[:, :, columns].reshape(128, 512))
    branch = turned.T
    r.branch[...] = branch
    branch_normed, branch_inverse = normalize(branch, r.attention_gain[...])
    residual = r.row[z, :, c].reshape(128, 1024).astype(F32) + branch_normed
    r.residual[...] = residual
    r.residual_low[...] = residual.astype(BF16)
    def rows_of(group, index):
        def slot_of(who):
            return group.at[aligned(index(who) * 2 + who[4], 128), :]

        def half_of(who, half):
            return group.at[aligned((index(who) * 2 + who[4]) * 2 + half, 64), :]

        return (slot_of, half_of)

    def y_of(who):
        return who[1]

    def x_of(who):
        return who[0] * 2 + who[3]

    residual_chain = chain(lambda step: shifted(at, dy=step), r.residual_low, *rows_of(r.residual_y, y_of))
    load_wgu.wait()

    @pl.loop(0, 3)
    def _(tile):
        columns, up_columns = aligned(tile, 1024), aligned(tile + 3, 1024)
        gate = dot_nn(r.residual_low[...], r.wgu[:, columns])
        up = dot_nn(r.residual_low[...], r.wgu[:, up_columns])
        sigmoid_gate = lax.logistic(gate)
        silu = gate * sigmoid_gate
        r.activated[:, columns] = (silu * up).astype(BF16)
        r.up_factor[:, columns] = silu
        r.gate_factor[:, columns] = up * sigmoid_gate * (1.0 + gate * (1.0 - sigmoid_gate))

    def to_columns(src, first, group, index, targets):
        slot = group.at[aligned(index(at) * 2 + c, 128), :]
        items = net.together(
            [(src.at[:, aligned(first + index(t) * 2 + t[4], 384)], slot, t) for t in targets]
        )
        return [items, net.keep(src.at[:, aligned(first + index(at) * 2 + c, 384)], slot)]

    activated_landings = to_columns(r.activated, 0, r.activated_all, x_of, xc)
    load_wd.wait()

    @pl.loop(0, 2)
    def _(part):
        rows = aligned(part, 512)
        r.down[:, rows] = dot_nt(r.wd[rows, :], r.activated[...]).T

    down = r.down[...]
    upstream_landing.wait()
    upstream_own.wait()
    down_normed, down_inverse = normalize(down, r.feedforward_gain[...])
    layer_output = (r.residual[...] + down_normed).reshape(2, 64, 1024)
    r.layer_output[...] = layer_output
    r.out_low[...] = layer_output.astype(BF16)
    upstream = r.upstream[...].reshape(128, 1024).astype(F32)
    down_grad, feedforward_gain_grad = norm_back(upstream, down, down_inverse, r.feedforward_gain[...])
    r.down_low[...] = down_grad.astype(BF16)
    down_chain = chain(lambda step: shifted(at, dx=step), r.down_low, *rows_of(r.down_all, x_of))

    @pl.loop(0, 3)
    def _(tile):
        columns, up_columns = aligned(tile, 1024), aligned(tile + 3, 1024)
        act_grad = dot_nn(r.down_low[...], r.wd[:, columns])
        r.gate_up_low[:, columns] = (act_grad * r.gate_factor[:, columns]).astype(BF16)
        r.gate_up_low[:, up_columns] = (act_grad * r.up_factor[:, columns]).astype(BF16)

    up_landings = to_columns(r.gate_up_low, 8, r.up_all, y_of, yc)

    @pl.loop(0, 2)
    def _(part):
        rows = aligned(part, 512)
        r.residual_grad[:, rows] = dot_nt(r.wgu[rows, :], r.gate_up_low[...]).T

    chain_middle(residual_chain)
    residual_grad = r.upstream[...].reshape(128, 1024).astype(F32) + r.residual_grad[...]
    r.residual_grad[...] = residual_grad
    branch_grad, attention_gain_grad = norm_back(
        residual_grad, r.branch[...], branch_inverse, r.attention_gain[...]
    )
    for i in range(8):
        r.gains_own[i : i + 1, :] = attention_gain_grad[:, i * 128 : (i + 1) * 128]
        r.gains_own[8 + i : 9 + i, :] = feedforward_gain_grad[:, i * 128 : (i + 1) * 128]
    branch_low = branch_grad.astype(BF16)
    r.branch_low[...] = branch_low.reshape(2, 64, 1024)
    attn_grad_landings = net.group()
    for dz in (2, 1, 3, 0):
        columns = aligned((z + dz) % ZS, 512)
        product = dot_nn(r.branch_low[...].reshape(128, 1024), r.wo[:, columns])
        r.attn_grad[:, :, columns] = product.astype(BF16).reshape(2, 64, 512)
        for (step, _), t in zip(ZC, zc):
            if step == dz:
                attn_grad_landings.add(
                    r.attn_grad.at[:, :, aligned(t[2] * 2 + t[4], 256)], r.attn_grad_row.at[z, :, c], t
                )
    attn_grad_own = net.keep(r.attn_grad.at[:, :, aligned(head, 256)], r.attn_grad_row.at[z, :, c])
    branch_chain = chain(
        lambda step: shifted(at, dz=step),
        r.branch_low,
        lambda who: r.branch_row.at[who[2], :, who[4]],
        lambda who, half: r.branch_row.at[who[2], half, who[4]],
    )
    gate_landings = to_columns(r.gate_up_low, 0, r.gate_all, y_of, yc)
    head_loads = net.local_group()
    for i in range(8):
        for ref, start, width in (
            (r.query_weight, 0, 256),
            (r.key_weight, 256, 128),
            (r.value_weight, 384, 128),
        ):
            head_loads.add(ref.at[:, pl.ds(i * width, width)], r.wgu.at[:, pl.ds(i * 512 + start, width)])
    def total(own, others, landings):
        for landing in landings:
            landing.wait()
        result = own.astype(F32)
        for i in range(others.shape[0]):
            result = result + others[i].astype(F32)
        return result

    def wait_all(items):
        for item in items:
            item.wait()

    across = shifted(at, flip_xh=1)
    ending, swaps = net.group(), net.group()
    ending_own = net.local_group()

    def replicate(pieces, slot_of, wide_of, y_first):
        along = [net.group() if y_first else ending for _ in ys]
        over = ending if y_first else net.group()
        for src, (xl_to, c_to), mine in pieces:
            if mine:
                ending_own.add(src, slot_of(at))
            else:
                ending.add(src, slot_of(at), (xh, y, z, xl_to, c_to))
            over.add(src, slot_of(at), (1 - xh, y, z, xl_to, c_to))
            for group, t in zip(along, ys):
                group.add(src, slot_of(at), (xh, t[1], z, xl_to, c_to))

        def second():
            if y_first:
                for step, group in enumerate(along):
                    group.wait()
                    source = shifted(at, dy=-(step + 1))
                    ending.add(wide_of(source), wide_of(source), across)
            else:
                over.wait()
                for t in ys:
                    ending.add(wide_of(across), wide_of(across), t)

        return second

    def both_cores(done):
        return [(done.at[c], (xl, c), True), (done.at[1 - c], (xl, 1 - c), False)]

    def four_devices(done):
        return [
            (done.at[xl_to, c_to], (xl_to, c_to), (same_xl, same_c) == (True, True))
            for xl_to, same_xl in ((xl, True), (1 - xl, False))
            for c_to, same_c in ((c, True), (1 - c, False))
        ]

    def one_device(got):
        return [(got, (xl, c), True)]

    def ring_start(piece_of, far, landed, targets):
        ahead, opposite, behind = targets
        half = far.shape[1]
        first, last = pl.ds(0, half), pl.ds(half, half)
        state = Refs()
        state.targets, state.far, state.landed = targets, far, landed
        state.from_far = net.together(
            [
                (piece_of(opposite).at[first], far.at[0], ahead),
                (piece_of(opposite).at[last], far.at[1], behind),
            ]
        )
        state.near = net.together(
            [
                (piece_of(ahead).at[last], landed.at[0, last], ahead),
                (piece_of(behind).at[first], landed.at[1, first], behind),
            ]
        )
        state.wait = lambda: (state.near.wait(), state.summed.wait())
        return [state]

    def ring_middle(states, value_of, middle):
        (state,) = states
        ahead, _, behind = state.targets
        half = state.far.shape[1]
        first, last = pl.ds(0, half), pl.ds(half, half)
        state.from_far.wait()
        middle[0] = (value_of(ahead)[:half].astype(F32) + state.far[0].astype(F32)).astype(BF16)
        middle[1] = (value_of(behind)[half:].astype(F32) + state.far[1].astype(F32)).astype(BF16)
        state.summed = net.together(
            [
                (middle.at[0], state.landed.at[0, first], ahead),
                (middle.at[1], state.landed.at[1, last], behind),
            ]
        )

    def along_y(src, slot):
        ending_own.add(src, slot)
        for t in ys:
            ending.add(src, slot, t)

    def swap(own, low, own_to, got_to):
        swaps.add(low.at[1 - xl], got_to, partner)
        ending_own.add(own.at[xl], own_to)

    r.key_sum[...] = jnp.zeros_like(r.key_sum)
    r.value_sum[...] = jnp.zeros_like(r.value_sum)
    attn_grad_landings.wait()
    attn_grad_own.wait()

    def rope_norm_back(grad, part, rows, gain):
        turned = grad * r.cosines[rows, :] - pltpu.roll(grad, 64, 1) * r.sines[rows, :]
        vector = r.raw[rows, part * HD : (part + 1) * HD]
        result, gain_part = norm_back(turned, vector, r.inverses[rows, part : part + 1], gain)
        return (result.astype(BF16).reshape(2, 2, 64, HD), gain_part)

    def backward_block(block):
        rows = slice(block * BLOCK, (block + 1) * BLOCK)
        count = (block + 1) * BLOCK
        visible = visible_in(block)
        for h in range(2):
            columns = slice(h * HD, (h + 1) * HD)
            query = r.queries[rows, columns]
            grad = r.attn_grad_row[block, :, :, :, columns].reshape(BLOCK, HD)
            delta = jnp.sum(grad.astype(F32) * r.attended[rows, columns], axis=-1, keepdims=True)
            scores = dot_nt(query, r.keys[:count, :]) * (SCALE * LOG2E)
            soft = jnp.exp2(jnp.where(visible, scores - r.log_total[h, rows, :], MASKED))
            r.value_sum[:count, :] += dot_tn(soft.astype(BF16), grad)
            soft_grad = dot_nt(grad, r.values[:count, :])
            score_low = (soft * (soft_grad - delta)).astype(BF16)
            query_grad = dot_nn(score_low, r.keys[:count, :]) * SCALE
            r.key_sum[:count, :] += dot_tn(score_low, query)
            low, gain_part = rope_norm_back(query_grad, h, rows, r.query_gain[...])
            r.lows[block, :, :, :, columns] = low
            r.gains_own[16:17, :] += gain_part

    def by_rows(product):
        return product.astype(BF16).reshape(4, 2, 2, 2, 32, 384)

    def to_heads(done, got, width):
        items = [net.together([(done.at[t[2], t[4]], got.at[:, aligned(head, width)], t) for t in zc])]
        return items + [net.keep(done.at[z, c], got.at[:, aligned(head, width)])]

    r.gains_own[16:24, :] = jnp.zeros((8, 128), F32)
    wait_all(activated_landings)
    load_activated = net.keep(r.activated_all, r.wd.at[:, pl.ds(768, 384)])
    backward_block(0)
    chain_middle(down_chain)
    swap(r.layer_output, r.out_low, r.out_own, r.out_got)
    chain_near(residual_chain)
    near_up = net.local_group()
    for who in (at, residual_chain.behind, residual_chain.ahead):
        rows = aligned(y_of(who), 256)
        near_up.add(r.residual_y.at[rows, :], r.wo.at[rows, pl.ds(0, 1024)])
    chain_forward(residual_chain)
    backward_block(1)
    backward_block(2)
    chain_wait(residual_chain)
    rows = aligned(y_of(residual_chain.far), 256)
    far_up = net.keep(r.residual_y.at[rows, :], r.wo.at[rows, pl.ds(0, 1024)])
    wait_all(up_landings)
    load_up = net.keep(r.up_all, r.wd.at[:, pl.ds(0, 384)])
    backward_block(3)
    wait_all([near_up, far_up, load_up])
    r.own_up[...] = by_rows(dot_tn(r.wo[:, :1024], r.wd[:, :384]))
    first_up = [net.together([(r.own_up.at[:, t[3], :, t[0]], r.all_up.at[i], t) for i, t in enumerate(xs)])]
    chain_middle(branch_chain)
    chain_near(down_chain)
    near_down = net.local_group()
    for who in (at, down_chain.behind, down_chain.ahead):
        rows = aligned(x_of(who), 256)
        near_down.add(r.down_all.at[rows, :], r.wgu.at[rows, pl.ds(4096, 1024)])
    chain_forward(down_chain)
    key_total = jnp.zeros((1, HD), F32)
    for block in range(4):
        rows = slice(block * BLOCK, (block + 1) * BLOCK)
        low, gain_part = rope_norm_back(r.key_sum[rows, :] * SCALE, 2, rows, r.key_gain[...])
        r.lows[block, :, :, :, 256:384] = low
        r.lows[block, :, :, :, 384:] = r.value_sum[rows, :].astype(BF16).reshape(2, 2, 64, HD)
        key_total = key_total + gain_part
    r.gains_own[17:18, :] = key_total
    low_landings = {dz: net.group() for dz in ORDER}

    def send_lows(dz_here):
        for (dz, dc), t in zip(ZC, zc):
            if dz == dz_here:
                low_landings[dz].add(r.lows.at[t[2], :, t[4]], r.low_tokens.at[:, :, aligned(head, 512)], t)

    low_own = net.keep(r.lows.at[z, :, c], r.low_tokens.at[:, :, aligned(head, 512)])
    send_lows(0)
    gains_y = [net.together([(r.gains_own, r.gains_y.at[i], ys[i]) for i in range(3)])]
    row = r.row[...].reshape(1024, 1024)
    low_columns = dot_tn(row, r.lows[...].reshape(1024, 512)).astype(BF16)
    r.own_query[...] = low_columns[:, :256].reshape(4, 2, 2, 4, 16, 256)
    first_query = ring_start(lambda t: r.own_query.at[:, :, :, t[1]], r.far_query, r.all_query, ys)
    r.own_kv[...] = low_columns[:, 256:].reshape(4, 2, 2, 4, 16, 256)
    first_kv = [net.together([(r.own_kv.at[:, t[3], :, :, :, aligned(t[0], 128)], r.all_kv.at[i], t) for i, t in enumerate(xs)])]
    send_lows(1)
    wait_all(gate_landings)
    load_gate = net.keep(r.gate_all, r.wd.at[:, pl.ds(384, 384)])
    chain_wait(down_chain)
    rows = aligned(x_of(down_chain.far), 256)
    load_down = net.keep(r.down_all.at[rows, :], r.wgu.at[rows, pl.ds(4096, 1024)])
    wait_all([near_down, load_down, load_activated])
    product = dot_tn(r.wgu[:, 4096:5120], r.wd[:, 768:1152])
    r.own_down[...] = product.astype(BF16).reshape(4, 2, 2, 4, 16, 384)
    first_down = ring_start(lambda t: r.own_down.at[:, :, :, t[1]], r.far_down, r.all_down, ys)
    load_gate.wait()
    r.own_gate[...] = by_rows(dot_tn(r.wo[:, :1024], r.wd[:, 384:768]))
    first_gate = [net.together([(r.own_gate.at[t[2]], r.all_gate.at[i], t) for i, t in enumerate(zs)])]
    chain_forward(branch_chain)
    ring_middle(first_query, lambda t: r.own_query[:, :, :, t[1]], r.mid_query)
    ring_middle(first_down, lambda t: r.own_down[:, :, :, t[1]], r.mid_down)
    chain_wait(branch_chain)
    output_columns = dot_tn(r.branch_row[...].reshape(1024, 1024), r.attn_heads[...].reshape(1024, 256))
    r.own_output[...] = output_columns.astype(BF16).reshape(4, 2, 2, 4, 16, 256)
    first_output = ring_start(lambda t: r.own_output.at[:, :, :, t[1]], r.far_output, r.all_output, ys)
    r.next_up[...] = total(r.own_up[:, at[3], :, at[0]], r.all_up, first_up).astype(BF16)
    then_up = [net.together([(r.next_up.at[t[2]], r.then_up.at[i], t) for i, t in enumerate(zs)])]
    r.gains_next[...] = total(r.gains_own[...], r.gains_y, gains_y)
    gains_x = [net.together([(r.gains_next, r.gains_x.at[i], xs[i]) for i in range(3)])]
    r.next_query[...] = total(r.own_query[:, :, :, at[1]], r.all_query, first_query).astype(BF16)
    then_query = [net.together([(r.next_query.at[:, t[3]], r.then_query.at[i], t) for i, t in enumerate(xs)])]
    r.next_down[...] = total(r.own_down[:, :, :, at[1]], r.all_down, first_down).astype(BF16)
    then_down = [net.together([(r.next_down.at[t[2]], r.then_down.at[i], t) for i, t in enumerate(zs)])]
    r.next_kv[...] = total(r.own_kv[:, at[3], :, :, :, aligned(at[0], 128)], r.all_kv, first_kv).astype(BF16)
    then_kv = [net.together([(r.next_kv.at[:, :, t[1]], r.then_kv.at[i], t) for i, t in enumerate(ys)])]
    ring_middle(first_output, lambda t: r.own_output[:, :, :, t[1]], r.mid_output)
    send_lows(3)
    r.next_gate[...] = total(r.own_gate[at[2]], r.all_gate, first_gate).astype(BF16)
    then_gate = [net.together([(r.next_gate.at[t[3], :, t[0]], r.then_gate.at[i], t) for i, t in enumerate(xs)])]
    r.gains_last[...] = total(r.gains_next[...], r.gains_x, gains_x)
    gains_zc = [net.together([(r.gains_last, r.gains_zc.at[i], t) for i, t in enumerate(zc)])]
    r.done_up[...] = total(r.next_up[z], r.then_up, then_up).astype(BF16)
    second_up = replicate(
        both_cores(r.done_up),
        lambda who: r.up_grad.at[aligned(who[0], 32), aligned(who[1] * 2 + who[4], 384)],
        lambda who: r.up_grad.at[aligned(who[0], 32), aligned(who[1], 768)],
        True,
    )
    r.done_kv[...] = total(r.next_kv[:, :, y], r.then_kv, then_kv).astype(BF16)
    got_kv = to_heads(r.done_kv, r.got_kv, 128)
    r.done_down[...] = total(r.next_down[z], r.then_down, then_down).astype(BF16)
    second_down = replicate(
        four_devices(r.done_down),
        lambda who: r.down_grad.at[aligned(who[1], 16), aligned((who[0] * 2 + who[3]) * 2 + who[4], 384)],
        lambda who: r.down_grad.at[aligned(who[1], 16), aligned(who[0], 1536)],
        False,
    )
    r.next_output[...] = total(r.own_output[:, :, :, at[1]], r.all_output, first_output).astype(BF16)
    then_output = [net.together([(r.next_output.at[:, t[3]], r.then_output.at[i], t) for i, t in enumerate(xs)])]
    r.done_query[...] = total(r.next_query[:, xl], r.then_query, then_query).astype(BF16)
    got_query = to_heads(r.done_query, r.got_query, 256)
    send_lows(2)
    r.done_gate[...] = total(r.next_gate[xl, :, xh], r.then_gate, then_gate).astype(BF16)
    second_gate = replicate(
        both_cores(r.done_gate),
        lambda who: r.gate_grad.at[aligned(who[0], 32), aligned(who[1] * 2 + who[4], 384)],
        lambda who: r.gate_grad.at[aligned(who[0], 32), aligned(who[1], 768)],
        True,
    )
    wait_all(got_kv)
    second_kv = replicate(
        one_device(r.got_kv),
        lambda who: r.key_value_grad.at[who[0], aligned(who[1], 16), :],
        lambda who: r.key_value_grad.at[who[0], aligned(who[1], 16), :],
        False,
    )
    second_down()
    second_up()
    head_loads.wait()
    low_own.wait()
    for dz in (0, 1, 3):
        low_landings[dz].wait()

    @pl.loop(0, 2)
    def _(part):
        rows = aligned(part, 512)
        turned = jnp.zeros((512, 128), F32)
        for dz in (0, 1, 3):
            columns = aligned((z - dz) % ZS, 1024)
            turned = turned + dot_nt(r.wgu[rows, columns], r.low_tokens[:, :, columns].reshape(128, 1024))
        r.down[:, rows] = turned.T

    r.done_output[...] = total(r.next_output[:, xl], r.then_output, then_output).astype(BF16)
    got_output = to_heads(r.done_output, r.got_output, 256)
    wait_all(got_query)
    along_y(r.got_query, r.query_weight_grad.at[aligned(y, 16), :])
    second_gate()
    second_kv()
    low_landings[2].wait()
    columns = aligned((z - 2) % ZS, 1024)
    turned = dot_nt(r.wgu[:, columns], r.low_tokens[:, :, columns].reshape(128, 1024))
    input_grad = (r.residual_grad[...] + r.down[...] + turned.T).reshape(2, 64, 1024)
    r.input_grad[...] = input_grad
    r.grad_low[...] = input_grad.astype(BF16)
    swap(r.input_grad, r.grad_low, r.grad_own, r.grad_got)
    wait_all(got_output)
    along_y(r.got_output, r.output_weight_grad.at[aligned(y, 16), :])
    wait_all(gains_zc)
    gains = r.gains_last[...]
    for i in range(7):
        gains = gains + r.gains_zc[i]
    r.gains_final[...] = gains
    net.keep(r.gains_final, r.gains)
    assert (net.next_send, net.next_keep) == (SENDS, KEEPS), (net.next_send, net.next_keep)
    net.drain()


def layer(*arrays):
    return pl.pallas_call(
        layer_kernel,
        out_shape=[shape(*item) for item in OUTPUTS.values()],
        in_specs=[pl.BlockSpec(memory_space=pl.ANY)] * len(INPUTS),
        out_specs=[pl.BlockSpec(memory_space=pl.ANY)] * len(OUTPUTS),
        scratch_shapes=[pltpu.VMEM(*item) for item in [*SCRATCH.values(), *SMALL.values()]]
        + [
            pltpu.SemaphoreType.DMA((len(BUCKETS) + 1,)),
            pltpu.SemaphoreType.DMA((SENDS,)),
            pltpu.SemaphoreType.DMA((KEEPS,)),
        ],
        compiler_params=pltpu.CompilerParams(
            collective_id=0, has_side_effects=True, vmem_limit_bytes=VMEM_LIMIT
        ),
        name="layer",
    )(*arrays)


def widen_kernel(
    out_own, grad_own, out_got, grad_got, query, key_value, output, gate, up, down, gains,
    out_to, grad_to, query_to, key_to, value_to, output_to, gate_to, up_to, down_to,
    query_gain, key_gain, attention_gain, feedforward_gain,
):
    lower = (lax.axis_index("seq") // 2) % 2 == 0
    for own, got, to in ((out_own, out_got, out_to), (grad_own, grad_got, grad_to)):
        mine, other = own[...], got[...].astype(F32)
        to[0] = jnp.where(lower, mine, other)
        to[1] = jnp.where(lower, other, mine)
    query_to[...] = query[...].astype(F32)
    key_to[...] = key_value[0].astype(F32)
    value_to[...] = key_value[1].astype(F32)
    output_to[...] = output[...].astype(F32)
    gate_to[...] = gate[...].astype(F32)
    up_to[...] = up[...].astype(F32)
    down_to[...] = down[...].astype(F32)
    attention_gain[...] = gains[0:8, :]
    feedforward_gain[...] = gains[8:16, :]
    query_gain[...] = gains[16:17, :]
    key_gain[...] = gains[17:18, :]


def widen(*arrays):
    steps = 2
    rows = 64 // steps

    def flat(columns):
        return pl.BlockSpec((rows, columns), lambda i: (i, 0))

    def paired(columns):
        return pl.BlockSpec((2, rows, columns), lambda i: (0, i, 0))

    def whole(count):
        return pl.BlockSpec((count, 128), lambda i: (0, 0))

    return pl.pallas_call(
        widen_kernel,
        grid=(steps,),
        out_shape=[shape((2, 64, 1024), F32)] * 2
        + [shape((64, n), F32) for n in (2048, 1024, 1024, 2048, 3072, 3072, 3072)]
        + [shape((n, 128), F32) for n in (1, 1, 8, 8)],
        in_specs=[flat(1024)] * 4
        + [flat(2048), paired(1024), flat(2048)]
        + [flat(3072)] * 3
        + [whole(24)],
        out_specs=[paired(1024)] * 2
        + [flat(n) for n in (2048, 1024, 1024, 2048, 3072, 3072, 3072)]
        + [whole(n) for n in (1, 1, 8, 8)],
        name="widen",
    )(*arrays)


VMEM_LIMIT = 63 * 2**20


def per_device(
    hidden_in,
    query_weight,
    key_weight,
    value_weight,
    output_weight,
    gate_weight,
    up_weight,
    down_weight,
    query_gain,
    key_gain,
    attention_gain,
    feedforward_gain,
    document_ids,
    cotangent,
):
    results = layer(
        hidden_in, cotangent,
        query_weight, key_weight, value_weight, output_weight, gate_weight, up_weight, down_weight,
        document_ids, *rope_tables(),
        query_gain[None, :], key_gain[None, :], attention_gain[None, :], feedforward_gain[None, :],
    )[:11]
    results = widen(*results)
    return tuple(results[:9]) + (results[9][0], results[10][0], results[11].reshape(1024), results[12].reshape(1024))


def solution(mesh):
    tokens = P("rows", "seq", None)
    split = P("seq", None)
    return jax.shard_map(
        per_device,
        mesh=mesh,
        in_specs=(tokens,) + (P(),) * 11 + (P("rows", "seq"), tokens),
        out_specs=(tokens, tokens) + (split,) * 7 + (P(),) * 4,
        check_vma=False,
    )
```
